512 devices in a mesh: row: 32 (over z_hi, x, core), col: 16 (over y, z_lo).
Axes of the slice: x: 4, y: 4, z: 16 (z_hi: 4, z_lo: 4; z = z_hi * 4 + z_lo), core: 2. Of those that a mesh axis runs over, the one named last changes fastest.
Arguments:
- pair: bfloat16 [1024, 1024, 128], P('row', 'col'), may hold values from -110 to 110
- mask: int32 [1024], replicated, may hold values 0 or 1
- w_tri_in: bfloat16 [128, 640], replicated, may hold values from -0.5 to 0.5
- w_tri_out: bfloat16 [128, 128], replicated, may hold values from -0.5 to 0.5
- w_bias: bfloat16 [128, 64], replicated, may hold values from -0.5 to 0.5
- single: bfloat16 [16, 1024, 768], P(None, 'row'), may hold values from -6 to 6
- w_attn: bfloat16 [768, 16, 192], P(None, 'col'), may hold values from -2 to 2
- w_out: bfloat16 [768, 768], P('col'), may hold values from -0.21875 to 0.21875
Outputs:
- new_pair: bfloat16 [1024, 1024, 128], P('row', 'col')
- biases: bfloat16 [4, 16, 1024, 1024], P(None, 'col', 'row')
- attended: bfloat16 [16, 1024, 768], P('col', 'row')
The draws below stay inside these ranges and needn't reach their ends.
All inputs are finite; a program needn't handle non-finite values.
Results may differ from the reference program's by a relative error of at most 0.025.
The reference program's roundings to bfloat16 on the way count: a program that leaves them out, or rounds other values in their place, can miss the bound.
Values may be sent and summed in bfloat16 or wider, within the bound.
A program may use at most 64 MiB of HBM per device.

```python
import jax
import jax.numpy as jnp
from jax import lax

TOKENS = 1024
PAIR_CH = 128
D_TOKEN = 768
HEADS = 16
HEAD_DIM = 48
LAYERS = 4
SAMPLES = 16


def draw_pair(key, part):
    key = jax.random.fold_in(key, 11)
    base_key = jax.random.fold_in(key, 0)
    base = jax.random.truncated_normal(base_key, -6.0, 6.0, (TOKENS, TOKENS, PAIR_CH), jnp.float32)
    return base.astype(jnp.bfloat16)


def draw_w_attn(key, part):
    key = jax.random.fold_in(key, 12)
    base_key = jax.random.fold_in(key, 0)
    base = jax.random.truncated_normal(base_key, -6.0, 6.0, (D_TOKEN, HEADS, 4 * HEAD_DIM), jnp.float32)
    base = base * D_TOKEN ** (-0.5)
    return jnp.clip(base, -2.0, 2.0).astype(jnp.bfloat16)


def set_ends(result, rng, low, high):
    longest = result.shape.index(max(result.shape))
    spots = []
    for shift in (0, 1):
        where = [jax.random.randint(jax.random.fold_in(rng, axis), (), 0, length) for axis, length in enumerate(result.shape)]
        where[longest] = (where[longest] + shift) % result.shape[longest]
        spots.append(tuple(where))
    return result.at[spots[0]].set(low).at[spots[1]].set(high)


def block_levels(key, extent, cuts, low, top_value):
    level = 1.0
    for dim, parts in cuts:
        steps = jax.random.uniform(jax.random.fold_in(jax.random.fold_in(key, 6), dim), (parts,), jnp.float32, low / len(cuts), top_value / len(cuts))
        level = level * jnp.repeat(jnp.exp(steps), extent[dim] // parts).reshape((-1,) + (1,) * (len(extent) - 1 - dim))
    return level


def normal_values(stream_key, dims, deviation, reach, pieces=(), dtype=jnp.bfloat16):
    values = jax.random.normal(stream_key, dims, jnp.float32) * deviation
    if len(pieces) > 0:
        values = block_levels(stream_key, dims, pieces, -0.22, 0.18) * values
    return jnp.clip(values, min=-reach, max=reach).astype(dtype)


def setup_inputs(seed: int = 0) -> dict:
    arg_keys = jax.random.split(jax.random.key(seed), 9)
    return {
        "pair": draw_pair(jax.random.fold_in(arg_keys[8], 71), 0),
        "mask": set_ends((jax.random.randint(arg_keys[1], (TOKENS,), 0, 8) < 7).astype(jnp.int32), jax.random.fold_in(arg_keys[1], 1), 0, 1),
        "w_tri_in": normal_values(arg_keys[2], (PAIR_CH, 5 * PAIR_CH), PAIR_CH ** -0.5, 0.5),
        "w_tri_out": normal_values(arg_keys[3], (PAIR_CH, PAIR_CH), PAIR_CH ** -0.5, 0.5),
        "w_bias": normal_values(arg_keys[4], (PAIR_CH, LAYERS * HEADS), PAIR_CH ** -0.5, 0.5),
        "single": normal_values(arg_keys[5], (SAMPLES, TOKENS, D_TOKEN), 1.0, 6.0, ((1, 32),)),
        "w_attn": draw_w_attn(jax.random.fold_in(arg_keys[8], 71), 0),
        "w_out": normal_values(arg_keys[7], (HEADS * HEAD_DIM, D_TOKEN), D_TOKEN ** -0.5, 0.21875, ((0, 16),)),
    }


def layer_norm(value, axis):
    mean = lax.optimization_barrier(jnp.mean(value, axis=axis, keepdims=True))
    centred = value - mean
    var = lax.optimization_barrier(jnp.mean(centred * centred, axis=axis, keepdims=True))
    return centred * lax.rsqrt(var + 1e-05)

def reference(pair, mask, w_tri_in, w_tri_out, w_bias, single, w_attn, w_out):
    cells = TOKENS * TOKENS
    chans = PAIR_CH
    pair_f = pair.astype(jnp.float32).reshape(cells, chans)
    normed = layer_norm(pair_f, 1).astype(jnp.bfloat16)
    maskf = mask.astype(jnp.float32)
    pair_mask = (maskf[:, None] * maskf[None, :]).reshape(cells, 1)

    def factor(first):
        value = jnp.dot(normed, w_tri_in[:, first:first + chans], preferred_element_type=jnp.float32)
        gating = jnp.dot(normed, w_tri_in[:, first + chans:first + 2 * chans], preferred_element_type=jnp.float32)
        return (jax.nn.sigmoid(gating) * value * pair_mask).astype(jnp.bfloat16)
    left = factor(0).reshape(TOKENS, TOKENS, chans).transpose(2, 0, 1)
    right = factor(2 * chans).reshape(TOKENS, TOKENS, chans).transpose(2, 0, 1)
    gate = jax.nn.sigmoid(jnp.dot(normed, w_tri_in[:, 4 * chans:], preferred_element_type=jnp.float32))

    def contract(operands):
        return jnp.dot(operands[0].T, operands[1], preferred_element_type=jnp.float32).astype(jnp.bfloat16)
    tri = lax.map(contract, (left, right))
    tnorm = layer_norm(tri.astype(jnp.float32), 0).astype(jnp.bfloat16)
    update = jnp.dot(tnorm.reshape(chans, cells).T, w_tri_out, preferred_element_type=jnp.float32)
    new_flat = (pair_f + gate * update).astype(jnp.bfloat16)
    pnorm = layer_norm(new_flat.astype(jnp.float32), 1).astype(jnp.bfloat16)
    bias_flat = jnp.dot(pnorm, w_bias, preferred_element_type=jnp.float32).astype(jnp.bfloat16)
    biases = bias_flat.reshape(TOKENS, TOKENS, LAYERS, HEADS).transpose(2, 3, 0, 1)
    xn = layer_norm(single.astype(jnp.float32), 2).astype(jnp.bfloat16)
    projected = jnp.einsum('snd,dhe->hsne', xn.astype(jnp.float32), w_attn.astype(jnp.float32))
    query = projected[..., :HEAD_DIM].astype(jnp.bfloat16)
    keys = projected[..., HEAD_DIM:2 * HEAD_DIM].astype(jnp.bfloat16)
    values = projected[..., 2 * HEAD_DIM:3 * HEAD_DIM].astype(jnp.bfloat16)
    agate = jax.nn.sigmoid(projected[..., 3 * HEAD_DIM:])
    key_ok = (mask > 0)[None, None, :]
    scale = HEAD_DIM ** (-0.5)

    def one_head(operands):
        q_head, k_head, v_head, g_head, b_head = operands
        score = jnp.einsum('sqe,ske->sqk', q_head.astype(jnp.float32), k_head.astype(jnp.float32)) * scale
        score = score + b_head.astype(jnp.float32)[None]
        score = jnp.where(key_ok, score, -1000000000.0)
        peak = lax.optimization_barrier(jnp.max(score, axis=2, keepdims=True))
        expo = jnp.exp(score - peak)
        probs = (expo / lax.optimization_barrier(jnp.sum(expo, axis=2, keepdims=True))).astype(jnp.bfloat16)
        out = jnp.einsum('sqk,ske->sqe', probs.astype(jnp.float32), v_head.astype(jnp.float32))
        return (g_head * out).astype(jnp.bfloat16)
    heads_out = lax.map(one_head, (query, keys, values, agate, biases[0]))
    merged = heads_out.transpose(1, 2, 0, 3).reshape(SAMPLES * TOKENS, HEADS * HEAD_DIM)
    attended = jnp.dot(merged, w_out, preferred_element_type=jnp.float32).astype(jnp.bfloat16)
    new_pair = new_flat.reshape(TOKENS, TOKENS, chans)
    return (new_pair, biases, attended.reshape(SAMPLES, TOKENS, D_TOKEN))
```

```python
import jax
import jax.numpy as jnp
from jax import lax
from jax.experimental import pallas as pl
from jax.experimental.pallas import tpu as pltpu
from jax.sharding import Mesh
from jax.sharding import PartitionSpec as P

HEADS = 16
HEAD_DIM = 48
LAYERS = 4
ROW = ("z_hi", "x", "core")
COL = ("y", "z_lo")


def layer_norm(value, axis):
    mean = jnp.mean(value, axis=axis, keepdims=True)
    centred = value - mean
    var = jnp.mean(centred * centred, axis=axis, keepdims=True)
    return centred * lax.rsqrt(var + 1e-05)


def each(count, body):
    lax.fori_loop(0, count, lambda step, carry: (body(step), carry)[1], 0)


def wait_bytes(ref, sem):
    pltpu.make_async_copy(ref, ref, sem).wait()


def triangle_kernel(
    left_in, right_in, keyval_in, w_out_in,
    tri_out, keyval_out, w_out_all,
    left_x, right_x, left_z, right_z, left_all, right_own, sums, sums_x,
    send, recv, local,
):
    z_hi, z_lo = lax.axis_index("z_hi"), lax.axis_index("z_lo")
    x, core, y = lax.axis_index("x"), lax.axis_index("core"), lax.axis_index("y")
    z, xc = z_hi * 4 + z_lo, x * 2 + core
    head = y * 4 + z_lo

    def z_peer(step):
        peer = lax.rem(z + 1 + step, 16)
        return peer, {"z_hi": lax.div(peer, 4), "z_lo": lax.rem(peer, 4)}

    def xc_peer(step):
        peer = lax.rem(xc + 1 + step, 8)
        return peer, {"x": lax.div(peer, 2), "core": lax.rem(peer, 2)}

    def near(axis, place, step, size):
        return {axis: lax.rem(place + 1 + step, size)}

    barrier = pltpu.get_barrier_semaphore()

    def greet(peer):
        pl.semaphore_signal(barrier, inc=1, device_id=peer, device_id_type=pl.DeviceIdType.MESH)

    each(15, lambda step: greet(z_peer(step)[1]))
    each(7, lambda step: greet(xc_peer(step)[1]))
    each(3, lambda step: greet(near("y", y, step, 4)))
    pl.semaphore_wait(barrier, 25)

    def push(src, dst, slot, peer):
        pltpu.make_async_remote_copy(
            src_ref=src, dst_ref=dst, send_sem=send.at[slot], recv_sem=recv.at[slot],
            device_id=peer, device_id_type=pl.DeviceIdType.MESH,
        ).start()

    def keep(src, dst, slot):
        pltpu.make_async_copy(src, dst, local.at[slot]).start()

    def over_x(src, dst, slot):
        def body(step):
            peer, place = xc_peer(step)
            push(src.at[:, peer], dst.at[:, xc], slot, place)
        each(7, body)
        keep(src.at[:, xc], dst.at[:, xc], slot)

    def end_x(dst, slot):
        wait_bytes(dst.at[pl.ds(0, 14)], recv.at[slot])
        wait_bytes(dst.at[pl.ds(0, 2)], local.at[slot])

    def over_z(src, dst, slot):
        def body(step):
            peer, place = z_peer(step)
            push(src.at[peer], dst.at[z], slot, place)
        each(15, body)
        keep(src.at[z], dst.at[z], slot)

    def end_z(dst, slot):
        wait_bytes(dst.at[pl.ds(0, 15)], recv.at[slot])
        wait_bytes(dst.at[pl.ds(0, 1)], local.at[slot])

    over_x(left_in, left_x, 0)
    over_x(right_in, right_x, 1)
    half = w_out_in.at[:, pl.ds(pl.multiple_of(core * 384, 128), 384)]
    each(3, lambda step: push(half, w_out_all.at[core, head], 6, near("z_lo", z_lo, step, 4)))
    keep(half, w_out_all.at[core, head], 6)
    end_x(left_x, 0)
    over_z(left_x, left_z, 2)
    end_x(right_x, 1)
    over_z(right_x, right_z, 3)
    mine = keyval_out.at[z_hi * 4 + x, core]
    each(3, lambda step: push(keyval_in, mine, 9, near("z_hi", z_hi, step, 4)))
    keep(keyval_in, mine, 9)
    wait_bytes(w_out_all.at[0, pl.ds(0, 3)], recv.at[6])
    wait_bytes(w_out_all.at[0, pl.ds(0, 1)], local.at[6])
    quad = w_out_all.at[core, pl.ds(y * 4, 4)]
    each(3, lambda step: push(quad, quad, 7, near("y", y, step, 4)))

    def tiles(blocks, z_part, part):
        pieces = [blocks[z_part * 4 + lo, :, :, part * 64 : part * 64 + 64] for lo in range(4)]
        return jnp.concatenate(pieces, axis=-1).reshape(128, 256)

    end_z(left_z, 2)
    for z_part in range(4):
        for part in range(2):
            block = tiles(left_z, z_part, part)
            first = z_part * 256 + part * 128
            left_all[y, :, first : first + 128] = block.T
    own = left_all.at[y]
    each(3, lambda step: push(own, own, 5, near("y", y, step, 4)))
    end_z(right_z, 3)
    for z_part in range(4):
        for part in range(2):
            first = z_part * 256 + part * 128
            right_own[first : first + 128, :] = tiles(right_z, z_part, part)
    wait_bytes(left_all.at[pl.ds(0, 3)], recv.at[5])

    def contract(part):
        product = jnp.dot(left_all[part], right_own[...], preferred_element_type=jnp.float32)
        product = product.astype(jnp.bfloat16).reshape(8, 2, 16, 256)
        for lo in range(4):
            cut = slice(lo * 64, lo * 64 + 64)
            sums[part * 4 + lo] = jnp.concatenate(
                [product[:, 0, :, cut], product[:, 1, :, cut]], axis=-1
            )

    each(4, contract)
    over_x(sums, sums_x, 4)
    wait_bytes(keyval_out.at[pl.ds(0, 3), 0], recv.at[9])
    wait_bytes(keyval_out.at[pl.ds(0, 1), 0], local.at[9])
    end_x(sums_x, 4)
    over_z(sums_x, tri_out, 8)

    def spread(part):
        block = keyval_out.at[part * 4 + x, core]
        each(3, lambda step: push(block, block, 10, near("x", x, step, 4)))

    each(4, spread)
    wait_bytes(w_out_all.at[0, pl.ds(0, 12)], recv.at[7])
    other = {"core": 1 - core}
    push(w_out_all.at[core], w_out_all.at[core], 12, other)
    wait_bytes(keyval_out.at[pl.ds(0, 12), 0], recv.at[10])
    push(keyval_out.at[:, core], keyval_out.at[:, core], 11, other)
    end_z(tri_out, 8)
    wait_bytes(keyval_out.at[:, 0], recv.at[11])
    wait_bytes(w_out_all.at[0], recv.at[12])
    for slot in (0, 1, 4):
        wait_bytes(left_x.at[pl.ds(0, 14)], send.at[slot])
    for slot in (2, 3, 8):
        wait_bytes(left_z.at[pl.ds(0, 15)], send.at[slot])
    wait_bytes(left_all.at[pl.ds(0, 3)], send.at[5])
    wait_bytes(w_out_all.at[0, pl.ds(0, 3)], send.at[6])
    wait_bytes(w_out_all.at[0, pl.ds(0, 12)], send.at[7])
    wait_bytes(keyval_out.at[pl.ds(0, 3), 0], send.at[9])
    wait_bytes(keyval_out.at[pl.ds(0, 12), 0], send.at[10])
    wait_bytes(keyval_out.at[:, 0], send.at[11])
    wait_bytes(w_out_all.at[0], send.at[12])


def triangle(left, right, keyval, w_out):
    vmem = pl.BlockSpec(memory_space=pltpu.VMEM)
    hbm = pl.BlockSpec(memory_space=pl.ANY)
    blocks = pltpu.VMEM((16, 8, 16, 128), jnp.bfloat16)
    return pl.pallas_call(
        triangle_kernel,
        out_shape=(
            jax.ShapeDtypeStruct((16, 8, 16, 128), jnp.bfloat16),
            jax.ShapeDtypeStruct((16, 2, 4, 32, 384), jnp.bfloat16),
            jax.ShapeDtypeStruct((2, 16, 48, 384), jnp.bfloat16),
        ),
        in_specs=[vmem] * 4,
        out_specs=(vmem, vmem, vmem),
        scratch_shapes=[
            blocks, blocks, blocks, blocks,
            pltpu.VMEM((4, 256, 1024), jnp.bfloat16),
            pltpu.VMEM((1024, 256), jnp.bfloat16),
            blocks, blocks,
            pltpu.SemaphoreType.DMA((13,)),
            pltpu.SemaphoreType.DMA((13,)),
            pltpu.SemaphoreType.DMA((10,)),
        ],
        compiler_params=pltpu.CompilerParams(
            collective_id=0, has_side_effects=True, vmem_limit_bytes=40 * 1024 * 1024
        ),
        name="triangle",
    )(left, right, keyval, w_out)


def per_device(pair, mask, w_tri_in, w_tri_out, w_bias, single, w_attn, w_out):
    rows_dev, cols_dev, chans = pair.shape
    row_index = lax.axis_index(ROW)
    col_index = lax.axis_index(COL)
    maskf = mask.astype(jnp.float32)
    row_mask = lax.dynamic_slice_in_dim(maskf, row_index * rows_dev, rows_dev)
    col_mask = lax.dynamic_slice_in_dim(maskf, col_index * cols_dev, cols_dev)
    pair_mask = row_mask[:, None] * col_mask[None, :]
    pair_f = pair.astype(jnp.float32)
    normed = layer_norm(pair_f, 2).astype(jnp.bfloat16)
    leading = jnp.einsum(
        "ijc,cd->dij", normed, w_tri_in[:, : 4 * chans], preferred_element_type=jnp.float32
    )
    left = (jax.nn.sigmoid(leading[chans : 2 * chans]) * leading[:chans] * pair_mask).astype(
        jnp.bfloat16
    )
    right = (
        jax.nn.sigmoid(leading[3 * chans :]) * leading[2 * chans : 3 * chans] * pair_mask
    ).astype(jnp.bfloat16)
    gate = jax.nn.sigmoid(
        jnp.einsum(
            "ijc,cd->ijd", normed, w_tri_in[:, 4 * chans :], preferred_element_type=jnp.float32
        )
    )
    xn = layer_norm(single.astype(jnp.float32), 2).astype(jnp.bfloat16)
    projected = jnp.einsum("srd,dhe->shre", xn, w_attn, preferred_element_type=jnp.float32)
    query = projected[..., :HEAD_DIM].astype(jnp.bfloat16)
    keyval = projected[..., HEAD_DIM : 3 * HEAD_DIM].astype(jnp.bfloat16)
    packed = keyval[:, 0].reshape(2, 8, rows_dev, 2, HEAD_DIM).transpose(3, 0, 2, 1, 4)
    agate = jax.nn.sigmoid(projected[..., 3 * HEAD_DIM :])
    tri, keyval_all, w_out_all = triangle(
        left.reshape(16, 8, 16, 128),
        right.reshape(16, 8, 16, 128),
        packed.reshape(4, rows_dev, 8 * HEAD_DIM),
        w_out,
    )
    tri_tile = tri.reshape(chans, 16, 2, cols_dev).transpose(0, 2, 1, 3)
    tri_tile = tri_tile.reshape(chans, rows_dev, cols_dev)
    keyval_all = keyval_all.reshape(32, 2, 2, rows_dev, 8, HEAD_DIM).transpose(1, 2, 4, 0, 3, 5)
    keyval_all = keyval_all.reshape(2, 16, 1, 32 * rows_dev, HEAD_DIM)
    tnorm = layer_norm(tri_tile.astype(jnp.float32), 0).astype(jnp.bfloat16)
    update = jnp.einsum("cij,cd->ijd", tnorm, w_tri_out, preferred_element_type=jnp.float32)
    new_pair = (pair_f + gate * update).astype(jnp.bfloat16)
    pnorm = layer_norm(new_pair.astype(jnp.float32), 2).astype(jnp.bfloat16)
    bias_tile = jnp.einsum("ijc,cl->lij", pnorm, w_bias, preferred_element_type=jnp.float32).astype(
        jnp.bfloat16
    )
    bias_tile = bias_tile.reshape(LAYERS, HEADS, rows_dev, cols_dev)
    biases = lax.all_to_all(bias_tile, COL, split_axis=1, concat_axis=3, tiled=True)
    score = jnp.einsum(
        "shqe,shke->shqk", query, keyval_all[0], preferred_element_type=jnp.float32
    )
    score = score * HEAD_DIM ** (-0.5) + biases[0].astype(jnp.float32)[None]
    score = jnp.where((mask > 0)[None, None, None, :], score, -1000000000.0)
    peak = jnp.max(score, axis=3, keepdims=True)
    expo = jnp.exp(score - peak)
    probs = (expo / jnp.sum(expo, axis=3, keepdims=True)).astype(jnp.bfloat16)
    context = jnp.einsum(
        "shqk,shke->shqe", probs, keyval_all[1], preferred_element_type=jnp.float32
    )
    gated = (agate * context).astype(jnp.bfloat16)
    heads_out = lax.all_to_all(gated[:, 0], COL, split_axis=0, concat_axis=2, tiled=True)
    attended = jnp.einsum(
        "sqd,cde->sqce",
        heads_out,
        w_out_all.reshape(2, HEADS * HEAD_DIM, 384),
        preferred_element_type=jnp.float32,
    )
    attended = attended.astype(jnp.bfloat16).reshape(1, rows_dev, 768)
    return (new_pair, biases, attended)


def solution(mesh):
    fine = Mesh(mesh.devices.reshape(4, 4, 2, 4, 4), ("z_hi", "x", "core", "y", "z_lo"))
    placed = (
        P(ROW, COL, None),
        P(),
        P(),
        P(),
        P(),
        P(None, ROW, None),
        P(None, COL, None),
        P(COL, None),
    )
    return jax.shard_map(
        per_device,
        mesh=fine,
        in_specs=placed,
        out_specs=(P(ROW, COL, None), P(None, COL, ROW, None), P(COL, ROW, None)),
        check_vma=False,
    )
```

```python
import jax
import jax.numpy as jnp
import numpy as np
from jax import lax
from jax.experimental import pallas as pl
from jax.experimental.pallas import tpu as pltpu
from jax.sharding import Mesh
from jax.sharding import PartitionSpec as P

HEADS = 16
HEAD_DIM = 48
LAYERS = 4
WIDE = 8 * HEAD_DIM
ROW = ("z_hi", "x", "core")
COL = ("y", "z_lo")
BF16 = jnp.bfloat16
F32 = jnp.float32

LEFT_X, RIGHT_X, SUM_X = 0, 4, 8
LEFT_Z, RIGHT_Z, SUM_Z, LEFT_Y = 12, 13, 14, 15
OUT_Z, OUT_Y, OUT_CORE = 16, 17, 18
KV_Z, KV_X, KV_CORE = 19, 20, 21
BIAS_FIRST, BIAS_REST, HEADS_OUT = 22, 23, 24
SLOTS = 25


def selections():
    lane = np.arange(4 * WIDE)
    spread = np.arange(4 * HEAD_DIM)[:, None] == lane // WIDE * HEAD_DIM + lane % HEAD_DIM
    gather = np.arange(WIDE)[:, None] % HEAD_DIM == np.arange(128)[None, :]
    own = np.arange(256)[:, None] // 32 == np.arange(WIDE)[None, :] // HEAD_DIM
    return spread.astype(BF16), gather.astype(BF16), own.astype(np.float32)


def layer_norm(value, axis):
    mean = jnp.mean(value, axis=axis, keepdims=True)
    centred = value - mean
    var = jnp.mean(centred * centred, axis=axis, keepdims=True)
    return centred * lax.rsqrt(var + 1e-05)


def each(count, body):
    lax.fori_loop(0, count, lambda step, carry: (body(step), carry)[1], 0)


def wait_bytes(ref, sem):
    pltpu.make_async_copy(ref, ref, sem).wait()


def contract_last(a, b):
    return lax.dot_general(a, b, (((1,), (1,)), ((), ())), preferred_element_type=F32)


def matmul(a, b):
    return jnp.dot(a, b, preferred_element_type=F32)


def whole_kernel(
    pair, mask, w_tri_in, w_tri_out, w_bias, single, w_attn, w_out, spread_in, gather_in, own_in,
    new_pair, biases, attended,
    left_in, right_in, left_x, right_x, left_z, right_z, sums, sums_x, tri,
    left_all, right_own, keyval, keyval_in, w_out_all,
    normed, gate, rows_f, w_in_t, query, agate, score, bias_f, probs,
    bias_in, bias_all, heads_in, heads_all,
    send, recv, local,
):
    z_hi, z_lo = lax.axis_index("z_hi"), lax.axis_index("z_lo")
    x, core, y = lax.axis_index("x"), lax.axis_index("core"), lax.axis_index("y")
    z, xc, head = z_hi * 4 + z_lo, x * 2 + core, y * 4 + z_lo

    def z_place(peer):
        return {"z_hi": lax.div(peer, 4), "z_lo": lax.rem(peer, 4)}

    def xc_place(peer):
        return {"x": lax.div(peer, 2), "core": lax.rem(peer, 2)}

    def col_place(peer):
        return {"y": lax.div(peer, 4), "z_lo": lax.rem(peer, 4)}

    def after(place, step, size):
        return lax.rem(place + 1 + step, size)

    def near(axis, place, step, size):
        return {axis: after(place, step, size)}

    barrier = pltpu.get_barrier_semaphore()

    def greet(peer):
        pl.semaphore_signal(barrier, inc=1, device_id=peer, device_id_type=pl.DeviceIdType.MESH)

    each(15, lambda step: greet(z_place(after(z, step, 16))))
    each(7, lambda step: greet(xc_place(after(xc, step, 8))))
    each(15, lambda step: greet(col_place(after(head, step, 16))))

    def push(src, dst, slot, peer):
        pltpu.make_async_remote_copy(
            src_ref=src, dst_ref=dst, send_sem=send.at[slot], recv_sem=recv.at[slot],
            device_id=peer, device_id_type=pl.DeviceIdType.MESH,
        ).start()

    def keep(src, dst, slot):
        pltpu.make_async_copy(src, dst, local.at[slot]).start()

    def quarter(step):
        return after(z_hi, step, 4)

    def over_x(src, dst, slot, step):
        part = pl.ds(quarter(step) * 4, 4)

        def body(other):
            peer = after(xc, other, 8)
            push(src.at[part, peer], dst.at[part, xc], slot + step, xc_place(peer))

        each(7, body)
        keep(src.at[part, xc], dst.at[part, xc], slot + step)

    def end_x(dst, slot, step):
        wait_bytes(dst.at[0, pl.ds(0, 4)], local.at[slot + step])
        wait_bytes(dst.at[pl.ds(0, 4), pl.ds(0, 7)], recv.at[slot + step])

    def over_z(src, dst, slot, step):
        def body(low):
            peer = quarter(step) * 4 + low

            @pl.when(peer != z)
            def _():
                push(src.at[peer], dst.at[z], slot, z_place(peer))

            @pl.when(peer == z)
            def _():
                keep(src.at[z], dst.at[z], slot)

        each(4, body)

    def end_z(dst, slot):
        wait_bytes(dst.at[pl.ds(0, 1)], local.at[slot])
        wait_bytes(dst.at[pl.ds(0, 15)], recv.at[slot])

    mask_f = mask[...].astype(F32)
    lane = lax.broadcasted_iota(jnp.int32, (1024, 128), 1)
    token = lax.broadcasted_iota(jnp.int32, (1024, 128), 0)
    low_lane = jnp.where(lane < 64, lane, lane - 64)
    chosen = (token == head * 64 + low_lane).astype(F32).astype(BF16)
    col_mask = matmul(jnp.broadcast_to(mask_f, (16, 1024)).astype(BF16), chosen)
    token = lax.broadcasted_iota(jnp.int32, (16, 1024), 1)
    line = lax.broadcasted_iota(jnp.int32, (16, 1024), 0) * 2 + (z_hi * 8 + xc) * 32
    even = jnp.sum(jnp.where(token == line, mask_f, 0.0), axis=1, keepdims=True)
    odd = jnp.sum(jnp.where(token == line + 1, mask_f, 0.0), axis=1, keepdims=True)
    low = lax.broadcasted_iota(jnp.int32, (16, 128), 1) < 64
    cell_mask = jnp.where(low, even, odd) * col_mask

    w_in_t[...] = w_tri_in[:, 0:512].T

    def factor(block, first):
        rows = slice(block * 256, block * 256 + 256)
        both = contract_last(w_in_t[first : first + 256, :], normed[rows, :])
        value = jax.nn.sigmoid(both[128:]) * both[:128]
        for half in range(2):
            line = block * 2 + half
            part = value[:, half * 128 : half * 128 + 128] * cell_mask[line : line + 1]
            rows_f[pl.ds(line, 128, stride=16), :] = part

    for block in range(8):
        rows = slice(block * 256, block * 256 + 256)
        normed[rows, :] = layer_norm(pair[rows, :].astype(F32), 1).astype(BF16)
        factor(block, 0)
    left_in[...] = rows_f[...].astype(BF16).reshape(16, 8, 16, 128)
    pl.semaphore_wait(barrier, 37)
    for step in range(4):
        over_x(left_in, left_x, LEFT_X, step)
    for block in range(8):
        factor(block, 256)
    right_in[...] = rows_f[...].astype(BF16).reshape(16, 8, 16, 128)
    for step in range(4):
        end_x(left_x, LEFT_X, step)
        over_z(left_x, left_z, LEFT_Z, step)
    for step in range(4):
        over_x(right_in, right_x, RIGHT_X, step)
    half_out = w_out.at[:, pl.ds(pl.multiple_of(core * 384, 128), 384)]
    each(3, lambda step: push(half_out, w_out_all.at[core, head], OUT_Z, near("z_lo", z_lo, step, 4)))
    keep(half_out, w_out_all.at[core, head], OUT_Z)
    for step in range(4):
        end_x(right_x, RIGHT_X, step)
        over_z(right_x, right_z, RIGHT_Z, step)

    w_wide = matmul(w_attn[...], spread_in[...]).astype(BF16)
    for group in range(2):
        rows = slice(group * 256, group * 256 + 256)
        xn = layer_norm(single[rows, :].astype(F32), 1).astype(BF16)
        wide = matmul(xn, w_wide)
        query[rows, :] = (wide[:, 0:WIDE] * own_in[...]).astype(BF16)
        for which in range(2):
            part = wide[:, WIDE * (which + 1) : WIDE * (which + 2)] * own_in[...]
            packed = jnp.sum(part.reshape(8, 32, WIDE), axis=0)
            keyval_in[which * 2 + group] = packed.astype(BF16)
        agate[rows, :] = jax.nn.sigmoid(wide[:, 3 * WIDE :])

    mine = keyval.at[z_hi * 4 + x, core]
    each(3, lambda step: push(keyval_in, mine, KV_Z, near("z_hi", z_hi, step, 4)))
    keep(keyval_in, mine, KV_Z)
    wait_bytes(w_out_all.at[0, pl.ds(0, 1)], local.at[OUT_Z])
    wait_bytes(w_out_all.at[0, pl.ds(0, 3)], recv.at[OUT_Z])
    quad = w_out_all.at[core, pl.ds(y * 4, 4)]
    each(3, lambda step: push(quad, quad, OUT_Y, near("y", y, step, 4)))
    for block in range(8):
        rows = slice(block * 256, block * 256 + 256)
        gate[rows, :] = jax.nn.sigmoid(matmul(normed[rows, :], w_tri_in[:, 512:640]))

    def tiles(blocks, z_part, part):
        pieces = [blocks[z_part * 4 + low, :, :, part * 64 : part * 64 + 64] for low in range(4)]
        return jnp.concatenate(pieces, axis=-1).reshape(128, 256)

    end_z(left_z, LEFT_Z)
    for z_part in range(4):
        for part in range(2):
            first = z_part * 256 + part * 128
            left_all[y, :, first : first + 128] = tiles(left_z, z_part, part).T
    own = left_all.at[y]
    each(3, lambda step: push(own, own, LEFT_Y, near("y", y, step, 4)))
    end_z(right_z, RIGHT_Z)
    for z_part in range(4):
        for part in range(2):
            first = z_part * 256 + part * 128
            right_own[first : first + 128, :] = tiles(right_z, z_part, part)
    wait_bytes(left_all.at[pl.ds(0, 3)], recv.at[LEFT_Y])
    for step in range(4):
        part = quarter(step)
        product = matmul(left_all[part], right_own[...]).astype(BF16).reshape(8, 2, 16, 256)
        for low in range(4):
            cut = slice(low * 64, low * 64 + 64)
            sums[part * 4 + low] = jnp.concatenate(
                [product[:, 0, :, cut], product[:, 1, :, cut]], axis=-1
            )
        over_x(sums, sums_x, SUM_X, step)
    for step in range(4):
        end_x(sums_x, SUM_X, step)
        over_z(sums_x, tri, SUM_Z, step)
    wait_bytes(keyval.at[pl.ds(0, 1), 0], local.at[KV_Z])
    wait_bytes(keyval.at[pl.ds(0, 3), 0], recv.at[KV_Z])

    def pass_on(part):
        block = keyval.at[part * 4 + x, core]
        each(3, lambda step: push(block, block, KV_X, near("x", x, step, 4)))

    each(4, pass_on)
    wait_bytes(w_out_all.at[0, pl.ds(0, 12)], recv.at[OUT_Y])
    push(w_out_all.at[core], w_out_all.at[core], OUT_CORE, {"core": 1 - core})
    wait_bytes(keyval.at[pl.ds(0, 12), 0], recv.at[KV_X])
    push(keyval.at[:, core], keyval.at[:, core], KV_CORE, {"core": 1 - core})

    end_z(tri, SUM_Z)
    rows_f[...] = tri[...].reshape(2048, 128).astype(F32)
    w_bias_t = w_bias[...].T
    for block in range(8):
        lines = (block * 2, block * 2 + 16, block * 2 + 1, block * 2 + 17)
        value = jnp.concatenate(
            [rows_f[pl.ds(block * 2 + half, 128, stride=16), :] for half in range(2)], axis=1
        )
        tnorm = layer_norm(value, 0).T.astype(BF16)
        update = matmul(tnorm, w_tri_out[...])
        updated = []
        for place, line in enumerate(lines):
            cells = slice(line * 64, line * 64 + 64)
            change = gate[cells, :] * update[place * 64 : place * 64 + 64]
            updated.append((pair[cells, :].astype(F32) + change).astype(BF16))
            new_pair[cells, :] = updated[-1]
        pnorm = layer_norm(jnp.concatenate(updated, axis=0).astype(F32), 1).astype(BF16)
        bias = contract_last(w_bias_t, pnorm)
        for half in range(2):
            rows = pl.ds(block * 2 + half, 64, stride=16)
            bias_f[rows, :] = bias[:, half * 128 : half * 128 + 128]
    bias_in[...] = bias_f[...].astype(BF16).reshape(4, 16, 16, 128)

    def send_bias(layers, slot):
        def body(step):
            peer = after(head, step, 16)
            push(bias_in.at[layers, peer], bias_all.at[layers, head], slot, col_place(peer))

        each(15, body)
        keep(bias_in.at[layers, head], bias_all.at[layers, head], slot)

    send_bias(pl.ds(0, 1), BIAS_FIRST)
    send_bias(pl.ds(1, 3), BIAS_REST)
    wait_bytes(keyval.at[:, 0], recv.at[KV_CORE])
    for group in range(2):
        rows = slice(group * 256, group * 256 + 256)
        keys = keyval[:, :, group].reshape(1024, WIDE)
        score[rows, :] = contract_last(query[rows, :], keys)

    def bias_rows(layer):
        return jnp.concatenate(
            [
                jnp.concatenate(
                    [bias_all[layer, src, :, part * 64 : part * 64 + 64] for src in range(16)],
                    axis=-1,
                )
                for part in range(2)
            ],
            axis=0,
        )

    wait_bytes(bias_all.at[0, pl.ds(0, 1)], local.at[BIAS_FIRST])
    wait_bytes(bias_all.at[0, pl.ds(0, 15)], recv.at[BIAS_FIRST])
    first_bias = bias_rows(0)
    biases[0] = first_bias
    first_bias = first_bias.astype(F32)
    present = mask_f > 0.0
    for sample in range(16):
        rows = slice(sample * 32, sample * 32 + 32)
        logits = score[rows, :] * HEAD_DIM ** (-0.5) + first_bias
        logits = jnp.where(present, logits, -1000000000.0)
        expo = jnp.exp(logits - jnp.max(logits, axis=1, keepdims=True))
        probs[rows, :] = (expo * (1.0 / jnp.sum(expo, axis=1, keepdims=True))).astype(BF16)
    for group in range(2):
        rows = slice(group * 256, group * 256 + 256)
        values = keyval[:, :, 2 + group].reshape(1024, WIDE)
        context = matmul(probs[rows, :], values)
        gated = (agate[rows, :] * context * own_in[...]).astype(BF16)
        gathered = matmul(gated, gather_in[...]).astype(BF16)
        heads_in[group * 8 : group * 8 + 8] = gathered.reshape(8, 32, 128)

    def send_heads(step):
        peer = after(head, step, 16)
        push(heads_in.at[peer], heads_all.at[head], HEADS_OUT, col_place(peer))

    each(15, send_heads)
    keep(heads_in.at[head], heads_all.at[head], HEADS_OUT)
    wait_bytes(bias_all.at[pl.ds(0, 3), 0], local.at[BIAS_REST])
    wait_bytes(bias_all.at[pl.ds(0, 3), pl.ds(0, 15)], recv.at[BIAS_REST])
    for layer in range(1, 4):
        biases[layer] = bias_rows(layer)
    wait_bytes(w_out_all.at[0], recv.at[OUT_CORE])
    wait_bytes(heads_all.at[pl.ds(0, 1)], local.at[HEADS_OUT])
    wait_bytes(heads_all.at[pl.ds(0, 15)], recv.at[HEADS_OUT])
    merged = jnp.concatenate([heads_all[src, :, 0:HEAD_DIM] for src in range(16)], axis=-1)
    for half in range(2):
        weights = w_out_all[half].reshape(HEADS * HEAD_DIM, 384)
        attended[:, half * 384 : half * 384 + 384] = matmul(merged, weights).astype(BF16)

    for slot in (LEFT_X, RIGHT_X, SUM_X):
        for step in range(4):
            wait_bytes(left_x.at[pl.ds(0, 4), pl.ds(0, 7)], send.at[slot + step])
    for slot in (LEFT_Z, RIGHT_Z, SUM_Z):
        wait_bytes(left_z.at[pl.ds(0, 15)], send.at[slot])
    wait_bytes(left_all.at[pl.ds(0, 3)], send.at[LEFT_Y])
    wait_bytes(w_out_all.at[0, pl.ds(0, 3)], send.at[OUT_Z])
    wait_bytes(w_out_all.at[0, pl.ds(0, 12)], send.at[OUT_Y])
    wait_bytes(w_out_all.at[0], send.at[OUT_CORE])
    wait_bytes(keyval.at[pl.ds(0, 3), 0], send.at[KV_Z])
    wait_bytes(keyval.at[pl.ds(0, 12), 0], send.at[KV_X])
    wait_bytes(keyval.at[:, 0], send.at[KV_CORE])
    wait_bytes(bias_all.at[0, pl.ds(0, 15)], send.at[BIAS_FIRST])
    wait_bytes(bias_all.at[pl.ds(0, 3), pl.ds(0, 15)], send.at[BIAS_REST])
    wait_bytes(heads_all.at[pl.ds(0, 15)], send.at[HEADS_OUT])


def per_device(pair, mask, w_tri_in, w_tri_out, w_bias, single, w_attn, w_out):
    vmem = pl.BlockSpec(memory_space=pltpu.VMEM)
    blocks = pltpu.VMEM((16, 8, 16, 128), BF16)
    new_pair, biases, attended = pl.pallas_call(
        whole_kernel,
        out_shape=(
            jax.ShapeDtypeStruct((2048, 128), BF16),
            jax.ShapeDtypeStruct((LAYERS, 32, 1024), BF16),
            jax.ShapeDtypeStruct((32, 768), BF16),
        ),
        in_specs=[vmem] * 11,
        out_specs=(vmem, vmem, vmem),
        scratch_shapes=[blocks] * 9
        + [
            pltpu.VMEM((4, 256, 1024), BF16),
            pltpu.VMEM((1024, 256), BF16),
            pltpu.VMEM((16, 2, 4, 32, WIDE), BF16),
            pltpu.VMEM((4, 32, WIDE), BF16),
            pltpu.VMEM((2, HEADS, HEAD_DIM, 384), BF16),
            pltpu.VMEM((2048, 128), BF16),
            pltpu.VMEM((2048, 128), F32),
            pltpu.VMEM((2048, 128), F32),
            pltpu.VMEM((512, 128), BF16),
            pltpu.VMEM((512, WIDE), BF16),
            pltpu.VMEM((512, WIDE), F32),
            pltpu.VMEM((512, 1024), F32),
            pltpu.VMEM((1024, 128), F32),
            pltpu.VMEM((512, 1024), BF16),
            pltpu.VMEM((LAYERS, 16, 16, 128), BF16),
            pltpu.VMEM((LAYERS, 16, 16, 128), BF16),
            pltpu.VMEM((16, 32, 128), BF16),
            pltpu.VMEM((16, 32, 128), BF16),
            pltpu.SemaphoreType.DMA((SLOTS,)),
            pltpu.SemaphoreType.DMA((SLOTS,)),
            pltpu.SemaphoreType.DMA((SLOTS,)),
        ],
        compiler_params=pltpu.CompilerParams(
            collective_id=0, has_side_effects=True, vmem_limit_bytes=48 * 1024 * 1024
        ),
        name="whole",
    )(
        pair.reshape(2048, 128),
        mask.reshape(1, 1024),
        w_tri_in,
        w_tri_out,
        w_bias,
        single.reshape(512, 768),
        w_attn.reshape(768, 4 * HEAD_DIM),
        w_out,
        *(jnp.asarray(matrix) for matrix in selections()),
    )
    return (
        new_pair.reshape(32, 64, 128),
        biases.reshape(LAYERS, 1, 32, 1024),
        attended.reshape(1, 32, 768),
    )


def solution(mesh):
    fine = Mesh(mesh.devices.reshape(4, 4, 2, 4, 4), ("z_hi", "x", "core", "y", "z_lo"))
    placed = (
        P(ROW, COL, None),
        P(),
        P(),
        P(),
        P(),
        P(None, ROW, None),
        P(None, COL, None),
        P(COL, None),
    )
    return jax.shard_map(
        per_device,
        mesh=fine,
        in_specs=placed,
        out_specs=(P(ROW, COL, None), P(None, COL, ROW, None), P(COL, ROW, None)),
        check_vma=False,
    )
```

```python
import jax
import jax.numpy as jnp
from jax import lax
from jax.experimental import pallas as pl
from jax.experimental.pallas import tpu as pltpu
from jax.sharding import Mesh
from jax.sharding import PartitionSpec as P

HEADS = 16
HEAD_DIM = 48
LAYERS = 4
WIDE = 8 * HEAD_DIM
ROW = ("z_hi", "x", "core")
COL = ("y", "z_lo")
BF16 = jnp.bfloat16
F32 = jnp.float32

LEFT_X, RIGHT_X, SUM_X = 0, 4, 8
LEFT_Z, RIGHT_Z, SUM_Z = 12, 13, 14
OUT_Z, OUT_Y, OUT_CORE, KV_CORE = 15, 16, 17, 18
BIAS_FIRST, BIAS_REST, HEADS_OUT = 19, 20, 21
LEFT_NEAR, LEFT_FAR, KV_Z_NEAR, KV_Z_FAR, KV_X_NEAR, KV_X_FAR = 22, 24, 26, 28, 30, 32
SLOTS = 34


def block_of(index):
    return sum((index >= HEAD_DIM * edge).astype(jnp.int32) for edge in range(1, 32))


def layer_norm(value, axis):
    mean = jnp.mean(value, axis=axis, keepdims=True)
    centred = value - mean
    var = jnp.mean(centred * centred, axis=axis, keepdims=True)
    return centred * lax.rsqrt(var + 1e-05)


def each(count, body):
    lax.fori_loop(0, count, lambda step, carry: (body(step), carry)[1], 0)


def wait_bytes(ref, sem):
    pltpu.make_async_copy(ref, ref, sem).wait()


def contract_last(a, b):
    return lax.dot_general(a, b, (((1,), (1,)), ((), ())), preferred_element_type=F32)


def matmul(a, b):
    return jnp.dot(a, b, preferred_element_type=F32)


def whole_kernel(
    pair_h, mask_h, w_tri_in_h, w_tri_out_h, w_bias_h, single_h, w_attn_h, w_out_h,
    new_pair, biases, attended,
    pair, mask, w_tri_in, w_tri_out, w_bias, single, w_attn, w_out,
    left_in, right_in, left_x, right_x, left_z, right_z, sums, sums_x, tri,
    gather_in, own_in,
    left_all, right_own, keyval, keyval_in, w_out_all,
    normed, gate, rows_f, w_in_t, query, agate, score, bias_f, probs,
    bias_in, bias_all, heads_in, heads_all,
    send, recv, local, load,
):
    z_hi, z_lo = lax.axis_index("z_hi"), lax.axis_index("z_lo")
    x, core, y = lax.axis_index("x"), lax.axis_index("core"), lax.axis_index("y")
    z, xc, head = z_hi * 4 + z_lo, x * 2 + core, y * 4 + z_lo

    def z_place(peer):
        return {"z_hi": lax.div(peer, 4), "z_lo": lax.rem(peer, 4)}

    def xc_place(peer):
        return {"x": lax.div(peer, 2), "core": lax.rem(peer, 2)}

    def col_place(peer):
        return {"y": lax.div(peer, 4), "z_lo": lax.rem(peer, 4)}

    def after(place, step, size):
        return lax.rem(place + 1 + step, size)

    def near(axis, place, step, size):
        return {axis: after(place, step, size)}

    loads = [
        pltpu.make_async_copy(src, dst, load.at[slot])
        for slot, (src, dst) in enumerate(
            (
                (pair_h, pair), (w_tri_in_h, w_tri_in), (mask_h, mask), (w_out_h, w_out),
                (w_attn_h, w_attn), (single_h, single), (w_tri_out_h, w_tri_out), (w_bias_h, w_bias),
            )
        )
    ]
    for copy in loads:
        copy.start()
    barrier = pltpu.get_barrier_semaphore()

    def greet(peer):
        pl.semaphore_signal(barrier, inc=1, device_id=peer, device_id_type=pl.DeviceIdType.MESH)

    each(15, lambda step: greet(z_place(after(z, step, 16))))
    each(7, lambda step: greet(xc_place(after(xc, step, 8))))
    each(15, lambda step: greet(col_place(after(head, step, 16))))

    def push(src, dst, slot, peer):
        pltpu.make_async_remote_copy(
            src_ref=src, dst_ref=dst, send_sem=send.at[slot], recv_sem=recv.at[slot],
            device_id=peer, device_id_type=pl.DeviceIdType.MESH,
        ).start()

    def keep(src, dst, slot):
        pltpu.make_async_copy(src, dst, local.at[slot]).start()

    def quarter(step):
        return after(z_hi, step, 4)

    def over_x(src, dst, slot, step):
        part = pl.ds(quarter(step) * 4, 4)

        def body(other):
            peer = after(xc, other, 8)
            push(src.at[part, peer], dst.at[part, xc], slot + step, xc_place(peer))

        each(7, body)
        keep(src.at[part, xc], dst.at[part, xc], slot + step)

    def end_x(dst, slot, step):
        wait_bytes(dst.at[0, pl.ds(0, 4)], local.at[slot + step])
        wait_bytes(dst.at[pl.ds(0, 4), pl.ds(0, 7)], recv.at[slot + step])

    def over_z(src, dst, slot, step):
        def body(low):
            peer = quarter(step) * 4 + low

            @pl.when(peer != z)
            def _():
                push(src.at[peer], dst.at[z], slot, z_place(peer))

            @pl.when(peer == z)
            def _():
                keep(src.at[z], dst.at[z], slot)

        each(4, body)

    def end_z(dst, slot):
        wait_bytes(dst.at[pl.ds(0, 1)], local.at[slot])
        wait_bytes(dst.at[pl.ds(0, 15)], recv.at[slot])

    for copy in loads[:3]:
        copy.wait()
    mask_f = mask[...].astype(F32)
    lane = lax.broadcasted_iota(jnp.int32, (1024, 128), 1)
    token = lax.broadcasted_iota(jnp.int32, (1024, 128), 0)
    low_lane = jnp.where(lane < 64, lane, lane - 64)
    chosen = (token == head * 64 + low_lane).astype(F32).astype(BF16)
    col_mask = matmul(jnp.broadcast_to(mask_f, (16, 1024)).astype(BF16), chosen)
    token = lax.broadcasted_iota(jnp.int32, (16, 1024), 1)
    line = lax.broadcasted_iota(jnp.int32, (16, 1024), 0) * 2 + (z_hi * 8 + xc) * 32
    even = jnp.sum(jnp.where(token == line, mask_f, 0.0), axis=1, keepdims=True)
    odd = jnp.sum(jnp.where(token == line + 1, mask_f, 0.0), axis=1, keepdims=True)
    low = lax.broadcasted_iota(jnp.int32, (16, 128), 1) < 64
    cell_mask = jnp.where(low, even, odd) * col_mask

    w_in_t[...] = w_tri_in[:, 0:512].T

    def factor(block, first):
        rows = slice(block * 256, block * 256 + 256)
        both = contract_last(w_in_t[first : first + 256, :], normed[rows, :])
        value = jax.nn.sigmoid(both[128:]) * both[:128]
        for half in range(2):
            line = block * 2 + half
            part = value[:, half * 128 : half * 128 + 128] * cell_mask[line : line + 1]
            rows_f[pl.ds(line, 128, stride=16), :] = part

    for block in range(8):
        rows = slice(block * 256, block * 256 + 256)
        normed[rows, :] = layer_norm(pair[rows, :].astype(F32), 1).astype(BF16)
        factor(block, 0)
    left_in[...] = rows_f[...].astype(BF16).reshape(16, 8, 16, 128)
    pl.semaphore_wait(barrier, 37)
    for step in range(4):
        over_x(left_in, left_x, LEFT_X, step)
    for block in range(8):
        factor(block, 256)
    right_in[...] = rows_f[...].astype(BF16).reshape(16, 8, 16, 128)
    for step in range(4):
        end_x(left_x, LEFT_X, step)
        over_z(left_x, left_z, LEFT_Z, step)
    for step in range(4):
        over_x(right_in, right_x, RIGHT_X, step)
    loads[3].wait()
    half_out = w_out.at[:, pl.ds(pl.multiple_of(core * 384, 128), 384)]
    each(3, lambda step: push(half_out, w_out_all.at[core, head], OUT_Z, near("z_lo", z_lo, step, 4)))
    keep(half_out, w_out_all.at[core, head], OUT_Z)
    for step in range(4):
        end_x(right_x, RIGHT_X, step)
        over_z(right_x, right_z, RIGHT_Z, step)

    for copy in loads[4:]:
        copy.wait()
    lane = lax.broadcasted_iota(jnp.int32, (1, 4 * WIDE), 1)
    block = block_of(lane)
    source = lane - HEAD_DIM * block + HEAD_DIM * sum((block >= 8 * n).astype(jnp.int32) for n in (1, 2, 3))
    place = lax.broadcasted_iota(jnp.int32, (4 * HEAD_DIM, 4 * WIDE), 0)
    spread = (place == source).astype(F32).astype(BF16)
    place = lax.broadcasted_iota(jnp.int32, (256, WIDE), 0)
    own_block = ((place >= 32 * block[:, :WIDE]) & (place < 32 * block[:, :WIDE] + 32)).astype(F32)
    lane = lax.broadcasted_iota(jnp.int32, (WIDE, 128), 1)
    place = lax.broadcasted_iota(jnp.int32, (WIDE, 128), 0)
    gather = (place - HEAD_DIM * block_of(place) == lane).astype(F32).astype(BF16)
    own_in[...] = own_block
    gather_in[...] = gather
    w_wide = matmul(w_attn[...].T, spread).astype(BF16)
    for group in range(2):
        rows = slice(group * 256, group * 256 + 256)
        xn = layer_norm(single[rows, :].astype(F32), 1).astype(BF16)
        wide = matmul(xn, w_wide)
        query[rows, :] = (wide[:, 0:WIDE] * own_in[...]).astype(BF16)
        for which in range(2):
            part = wide[:, WIDE * (which + 1) : WIDE * (which + 2)] * own_in[...]
            packed = jnp.sum(part.reshape(8, 32, WIDE), axis=0)
            keyval_in[which * 2 + group] = packed.astype(BF16)
        agate[rows, :] = jax.nn.sigmoid(wide[:, 3 * WIDE :])

    wait_bytes(w_out_all.at[0, pl.ds(0, 1)], local.at[OUT_Z])
    wait_bytes(w_out_all.at[0, pl.ds(0, 3)], recv.at[OUT_Z])
    quad = w_out_all.at[core, pl.ds(y * 4, 4)]
    each(3, lambda step: push(quad, quad, OUT_Y, near("y", y, step, 4)))
    for block in range(8):
        rows = slice(block * 256, block * 256 + 256)
        gate[rows, :] = jax.nn.sigmoid(matmul(normed[rows, :], w_tri_in[:, 512:640]))

    def tiles(blocks, z_part, part):
        pieces = [blocks[z_part * 4 + low, :, :, part * 64 : part * 64 + 64] for low in range(4)]
        return jnp.concatenate(pieces, axis=-1).reshape(128, 256)

    end_z(left_z, LEFT_Z)
    for z_part in range(4):
        for part in range(2):
            first = z_part * 256 + part * 128
            left_all[y, :, first : first + 128] = tiles(left_z, z_part, part).T
    own = left_all.at[y]
    up, down = after(y, 0, 4), after(y, 2, 4)
    push(own, own, LEFT_NEAR, {"y": up})
    push(own, own, LEFT_NEAR + 1, {"y": down})
    wait_bytes(own, recv.at[LEFT_NEAR])
    passed = left_all.at[down, pl.ds(0, 128)]
    push(passed, passed, LEFT_FAR, {"y": up})
    wait_bytes(own, recv.at[LEFT_NEAR + 1])
    passed = left_all.at[up, pl.ds(128, 128)]
    push(passed, passed, LEFT_FAR + 1, {"y": down})
    end_z(right_z, RIGHT_Z)
    mine = keyval.at[z_hi * 4 + x, core]
    z_up, z_down, x_up, x_down = after(z_hi, 0, 4), after(z_hi, 2, 4), after(x, 0, 4), after(x, 2, 4)
    push(keyval_in, mine, KV_Z_NEAR, {"z_hi": z_up})
    push(keyval_in, mine, KV_Z_NEAR + 1, {"z_hi": z_down})
    keep(keyval_in, mine, KV_Z_NEAR)
    for z_part in range(4):
        for part in range(2):
            first = z_part * 256 + part * 128
            right_own[first : first + 128, :] = tiles(right_z, z_part, part)
    wait_bytes(left_all.at[0, pl.ds(0, 128)], recv.at[LEFT_FAR])
    wait_bytes(left_all.at[0, pl.ds(0, 128)], recv.at[LEFT_FAR + 1])
    for step in range(4):
        part = quarter(step)
        product = matmul(left_all[part], right_own[...]).astype(BF16).reshape(8, 2, 16, 256)
        for low in range(4):
            cut = slice(low * 64, low * 64 + 64)
            sums[part * 4 + low] = jnp.concatenate(
                [product[:, 0, :, cut], product[:, 1, :, cut]], axis=-1
            )
        over_x(sums, sums_x, SUM_X, step)
    for step in range(4):
        end_x(sums_x, SUM_X, step)
        over_z(sums_x, tri, SUM_Z, step)
    wait_bytes(keyval_in, local.at[KV_Z_NEAR])
    wait_bytes(keyval_in, recv.at[KV_Z_NEAR])
    passed = keyval.at[z_down * 4 + x, core, pl.ds(0, 2)]
    push(passed, passed, KV_Z_FAR, {"z_hi": z_up})
    wait_bytes(keyval_in, recv.at[KV_Z_NEAR + 1])
    passed = keyval.at[z_up * 4 + x, core, pl.ds(2, 2)]
    push(passed, passed, KV_Z_FAR + 1, {"z_hi": z_down})

    def over_x_ring(part):
        block = keyval.at[part * 4 + x, core]
        push(block, block, KV_X_NEAR, {"x": x_up})
        push(block, block, KV_X_NEAR + 1, {"x": x_down})

    each(3, lambda step: over_x_ring(lax.rem(z_hi + 3 + step, 4)))
    wait_bytes(w_out_all.at[0, pl.ds(0, 12)], recv.at[OUT_Y])
    push(w_out_all.at[core], w_out_all.at[core], OUT_CORE, {"core": 1 - core})
    wait_bytes(keyval_in.at[pl.ds(0, 2)], recv.at[KV_Z_FAR])
    wait_bytes(keyval_in.at[pl.ds(0, 2)], recv.at[KV_Z_FAR + 1])
    over_x_ring(lax.rem(z_hi + 2, 4))

    def pass_x(first, src, slot, place):
        def body(part):
            passed = keyval.at[part * 4 + src, core, pl.ds(first, 2)]
            push(passed, passed, slot, place)

        wait_bytes(keyval.at[pl.ds(0, 4), 0], recv.at[slot - 2])
        each(4, body)

    pass_x(0, x_down, KV_X_FAR, {"x": x_up})
    pass_x(2, x_up, KV_X_FAR + 1, {"x": x_down})
    wait_bytes(keyval.at[pl.ds(0, 2), 0], recv.at[KV_X_FAR])
    wait_bytes(keyval.at[pl.ds(0, 2), 0], recv.at[KV_X_FAR + 1])
    push(keyval.at[:, core], keyval.at[:, core], KV_CORE, {"core": 1 - core})

    end_z(tri, SUM_Z)
    rows_f[...] = tri[...].reshape(2048, 128).astype(F32)
    for block in range(8):
        lines = (block * 2, block * 2 + 16, block * 2 + 1, block * 2 + 17)
        value = jnp.concatenate(
            [rows_f[pl.ds(block * 2 + half, 128, stride=16), :] for half in range(2)], axis=1
        )
        tnorm = layer_norm(value, 0).T.astype(BF16)
        update = matmul(tnorm, w_tri_out[...])
        updated = []
        for place, line in enumerate(lines):
            cells = slice(line * 64, line * 64 + 64)
            change = gate[cells, :] * update[place * 64 : place * 64 + 64]
            updated.append((pair[cells, :].astype(F32) + change).astype(BF16))
            new_pair[cells, :] = updated[-1]
        pnorm = layer_norm(jnp.concatenate(updated, axis=0).astype(F32), 1).astype(BF16)
        bias = contract_last(w_bias[...], pnorm)
        for half in range(2):
            rows = pl.ds(block * 2 + half, 64, stride=16)
            bias_f[rows, :] = bias[:, half * 128 : half * 128 + 128]
    bias_in[...] = bias_f[...].astype(BF16).reshape(4, 16, 16, 128)

    def send_bias(layers, slot):
        def body(step):
            peer = after(head, step, 16)
            push(bias_in.at[layers, peer], bias_all.at[layers, head], slot, col_place(peer))

        each(15, body)
        keep(bias_in.at[layers, head], bias_all.at[layers, head], slot)

    send_bias(pl.ds(0, 1), BIAS_FIRST)
    send_bias(pl.ds(1, 3), BIAS_REST)
    wait_bytes(keyval.at[:, 0], recv.at[KV_CORE])
    for group in range(2):
        rows = slice(group * 256, group * 256 + 256)
        keys = keyval[:, :, group].reshape(1024, WIDE)
        score[rows, :] = contract_last(query[rows, :], keys)

    def bias_rows(layer):
        return jnp.concatenate(
            [
                jnp.concatenate(
                    [bias_all[layer, src, :, part * 64 : part * 64 + 64] for src in range(16)],
                    axis=-1,
                )
                for part in range(2)
            ],
            axis=0,
        )

    wait_bytes(bias_all.at[0, pl.ds(0, 1)], local.at[BIAS_FIRST])
    wait_bytes(bias_all.at[0, pl.ds(0, 15)], recv.at[BIAS_FIRST])
    first_bias = bias_rows(0)
    biases[0] = first_bias
    first_bias = first_bias.astype(F32)
    present = mask_f > 0.0
    for sample in range(16):
        rows = slice(sample * 32, sample * 32 + 32)
        logits = score[rows, :] * HEAD_DIM ** (-0.5) + first_bias
        logits = jnp.where(present, logits, -1000000000.0)
        expo = jnp.exp(logits - jnp.max(logits, axis=1, keepdims=True))
        probs[rows, :] = (expo * (1.0 / jnp.sum(expo, axis=1, keepdims=True))).astype(BF16)
    for group in range(2):
        rows = slice(group * 256, group * 256 + 256)
        values = keyval[:, :, 2 + group].reshape(1024, WIDE)
        context = matmul(probs[rows, :], values)
        gated = (agate[rows, :] * context * own_in[...]).astype(BF16)
        gathered = matmul(gated, gather_in[...]).astype(BF16)
        heads_in[group * 8 : group * 8 + 8] = gathered.reshape(8, 32, 128)

    def send_heads(step):
        peer = after(head, step, 16)
        push(heads_in.at[peer], heads_all.at[head], HEADS_OUT, col_place(peer))

    each(15, send_heads)
    keep(heads_in.at[head], heads_all.at[head], HEADS_OUT)
    wait_bytes(bias_all.at[pl.ds(0, 3), 0], local.at[BIAS_REST])
    wait_bytes(bias_all.at[pl.ds(0, 3), pl.ds(0, 15)], recv.at[BIAS_REST])
    for layer in range(1, 4):
        biases[layer] = bias_rows(layer)
    wait_bytes(w_out_all.at[0], recv.at[OUT_CORE])
    wait_bytes(heads_all.at[pl.ds(0, 1)], local.at[HEADS_OUT])
    wait_bytes(heads_all.at[pl.ds(0, 15)], recv.at[HEADS_OUT])
    merged = jnp.concatenate([heads_all[src, :, 0:HEAD_DIM] for src in range(16)], axis=-1)
    for half in range(2):
        weights = w_out_all[half].reshape(HEADS * HEAD_DIM, 384)
        attended[:, half * 384 : half * 384 + 384] = matmul(merged, weights).astype(BF16)

    for slot in (LEFT_X, RIGHT_X, SUM_X):
        for step in range(4):
            wait_bytes(left_x.at[pl.ds(0, 4), pl.ds(0, 7)], send.at[slot + step])
    for slot in (LEFT_Z, RIGHT_Z, SUM_Z):
        wait_bytes(left_z.at[pl.ds(0, 15)], send.at[slot])
    for way in range(2):
        wait_bytes(left_all.at[0], send.at[LEFT_NEAR + way])
        wait_bytes(left_all.at[0, pl.ds(0, 128)], send.at[LEFT_FAR + way])
        wait_bytes(keyval_in, send.at[KV_Z_NEAR + way])
        wait_bytes(keyval_in.at[pl.ds(0, 2)], send.at[KV_Z_FAR + way])
        wait_bytes(keyval.at[pl.ds(0, 4), 0], send.at[KV_X_NEAR + way])
        wait_bytes(keyval.at[pl.ds(0, 2), 0], send.at[KV_X_FAR + way])
    wait_bytes(w_out_all.at[0, pl.ds(0, 3)], send.at[OUT_Z])
    wait_bytes(w_out_all.at[0, pl.ds(0, 12)], send.at[OUT_Y])
    wait_bytes(w_out_all.at[0], send.at[OUT_CORE])
    wait_bytes(keyval.at[:, 0], send.at[KV_CORE])
    wait_bytes(bias_all.at[0, pl.ds(0, 15)], send.at[BIAS_FIRST])
    wait_bytes(bias_all.at[pl.ds(0, 3), pl.ds(0, 15)], send.at[BIAS_REST])
    wait_bytes(heads_all.at[pl.ds(0, 15)], send.at[HEADS_OUT])


def per_device(pair, mask, w_tri_in, w_tri_out, w_bias, single, w_attn, w_out):
    vmem = pl.BlockSpec(memory_space=pltpu.VMEM)
    blocks = pltpu.VMEM((16, 8, 16, 128), BF16)
    new_pair, biases, attended = pl.pallas_call(
        whole_kernel,
        out_shape=(
            jax.ShapeDtypeStruct((2048, 128), BF16),
            jax.ShapeDtypeStruct((LAYERS, 32, 1024), BF16),
            jax.ShapeDtypeStruct((32, 768), BF16),
        ),
        in_specs=[pl.BlockSpec(memory_space=pltpu.HBM)] * 8,
        out_specs=(vmem, vmem, vmem),
        scratch_shapes=[
            pltpu.VMEM((2048, 128), BF16),
            pltpu.VMEM((1, 1024), jnp.int32),
            pltpu.VMEM((128, 640), BF16),
            pltpu.VMEM((128, 128), BF16),
            pltpu.VMEM((64, 128), BF16),
            pltpu.VMEM((512, 768), BF16),
            pltpu.VMEM((4 * HEAD_DIM, 768), BF16),
            pltpu.VMEM((HEAD_DIM, 768), BF16),
        ]
        + [blocks] * 9
        + [
            pltpu.VMEM((WIDE, 128), BF16),
            pltpu.VMEM((256, WIDE), F32),
            pltpu.VMEM((4, 256, 1024), BF16),
            pltpu.VMEM((1024, 256), BF16),
            pltpu.VMEM((16, 2, 4, 32, WIDE), BF16),
            pltpu.VMEM((4, 32, WIDE), BF16),
            pltpu.VMEM((2, HEADS, HEAD_DIM, 384), BF16),
            pltpu.VMEM((2048, 128), BF16),
            pltpu.VMEM((2048, 128), F32),
            pltpu.VMEM((2048, 128), F32),
            pltpu.VMEM((512, 128), BF16),
            pltpu.VMEM((512, WIDE), BF16),
            pltpu.VMEM((512, WIDE), F32),
            pltpu.VMEM((512, 1024), F32),
            pltpu.VMEM((1024, 128), F32),
            pltpu.VMEM((512, 1024), BF16),
            pltpu.VMEM((LAYERS, 16, 16, 128), BF16),
            pltpu.VMEM((LAYERS, 16, 16, 128), BF16),
            pltpu.VMEM((16, 32, 128), BF16),
            pltpu.VMEM((16, 32, 128), BF16),
            pltpu.SemaphoreType.DMA((SLOTS,)),
            pltpu.SemaphoreType.DMA((SLOTS,)),
            pltpu.SemaphoreType.DMA((SLOTS,)),
            pltpu.SemaphoreType.DMA((8,)),
        ],
        compiler_params=pltpu.CompilerParams(
            collective_id=0, has_side_effects=True, vmem_limit_bytes=60 * 1024 * 1024
        ),
        name="whole",
    )(
        pair.reshape(2048, 128),
        mask.reshape(1, 1024),
        w_tri_in,
        w_tri_out,
        w_bias.T,
        single.reshape(512, 768),
        w_attn.transpose(1, 2, 0).reshape(4 * HEAD_DIM, 768),
        w_out,
    )
    return (
        new_pair.reshape(32, 64, 128),
        biases.reshape(LAYERS, 1, 32, 1024),
        attended.reshape(1, 32, 768),
    )


def solution(mesh):
    fine = Mesh(mesh.devices.reshape(4, 4, 2, 4, 4), ("z_hi", "x", "core", "y", "z_lo"))
    placed = (
        P(ROW, COL, None),
        P(),
        P(),
        P(),
        P(),
        P(None, ROW, None),
        P(None, COL, None),
        P(COL, None),
    )
    return jax.shard_map(
        per_device,
        mesh=fine,
        in_specs=placed,
        out_specs=(P(ROW, COL, None), P(None, COL, ROW, None), P(COL, ROW, None)),
        check_vma=False,
    )
```

```python
import jax
import jax.numpy as jnp
from jax import lax
from jax.experimental import pallas as pl
from jax.experimental.pallas import tpu as pltpu
from jax.sharding import Mesh
from jax.sharding import PartitionSpec as P

HEADS = 16
HEAD_DIM = 48
LAYERS = 4
WIDE = 8 * HEAD_DIM
ROW = ("z_hi", "x", "core")
COL = ("y", "z_lo")
BF16 = jnp.bfloat16
F32 = jnp.float32

LEFT_X, RIGHT_X, SUM_X = 0, 4, 8
RIGHT_Z, SUM_Z = 13, 14
OUT_Z, OUT_Y, OUT_CORE, KV_CORE = 15, 16, 17, 18
BIAS_FIRST, BIAS_REST, HEADS_OUT = 19, 20, 21
LEFT_FAR, KV_Z_NEAR, KV_Z_FAR, KV_X_NEAR, KV_X_FAR = 22, 24, 26, 28, 30
LEFT_UP, LEFT_DOWN, LEFT_QUARTER = 32, 36, 40
SLOTS = 44


def block_of(index):
    return sum((index >= HEAD_DIM * edge).astype(jnp.int32) for edge in range(1, 32))


def layer_norm(value, axis):
    mean = jnp.mean(value, axis=axis, keepdims=True)
    centred = value - mean
    var = jnp.mean(centred * centred, axis=axis, keepdims=True)
    return centred * lax.rsqrt(var + 1e-05)


def each(count, body):
    lax.fori_loop(0, count, lambda step, carry: (body(step), carry)[1], 0)


def wait_bytes(ref, sem):
    pltpu.make_async_copy(ref, ref, sem).wait()


def contract_last(a, b):
    return lax.dot_general(a, b, (((1,), (1,)), ((), ())), preferred_element_type=F32)


def matmul(a, b):
    return jnp.dot(a, b, preferred_element_type=F32)


def whole_kernel(
    pair_h, mask_h, w_tri_in_h, w_tri_out_h, w_bias_h, single_h, w_attn_h, w_out_h,
    new_pair, biases, attended,
    pair, mask, w_tri_in, w_tri_out, w_bias, single, w_attn, w_out,
    left_in, right_in, left_x, right_x, left_z, right_z, sums, sums_x, tri,
    gather_in, own_in,
    left_all, right_own, keyval, keyval_in, w_out_all,
    normed, gate, rows_f, w_in_t, query, agate, score, bias_f, probs,
    bias_in, bias_all, heads_in, heads_all,
    send, recv, local, load,
):
    z_hi, z_lo = lax.axis_index("z_hi"), lax.axis_index("z_lo")
    x, core, y = lax.axis_index("x"), lax.axis_index("core"), lax.axis_index("y")
    z, xc, head = z_hi * 4 + z_lo, x * 2 + core, y * 4 + z_lo

    def z_place(peer):
        return {"z_hi": lax.div(peer, 4), "z_lo": lax.rem(peer, 4)}

    def xc_place(peer):
        return {"x": lax.div(peer, 2), "core": lax.rem(peer, 2)}

    def col_place(peer):
        return {"y": lax.div(peer, 4), "z_lo": lax.rem(peer, 4)}

    def after(place, step, size):
        return lax.rem(place + 1 + step, size)

    def near(axis, place, step, size):
        return {axis: after(place, step, size)}

    loads = [
        pltpu.make_async_copy(src, dst, load.at[slot])
        for slot, (src, dst) in enumerate(
            (
                (pair_h, pair), (w_tri_in_h, w_tri_in), (mask_h, mask), (w_out_h, w_out),
                (w_attn_h, w_attn), (single_h, single), (w_tri_out_h, w_tri_out), (w_bias_h, w_bias),
            )
        )
    ]
    for copy in loads:
        copy.start()
    barrier = pltpu.get_barrier_semaphore()

    def greet(peer):
        pl.semaphore_signal(barrier, inc=1, device_id=peer, device_id_type=pl.DeviceIdType.MESH)

    each(15, lambda step: greet(z_place(after(z, step, 16))))
    each(7, lambda step: greet(xc_place(after(xc, step, 8))))
    each(15, lambda step: greet(col_place(after(head, step, 16))))

    def push(src, dst, slot, peer):
        pltpu.make_async_remote_copy(
            src_ref=src, dst_ref=dst, send_sem=send.at[slot], recv_sem=recv.at[slot],
            device_id=peer, device_id_type=pl.DeviceIdType.MESH,
        ).start()

    def keep(src, dst, slot):
        pltpu.make_async_copy(src, dst, local.at[slot]).start()

    def quarter(step):
        return after(z_hi, step, 4)

    def over_x(src, dst, slot, step):
        part = pl.ds(quarter(step) * 4, 4)

        def body(other):
            peer = after(xc, other, 8)
            push(src.at[part, peer], dst.at[part, xc], slot + step, xc_place(peer))

        each(7, body)
        keep(src.at[part, xc], dst.at[part, xc], slot + step)

    def end_x(dst, slot, step):
        wait_bytes(dst.at[0, pl.ds(0, 4)], local.at[slot + step])
        wait_bytes(dst.at[pl.ds(0, 4), pl.ds(0, 7)], recv.at[slot + step])

    def over_z(src, dst, slot, step):
        def body(low):
            peer = quarter(step) * 4 + low

            @pl.when(peer != z)
            def _():
                push(src.at[peer], dst.at[z], slot, z_place(peer))

            @pl.when(peer == z)
            def _():
                keep(src.at[z], dst.at[z], slot)

        each(4, body)

    def end_z(dst, slot):
        wait_bytes(dst.at[pl.ds(0, 1)], local.at[slot])
        wait_bytes(dst.at[pl.ds(0, 15)], recv.at[slot])

    for copy in loads[:3]:
        copy.wait()
    mask_f = mask[...].astype(F32)
    lane = lax.broadcasted_iota(jnp.int32, (1024, 128), 1)
    token = lax.broadcasted_iota(jnp.int32, (1024, 128), 0)
    low_lane = jnp.where(lane < 64, lane, lane - 64)
    chosen = (token == head * 64 + low_lane).astype(F32).astype(BF16)
    col_mask = matmul(jnp.broadcast_to(mask_f, (16, 1024)).astype(BF16), chosen)
    token = lax.broadcasted_iota(jnp.int32, (16, 1024), 1)
    line = lax.broadcasted_iota(jnp.int32, (16, 1024), 0) * 2 + (z_hi * 8 + xc) * 32
    even = jnp.sum(jnp.where(token == line, mask_f, 0.0), axis=1, keepdims=True)
    odd = jnp.sum(jnp.where(token == line + 1, mask_f, 0.0), axis=1, keepdims=True)
    low = lax.broadcasted_iota(jnp.int32, (16, 128), 1) < 64
    cell_mask = jnp.where(low, even, odd) * col_mask

    w_in_t[...] = w_tri_in[:, 0:512].T

    def factor(block, first):
        rows = slice(block * 256, block * 256 + 256)
        both = contract_last(w_in_t[first : first + 256, :], normed[rows, :])
        value = jax.nn.sigmoid(both[128:]) * both[:128]
        for half in range(2):
            line = block * 2 + half
            part = value[:, half * 128 : half * 128 + 128] * cell_mask[line : line + 1]
            rows_f[pl.ds(line, 128, stride=16), :] = part

    for block in range(8):
        rows = slice(block * 256, block * 256 + 256)
        normed[rows, :] = layer_norm(pair[rows, :].astype(F32), 1).astype(BF16)
        factor(block, 0)
    left_in[...] = rows_f[...].astype(BF16).reshape(16, 8, 16, 128)
    pl.semaphore_wait(barrier, 37)
    for step in range(4):
        over_x(left_in, left_x, LEFT_X, step)
    for block in range(8):
        factor(block, 256)
    right_in[...] = rows_f[...].astype(BF16).reshape(16, 8, 16, 128)
    for step in range(4):
        end_x(left_x, LEFT_X, step)
        over_z(left_x, left_z, LEFT_QUARTER + step, step)
    for step in range(4):
        over_x(right_in, right_x, RIGHT_X, step)
    loads[3].wait()
    half_out = w_out.at[:, pl.ds(pl.multiple_of(core * 384, 128), 384)]
    each(3, lambda step: push(half_out, w_out_all.at[core, head], OUT_Z, near("z_lo", z_lo, step, 4)))
    keep(half_out, w_out_all.at[core, head], OUT_Z)

    for copy in loads[4:]:
        copy.wait()
    lane = lax.broadcasted_iota(jnp.int32, (1, 4 * WIDE), 1)
    block = block_of(lane)
    source = lane - HEAD_DIM * block + HEAD_DIM * sum((block >= 8 * n).astype(jnp.int32) for n in (1, 2, 3))
    place = lax.broadcasted_iota(jnp.int32, (4 * HEAD_DIM, 4 * WIDE), 0)
    spread = (place == source).astype(F32).astype(BF16)
    place = lax.broadcasted_iota(jnp.int32, (256, WIDE), 0)
    own_block = ((place >= 32 * block[:, :WIDE]) & (place < 32 * block[:, :WIDE] + 32)).astype(F32)
    lane = lax.broadcasted_iota(jnp.int32, (WIDE, 128), 1)
    place = lax.broadcasted_iota(jnp.int32, (WIDE, 128), 0)
    gather = (place - HEAD_DIM * block_of(place) == lane).astype(F32).astype(BF16)
    own_in[...] = own_block
    gather_in[...] = gather
    w_wide = matmul(w_attn[...].T, spread).astype(BF16)
    for group in range(2):
        rows = slice(group * 256, group * 256 + 256)
        xn = layer_norm(single[rows, :].astype(F32), 1).astype(BF16)
        wide = matmul(xn, w_wide)
        query[rows, :] = (wide[:, 0:WIDE] * own_in[...]).astype(BF16)
        for which in range(2):
            part = wide[:, WIDE * (which + 1) : WIDE * (which + 2)] * own_in[...]
            packed = jnp.sum(part.reshape(8, 32, WIDE), axis=0)
            keyval_in[which * 2 + group] = packed.astype(BF16)
        agate[rows, :] = jax.nn.sigmoid(wide[:, 3 * WIDE :])

    def sent_z(slot, step):
        wait_bytes(left_z.at[pl.ds(0, 3 if step == 3 else 4)], send.at[slot + step])

    for step in range(4):
        end_x(right_x, RIGHT_X, step)
        sent_z(LEFT_QUARTER, step)
        over_z(right_x, right_z, RIGHT_Z, step)
    wait_bytes(w_out_all.at[0, pl.ds(0, 1)], local.at[OUT_Z])
    wait_bytes(w_out_all.at[0, pl.ds(0, 3)], recv.at[OUT_Z])
    quad = w_out_all.at[core, pl.ds(y * 4, 4)]
    each(3, lambda step: push(quad, quad, OUT_Y, near("y", y, step, 4)))
    for block in range(8):
        rows = slice(block * 256, block * 256 + 256)
        gate[rows, :] = jax.nn.sigmoid(matmul(normed[rows, :], w_tri_in[:, 512:640]))

    def tiles(blocks, z_part, part):
        pieces = [blocks[z_part * 4 + low, :, :, part * 64 : part * 64 + 64] for low in range(4)]
        return jnp.concatenate(pieces, axis=-1).reshape(128, 256)

    up, down = after(y, 0, 4), after(y, 2, 4)
    for step in range(4):
        if step == 3:
            wait_bytes(left_z.at[pl.ds(0, 1)], local.at[LEFT_QUARTER + step])
        wait_bytes(left_z.at[pl.ds(0, 3 if step == 3 else 4)], recv.at[LEFT_QUARTER + step])
        source = lax.rem(z_hi + 3 - step, 4)
        for part in range(2):
            left_all[y, source, :, part * 128 : part * 128 + 128] = tiles(left_z, source, part).T
        own = left_all.at[y, source]
        push(own, own, LEFT_UP + step, {"y": up})
        push(own, own, LEFT_DOWN + step, {"y": down})
    for step in range(4):
        source = lax.rem(z_hi + 3 - step, 4)
        wait_bytes(left_all.at[y, 0], recv.at[LEFT_UP + step])
        passed = left_all.at[down, source, pl.ds(0, 128)]
        push(passed, passed, LEFT_FAR, {"y": up})
        wait_bytes(left_all.at[y, 0], recv.at[LEFT_DOWN + step])
        passed = left_all.at[up, source, pl.ds(128, 128)]
        push(passed, passed, LEFT_FAR + 1, {"y": down})
    end_z(right_z, RIGHT_Z)
    mine = keyval.at[z_hi * 4 + x, core]
    z_up, z_down, x_up, x_down = after(z_hi, 0, 4), after(z_hi, 2, 4), after(x, 0, 4), after(x, 2, 4)
    push(keyval_in, mine, KV_Z_NEAR, {"z_hi": z_up})
    push(keyval_in, mine, KV_Z_NEAR + 1, {"z_hi": z_down})
    keep(keyval_in, mine, KV_Z_NEAR)
    for z_part in range(4):
        for part in range(2):
            first = z_part * 256 + part * 128
            right_own[first : first + 128, :] = tiles(right_z, z_part, part)
    for way in range(2):
        wait_bytes(left_all.at[0, pl.ds(0, 2)], recv.at[LEFT_FAR + way])
    for step in range(4):
        part = quarter(step)
        product = sum(
            matmul(left_all[part, quad], right_own[quad * 256 : quad * 256 + 256]) for quad in range(4)
        )
        product = product.astype(BF16).reshape(8, 2, 16, 256)
        for low in range(4):
            cut = slice(low * 64, low * 64 + 64)
            sums[part * 4 + low] = jnp.concatenate(
                [product[:, 0, :, cut], product[:, 1, :, cut]], axis=-1
            )
        over_x(sums, sums_x, SUM_X, step)
    for step in range(4):
        end_x(sums_x, SUM_X, step)
        over_z(sums_x, tri, SUM_Z, step)
    wait_bytes(keyval_in, local.at[KV_Z_NEAR])
    wait_bytes(keyval_in, recv.at[KV_Z_NEAR])
    passed = keyval.at[z_down * 4 + x, core, pl.ds(0, 2)]
    push(passed, passed, KV_Z_FAR, {"z_hi": z_up})
    wait_bytes(keyval_in, recv.at[KV_Z_NEAR + 1])
    passed = keyval.at[z_up * 4 + x, core, pl.ds(2, 2)]
    push(passed, passed, KV_Z_FAR + 1, {"z_hi": z_down})

    def over_x_ring(part):
        block = keyval.at[part * 4 + x, core]
        push(block, block, KV_X_NEAR, {"x": x_up})
        push(block, block, KV_X_NEAR + 1, {"x": x_down})

    each(3, lambda step: over_x_ring(lax.rem(z_hi + 3 + step, 4)))
    wait_bytes(w_out_all.at[0, pl.ds(0, 12)], recv.at[OUT_Y])
    push(w_out_all.at[core], w_out_all.at[core], OUT_CORE, {"core": 1 - core})
    wait_bytes(keyval_in.at[pl.ds(0, 2)], recv.at[KV_Z_FAR])
    wait_bytes(keyval_in.at[pl.ds(0, 2)], recv.at[KV_Z_FAR + 1])
    over_x_ring(lax.rem(z_hi + 2, 4))

    def pass_x(first, src, slot, place):
        def body(part):
            passed = keyval.at[part * 4 + src, core, pl.ds(first, 2)]
            push(passed, passed, slot, place)

        wait_bytes(keyval.at[pl.ds(0, 4), 0], recv.at[slot - 2])
        each(4, body)

    pass_x(0, x_down, KV_X_FAR, {"x": x_up})
    pass_x(2, x_up, KV_X_FAR + 1, {"x": x_down})
    wait_bytes(keyval.at[pl.ds(0, 2), 0], recv.at[KV_X_FAR])
    wait_bytes(keyval.at[pl.ds(0, 2), 0], recv.at[KV_X_FAR + 1])
    push(keyval.at[:, core], keyval.at[:, core], KV_CORE, {"core": 1 - core})

    end_z(tri, SUM_Z)
    rows_f[...] = tri[...].reshape(2048, 128).astype(F32)
    for block in range(8):
        lines = (block * 2, block * 2 + 16, block * 2 + 1, block * 2 + 17)
        value = jnp.concatenate(
            [rows_f[pl.ds(block * 2 + half, 128, stride=16), :] for half in range(2)], axis=1
        )
        tnorm = layer_norm(value, 0).T.astype(BF16)
        update = matmul(tnorm, w_tri_out[...])
        updated = []
        for place, line in enumerate(lines):
            cells = slice(line * 64, line * 64 + 64)
            change = gate[cells, :] * update[place * 64 : place * 64 + 64]
            updated.append((pair[cells, :].astype(F32) + change).astype(BF16))
            new_pair[cells, :] = updated[-1]
        pnorm = layer_norm(jnp.concatenate(updated, axis=0).astype(F32), 1).astype(BF16)
        bias = contract_last(w_bias[...], pnorm)
        for half in range(2):
            rows = pl.ds(block * 2 + half, 64, stride=16)
            bias_f[rows, :] = bias[:, half * 128 : half * 128 + 128]
    bias_in[...] = bias_f[...].astype(BF16).reshape(4, 16, 16, 128)

    def send_bias(layers, slot):
        def body(step):
            peer = after(head, step, 16)
            push(bias_in.at[layers, peer], bias_all.at[layers, head], slot, col_place(peer))

        each(15, body)
        keep(bias_in.at[layers, head], bias_all.at[layers, head], slot)

    send_bias(pl.ds(0, 1), BIAS_FIRST)
    send_bias(pl.ds(1, 3), BIAS_REST)
    wait_bytes(keyval.at[:, 0], recv.at[KV_CORE])
    for group in range(2):
        rows = slice(group * 256, group * 256 + 256)
        keys = keyval[:, :, group].reshape(1024, WIDE)
        score[rows, :] = contract_last(query[rows, :], keys)

    def bias_rows(layer):
        return jnp.concatenate(
            [
                jnp.concatenate(
                    [bias_all[layer, src, :, part * 64 : part * 64 + 64] for src in range(16)],
                    axis=-1,
                )
                for part in range(2)
            ],
            axis=0,
        )

    wait_bytes(bias_all.at[0, pl.ds(0, 1)], local.at[BIAS_FIRST])
    wait_bytes(bias_all.at[0, pl.ds(0, 15)], recv.at[BIAS_FIRST])
    first_bias = bias_rows(0)
    biases[0] = first_bias
    first_bias = first_bias.astype(F32)
    present = mask_f > 0.0
    for sample in range(16):
        rows = slice(sample * 32, sample * 32 + 32)
        logits = score[rows, :] * HEAD_DIM ** (-0.5) + first_bias
        logits = jnp.where(present, logits, -1000000000.0)
        expo = jnp.exp(logits - jnp.max(logits, axis=1, keepdims=True))
        probs[rows, :] = (expo * (1.0 / jnp.sum(expo, axis=1, keepdims=True))).astype(BF16)
    for group in range(2):
        rows = slice(group * 256, group * 256 + 256)
        values = keyval[:, :, 2 + group].reshape(1024, WIDE)
        context = matmul(probs[rows, :], values)
        gated = (agate[rows, :] * context * own_in[...]).astype(BF16)
        gathered = matmul(gated, gather_in[...]).astype(BF16)
        heads_in[group * 8 : group * 8 + 8] = gathered.reshape(8, 32, 128)

    def send_heads(step):
        peer = after(head, step, 16)
        push(heads_in.at[peer], heads_all.at[head], HEADS_OUT, col_place(peer))

    each(15, send_heads)
    keep(heads_in.at[head], heads_all.at[head], HEADS_OUT)
    wait_bytes(bias_all.at[pl.ds(0, 3), 0], local.at[BIAS_REST])
    wait_bytes(bias_all.at[pl.ds(0, 3), pl.ds(0, 15)], recv.at[BIAS_REST])
    for layer in range(1, 4):
        biases[layer] = bias_rows(layer)
    wait_bytes(w_out_all.at[0], recv.at[OUT_CORE])
    wait_bytes(heads_all.at[pl.ds(0, 1)], local.at[HEADS_OUT])
    wait_bytes(heads_all.at[pl.ds(0, 15)], recv.at[HEADS_OUT])
    merged = jnp.concatenate([heads_all[src, :, 0:HEAD_DIM] for src in range(16)], axis=-1)
    for half in range(2):
        weights = w_out_all[half].reshape(HEADS * HEAD_DIM, 384)
        attended[:, half * 384 : half * 384 + 384] = matmul(merged, weights).astype(BF16)

    for slot in (LEFT_X, RIGHT_X, SUM_X):
        for step in range(4):
            wait_bytes(left_x.at[pl.ds(0, 4), pl.ds(0, 7)], send.at[slot + step])
    for slot in (RIGHT_Z, SUM_Z):
        wait_bytes(left_z.at[pl.ds(0, 15)], send.at[slot])
    for way in range(2):
        for step in range(4):
            wait_bytes(left_all.at[0, 0], send.at[(LEFT_UP, LEFT_DOWN)[way] + step])
        wait_bytes(left_all.at[0, pl.ds(0, 2)], send.at[LEFT_FAR + way])
        wait_bytes(keyval_in, send.at[KV_Z_NEAR + way])
        wait_bytes(keyval_in.at[pl.ds(0, 2)], send.at[KV_Z_FAR + way])
        wait_bytes(keyval.at[pl.ds(0, 4), 0], send.at[KV_X_NEAR + way])
        wait_bytes(keyval.at[pl.ds(0, 2), 0], send.at[KV_X_FAR + way])
    wait_bytes(w_out_all.at[0, pl.ds(0, 3)], send.at[OUT_Z])
    wait_bytes(w_out_all.at[0, pl.ds(0, 12)], send.at[OUT_Y])
    wait_bytes(w_out_all.at[0], send.at[OUT_CORE])
    wait_bytes(keyval.at[:, 0], send.at[KV_CORE])
    wait_bytes(bias_all.at[0, pl.ds(0, 15)], send.at[BIAS_FIRST])
    wait_bytes(bias_all.at[pl.ds(0, 3), pl.ds(0, 15)], send.at[BIAS_REST])
    wait_bytes(heads_all.at[pl.ds(0, 15)], send.at[HEADS_OUT])


def per_device(pair, mask, w_tri_in, w_tri_out, w_bias, single, w_attn, w_out):
    vmem = pl.BlockSpec(memory_space=pltpu.VMEM)
    blocks = pltpu.VMEM((16, 8, 16, 128), BF16)
    new_pair, biases, attended = pl.pallas_call(
        whole_kernel,
        out_shape=(
            jax.ShapeDtypeStruct((2048, 128), BF16),
            jax.ShapeDtypeStruct((LAYERS, 32, 1024), BF16),
            jax.ShapeDtypeStruct((32, 768), BF16),
        ),
        in_specs=[pl.BlockSpec(memory_space=pltpu.HBM)] * 8,
        out_specs=(vmem, vmem, vmem),
        scratch_shapes=[
            pltpu.VMEM((2048, 128), BF16),
            pltpu.VMEM((1, 1024), jnp.int32),
            pltpu.VMEM((128, 640), BF16),
            pltpu.VMEM((128, 128), BF16),
            pltpu.VMEM((64, 128), BF16),
            pltpu.VMEM((512, 768), BF16),
            pltpu.VMEM((4 * HEAD_DIM, 768), BF16),
            pltpu.VMEM((HEAD_DIM, 768), BF16),
        ]
        + [blocks] * 9
        + [
            pltpu.VMEM((WIDE, 128), BF16),
            pltpu.VMEM((256, WIDE), F32),
            pltpu.VMEM((4, 4, 256, 256), BF16),
            pltpu.VMEM((1024, 256), BF16),
            pltpu.VMEM((16, 2, 4, 32, WIDE), BF16),
            pltpu.VMEM((4, 32, WIDE), BF16),
            pltpu.VMEM((2, HEADS, HEAD_DIM, 384), BF16),
            pltpu.VMEM((2048, 128), BF16),
            pltpu.VMEM((2048, 128), F32),
            pltpu.VMEM((2048, 128), F32),
            pltpu.VMEM((512, 128), BF16),
            pltpu.VMEM((512, WIDE), BF16),
            pltpu.VMEM((512, WIDE), F32),
            pltpu.VMEM((512, 1024), F32),
            pltpu.VMEM((1024, 128), F32),
            pltpu.VMEM((512, 1024), BF16),
            pltpu.VMEM((LAYERS, 16, 16, 128), BF16),
            pltpu.VMEM((LAYERS, 16, 16, 128), BF16),
            pltpu.VMEM((16, 32, 128), BF16),
            pltpu.VMEM((16, 32, 128), BF16),
            pltpu.SemaphoreType.DMA((SLOTS,)),
            pltpu.SemaphoreType.DMA((SLOTS,)),
            pltpu.SemaphoreType.DMA((SLOTS,)),
            pltpu.SemaphoreType.DMA((8,)),
        ],
        compiler_params=pltpu.CompilerParams(
            collective_id=0, has_side_effects=True, vmem_limit_bytes=60 * 1024 * 1024
        ),
        name="whole",
    )(
        pair.reshape(2048, 128),
        mask.reshape(1, 1024),
        w_tri_in,
        w_tri_out,
        w_bias.T,
        single.reshape(512, 768),
        w_attn.transpose(1, 2, 0).reshape(4 * HEAD_DIM, 768),
        w_out,
    )
    return (
        new_pair.reshape(32, 64, 128),
        biases.reshape(LAYERS, 1, 32, 1024),
        attended.reshape(1, 32, 768),
    )


def solution(mesh):
    fine = Mesh(mesh.devices.reshape(4, 4, 2, 4, 4), ("z_hi", "x", "core", "y", "z_lo"))
    placed = (
        P(ROW, COL, None),
        P(),
        P(),
        P(),
        P(),
        P(None, ROW, None),
        P(None, COL, None),
        P(COL, None),
    )
    return jax.shard_map(
        per_device,
        mesh=fine,
        in_specs=placed,
        out_specs=(P(ROW, COL, None), P(None, COL, ROW, None), P(COL, ROW, None)),
        check_vma=False,
    )
```

```python
import jax
import jax.numpy as jnp
from jax import lax
from jax.experimental import pallas as pl
from jax.experimental.pallas import tpu as pltpu
from jax.sharding import Mesh
from jax.sharding import PartitionSpec as P

HEADS = 16
HEAD_DIM = 48
LAYERS = 4
WIDE = 8 * HEAD_DIM
ROW = ("z_hi", "x", "core")
COL = ("y", "z_lo")
BF16 = jnp.bfloat16
F32 = jnp.float32

LEFT_X, RIGHT_X, SUM_X = 0, 4, 8
RIGHT_Z, SUM_Z = 13, 14
OUT_Z, OUT_Y, OUT_CORE, KV_CORE = 15, 16, 17, 18
BIAS_FIRST, BIAS_REST, HEADS_OUT = 19, 20, 21
LEFT_FAR, KV_Z_NEAR, KV_Z_FAR, KV_X_NEAR, KV_X_FAR = 22, 24, 26, 28, 30
LEFT_UP, LEFT_DOWN, LEFT_QUARTER = 32, 36, 40
SLOTS = 44


def block_of(index):
    return sum((index >= HEAD_DIM * edge).astype(jnp.int32) for edge in range(1, 32))


def layer_norm(value, axis):
    mean = jnp.mean(value, axis=axis, keepdims=True)
    centred = value - mean
    var = jnp.mean(centred * centred, axis=axis, keepdims=True)
    return centred * lax.rsqrt(var + 1e-05)


def each(count, body):
    lax.fori_loop(0, count, lambda step, carry: (body(step), carry)[1], 0)


def wait_bytes(ref, sem):
    pltpu.make_async_copy(ref, ref, sem).wait()


def contract_last(a, b):
    return lax.dot_general(a, b, (((1,), (1,)), ((), ())), preferred_element_type=F32)


def matmul(a, b):
    return jnp.dot(a, b, preferred_element_type=F32)


def whole_kernel(
    pair_h, mask_h, w_tri_in_h, w_tri_out_h, w_bias_h, single_h, w_attn_h, w_out_h,
    new_pair, biases, attended,
    pair, mask, w_tri_in, w_tri_out, w_bias, single, w_attn, w_out,
    left_in, right_in, left_x, right_x, left_z, right_z, sums, sums_x, tri,
    gather_in, own_in,
    left_all, right_own, keyval, keyval_in, w_out_all,
    normed, gate, rows_f, w_in_t, query, agate, score, bias_f, probs,
    bias_in, bias_all, heads_in, heads_all,
    send, recv, local, load,
):
    z_hi, z_lo = lax.axis_index("z_hi"), lax.axis_index("z_lo")
    x, core, y = lax.axis_index("x"), lax.axis_index("core"), lax.axis_index("y")
    z, xc, head = z_hi * 4 + z_lo, x * 2 + core, y * 4 + z_lo

    def z_place(peer):
        return {"z_hi": lax.div(peer, 4), "z_lo": lax.rem(peer, 4)}

    def xc_place(peer):
        return {"x": lax.div(peer, 2), "core": lax.rem(peer, 2)}

    def col_place(peer):
        return {"y": lax.div(peer, 4), "z_lo": lax.rem(peer, 4)}

    def after(place, step, size):
        return lax.rem(place + 1 + step, size)

    def near(axis, place, step, size):
        return {axis: after(place, step, size)}

    loads = [
        pltpu.make_async_copy(src, dst, load.at[slot])
        for slot, (src, dst) in enumerate(
            (
                (pair_h, pair), (w_tri_in_h, w_tri_in), (mask_h, mask), (w_out_h, w_out),
                (w_attn_h, w_attn), (single_h, single), (w_tri_out_h, w_tri_out), (w_bias_h, w_bias),
            )
        )
    ]
    for copy in loads:
        copy.start()
    barrier = pltpu.get_barrier_semaphore()

    def greet(peer):
        pl.semaphore_signal(barrier, inc=1, device_id=peer, device_id_type=pl.DeviceIdType.MESH)

    each(15, lambda step: greet(z_place(after(z, step, 16))))
    each(7, lambda step: greet(xc_place(after(xc, step, 8))))
    each(15, lambda step: greet(col_place(after(head, step, 16))))

    def push(src, dst, slot, peer):
        pltpu.make_async_remote_copy(
            src_ref=src, dst_ref=dst, send_sem=send.at[slot], recv_sem=recv.at[slot],
            device_id=peer, device_id_type=pl.DeviceIdType.MESH,
        ).start()

    def keep(src, dst, slot):
        pltpu.make_async_copy(src, dst, local.at[slot]).start()

    def quarter(step):
        return after(z_hi, step, 4)

    def over_x(src, dst, slot, step, first):
        part = pl.ds(first * 4, 4)

        def body(other):
            peer = after(xc, other, 8)
            push(src.at[part, peer], dst.at[part, xc], slot + step, xc_place(peer))

        each(7, body)
        keep(src.at[part, xc], dst.at[part, xc], slot + step)

    def end_x(dst, slot, step):
        wait_bytes(dst.at[0, pl.ds(0, 4)], local.at[slot + step])
        wait_bytes(dst.at[pl.ds(0, 4), pl.ds(0, 7)], recv.at[slot + step])

    def over_z(src, dst, slot, step):
        def body(low):
            peer = quarter(step) * 4 + low

            @pl.when(peer != z)
            def _():
                push(src.at[peer], dst.at[z], slot, z_place(peer))

            @pl.when(peer == z)
            def _():
                keep(src.at[z], dst.at[z], slot)

        each(4, body)

    def end_z(dst, slot):
        wait_bytes(dst.at[pl.ds(0, 1)], local.at[slot])
        wait_bytes(dst.at[pl.ds(0, 15)], recv.at[slot])

    for copy in loads[:3]:
        copy.wait()
    mask_f = mask[...].astype(F32)
    lane = lax.broadcasted_iota(jnp.int32, (1024, 128), 1)
    token = lax.broadcasted_iota(jnp.int32, (1024, 128), 0)
    low_lane = jnp.where(lane < 64, lane, lane - 64)
    chosen = (token == head * 64 + low_lane).astype(F32).astype(BF16)
    col_mask = matmul(jnp.broadcast_to(mask_f, (16, 1024)).astype(BF16), chosen)
    token = lax.broadcasted_iota(jnp.int32, (16, 1024), 1)
    line = lax.broadcasted_iota(jnp.int32, (16, 1024), 0) * 2 + (z_hi * 8 + xc) * 32
    even = jnp.sum(jnp.where(token == line, mask_f, 0.0), axis=1, keepdims=True)
    odd = jnp.sum(jnp.where(token == line + 1, mask_f, 0.0), axis=1, keepdims=True)
    low = lax.broadcasted_iota(jnp.int32, (16, 128), 1) < 64
    cell_mask = jnp.where(low, even, odd) * col_mask

    w_in_t[...] = w_tri_in[:, 0:512].T

    def factor(block, first):
        rows = slice(block * 256, block * 256 + 256)
        both = contract_last(w_in_t[first : first + 256, :], normed[rows, :])
        value = jax.nn.sigmoid(both[128:]) * both[:128]
        for half in range(2):
            line = block * 2 + half
            part = value[:, half * 128 : half * 128 + 128] * cell_mask[line : line + 1]
            rows_f[pl.ds(line, 128, stride=16), :] = part

    for block in range(8):
        rows = slice(block * 256, block * 256 + 256)
        normed[rows, :] = layer_norm(pair[rows, :].astype(F32), 1).astype(BF16)
        factor(block, 0)
    left_in[...] = rows_f[...].astype(BF16).reshape(16, 8, 16, 128)
    pl.semaphore_wait(barrier, 37)
    for step in range(4):
        over_z(left_in, left_z, LEFT_QUARTER + step, step)
    for block in range(8):
        factor(block, 256)
    right_in[...] = rows_f[...].astype(BF16).reshape(16, 8, 16, 128)
    for step in range(4):
        over_x(right_in, right_x, RIGHT_X, step, quarter(step))
    loads[3].wait()
    half_out = w_out.at[:, pl.ds(pl.multiple_of(core * 384, 128), 384)]
    each(3, lambda step: push(half_out, w_out_all.at[core, head], OUT_Z, near("z_lo", z_lo, step, 4)))
    keep(half_out, w_out_all.at[core, head], OUT_Z)

    for copy in loads[4:]:
        copy.wait()
    lane = lax.broadcasted_iota(jnp.int32, (1, 4 * WIDE), 1)
    block = block_of(lane)
    source = lane - HEAD_DIM * block + HEAD_DIM * sum((block >= 8 * n).astype(jnp.int32) for n in (1, 2, 3))
    place = lax.broadcasted_iota(jnp.int32, (4 * HEAD_DIM, 4 * WIDE), 0)
    spread = (place == source).astype(F32).astype(BF16)
    place = lax.broadcasted_iota(jnp.int32, (256, WIDE), 0)
    own_block = ((place >= 32 * block[:, :WIDE]) & (place < 32 * block[:, :WIDE] + 32)).astype(F32)
    lane = lax.broadcasted_iota(jnp.int32, (WIDE, 128), 1)
    place = lax.broadcasted_iota(jnp.int32, (WIDE, 128), 0)
    gather = (place - HEAD_DIM * block_of(place) == lane).astype(F32).astype(BF16)
    own_in[...] = own_block
    gather_in[...] = gather
    w_wide = matmul(w_attn[...].T, spread).astype(BF16)
    for group in range(2):
        rows = slice(group * 256, group * 256 + 256)
        xn = layer_norm(single[rows, :].astype(F32), 1).astype(BF16)
        wide = matmul(xn, w_wide)
        query[rows, :] = (wide[:, 0:WIDE] * own_in[...]).astype(BF16)
        for which in range(2):
            part = wide[:, WIDE * (which + 1) : WIDE * (which + 2)] * own_in[...]
            packed = jnp.sum(part.reshape(8, 32, WIDE), axis=0)
            keyval_in[which * 2 + group] = packed.astype(BF16)
        agate[rows, :] = jax.nn.sigmoid(wide[:, 3 * WIDE :])

    def sent_z(slot, step):
        wait_bytes(left_z.at[pl.ds(0, 3 if step == 3 else 4)], send.at[slot + step])

    for step in range(4):
        end_x(right_x, RIGHT_X, step)
        sent_z(LEFT_QUARTER, step)
        over_z(right_x, right_z, RIGHT_Z, step)
    mine = keyval.at[z_hi * 4 + x, core]
    z_up, z_down, x_up, x_down = after(z_hi, 0, 4), after(z_hi, 2, 4), after(x, 0, 4), after(x, 2, 4)
    push(keyval_in, mine, KV_Z_NEAR, {"z_hi": z_up})
    push(keyval_in, mine, KV_Z_NEAR + 1, {"z_hi": z_down})
    keep(keyval_in, mine, KV_Z_NEAR)
    wait_bytes(w_out_all.at[0, pl.ds(0, 1)], local.at[OUT_Z])
    wait_bytes(w_out_all.at[0, pl.ds(0, 3)], recv.at[OUT_Z])
    quad = w_out_all.at[core, pl.ds(y * 4, 4)]
    each(3, lambda step: push(quad, quad, OUT_Y, near("y", y, step, 4)))
    for block in range(8):
        rows = slice(block * 256, block * 256 + 256)
        gate[rows, :] = jax.nn.sigmoid(matmul(normed[rows, :], w_tri_in[:, 512:640]))

    def tiles(blocks, z_part, part):
        pieces = [blocks[z_part * 4 + low, :, :, part * 64 : part * 64 + 64] for low in range(4)]
        return jnp.concatenate(pieces, axis=-1).reshape(128, 256)

    up, down = after(y, 0, 4), after(y, 2, 4)

    def origin(step):
        return lax.rem(z_hi + 3 - step, 4)

    for step in range(4):
        if step == 3:
            wait_bytes(left_z.at[pl.ds(0, 1)], local.at[LEFT_QUARTER + step])
        wait_bytes(left_z.at[pl.ds(0, 3 if step == 3 else 4)], recv.at[LEFT_QUARTER + step])
        over_x(left_z, left_x, LEFT_X, step, origin(step))
    for step in range(4):
        end_x(left_x, LEFT_X, step)
        source = origin(step)
        for part in range(2):
            left_all[y, source, :, part * 128 : part * 128 + 128] = tiles(left_x, source, part).T
        own = left_all.at[y, source]
        push(own, own, LEFT_UP + step, {"y": up})
        push(own, own, LEFT_DOWN + step, {"y": down})
    for step in range(4):
        source = origin(step)
        wait_bytes(left_all.at[y, 0], recv.at[LEFT_UP + step])
        passed = left_all.at[down, source, pl.ds(0, 128)]
        push(passed, passed, LEFT_FAR, {"y": up})
        wait_bytes(left_all.at[y, 0], recv.at[LEFT_DOWN + step])
        passed = left_all.at[up, source, pl.ds(128, 128)]
        push(passed, passed, LEFT_FAR + 1, {"y": down})
    wait_bytes(keyval_in, local.at[KV_Z_NEAR])
    wait_bytes(keyval_in, recv.at[KV_Z_NEAR])
    wait_bytes(keyval_in, recv.at[KV_Z_NEAR + 1])

    def over_x_ring(part):
        block = keyval.at[part * 4 + x, core]
        push(block, block, KV_X_NEAR, {"x": x_up})
        push(block, block, KV_X_NEAR + 1, {"x": x_down})

    each(3, lambda step: over_x_ring(lax.rem(z_hi + 3 + step, 4)))
    end_z(right_z, RIGHT_Z)
    passed = keyval.at[z_down * 4 + x, core, pl.ds(0, 2)]
    push(passed, passed, KV_Z_FAR, {"z_hi": z_up})
    passed = keyval.at[z_up * 4 + x, core, pl.ds(2, 2)]
    push(passed, passed, KV_Z_FAR + 1, {"z_hi": z_down})
    for z_part in range(4):
        for part in range(2):
            first = z_part * 256 + part * 128
            right_own[first : first + 128, :] = tiles(right_z, z_part, part)
    for way in range(2):
        wait_bytes(left_all.at[0, pl.ds(0, 2)], recv.at[LEFT_FAR + way])
    for step in range(4):
        part = quarter(step)
        product = sum(
            matmul(left_all[part, quad], right_own[quad * 256 : quad * 256 + 256]) for quad in range(4)
        )
        product = product.astype(BF16).reshape(8, 2, 16, 256)
        for low in range(4):
            cut = slice(low * 64, low * 64 + 64)
            sums[part * 4 + low] = jnp.concatenate(
                [product[:, 0, :, cut], product[:, 1, :, cut]], axis=-1
            )
        over_x(sums, sums_x, SUM_X, step, part)
    for step in range(4):
        end_x(sums_x, SUM_X, step)
        over_z(sums_x, tri, SUM_Z, step)
    wait_bytes(w_out_all.at[0, pl.ds(0, 12)], recv.at[OUT_Y])
    push(w_out_all.at[core], w_out_all.at[core], OUT_CORE, {"core": 1 - core})
    wait_bytes(keyval_in.at[pl.ds(0, 2)], recv.at[KV_Z_FAR])
    wait_bytes(keyval_in.at[pl.ds(0, 2)], recv.at[KV_Z_FAR + 1])
    over_x_ring(lax.rem(z_hi + 2, 4))

    def pass_x(first, src, slot, place):
        def body(part):
            passed = keyval.at[part * 4 + src, core, pl.ds(first, 2)]
            push(passed, passed, slot, place)

        wait_bytes(keyval.at[pl.ds(0, 4), 0], recv.at[slot - 2])
        each(4, body)

    pass_x(0, x_down, KV_X_FAR, {"x": x_up})
    pass_x(2, x_up, KV_X_FAR + 1, {"x": x_down})
    wait_bytes(keyval.at[pl.ds(0, 2), 0], recv.at[KV_X_FAR])
    wait_bytes(keyval.at[pl.ds(0, 2), 0], recv.at[KV_X_FAR + 1])
    push(keyval.at[:, core], keyval.at[:, core], KV_CORE, {"core": 1 - core})

    end_z(tri, SUM_Z)
    rows_f[...] = tri[...].reshape(2048, 128).astype(F32)
    for block in range(8):
        lines = (block * 2, block * 2 + 16, block * 2 + 1, block * 2 + 17)
        value = jnp.concatenate(
            [rows_f[pl.ds(block * 2 + half, 128, stride=16), :] for half in range(2)], axis=1
        )
        tnorm = layer_norm(value, 0).T.astype(BF16)
        update = matmul(tnorm, w_tri_out[...])
        updated = []
        for place, line in enumerate(lines):
            cells = slice(line * 64, line * 64 + 64)
            change = gate[cells, :] * update[place * 64 : place * 64 + 64]
            updated.append((pair[cells, :].astype(F32) + change).astype(BF16))
            new_pair[cells, :] = updated[-1]
        pnorm = layer_norm(jnp.concatenate(updated, axis=0).astype(F32), 1).astype(BF16)
        bias = contract_last(w_bias[...], pnorm)
        for half in range(2):
            rows = pl.ds(block * 2 + half, 64, stride=16)
            bias_f[rows, :] = bias[:, half * 128 : half * 128 + 128]
    bias_in[...] = bias_f[...].astype(BF16).reshape(4, 16, 16, 128)

    def send_bias(layers, slot):
        def body(step):
            peer = after(head, step, 16)
            push(bias_in.at[layers, peer], bias_all.at[layers, head], slot, col_place(peer))

        each(15, body)
        keep(bias_in.at[layers, head], bias_all.at[layers, head], slot)

    send_bias(pl.ds(0, 1), BIAS_FIRST)
    send_bias(pl.ds(1, 3), BIAS_REST)
    wait_bytes(keyval.at[:, 0], recv.at[KV_CORE])
    for group in range(2):
        rows = slice(group * 256, group * 256 + 256)
        keys = keyval[:, :, group].reshape(1024, WIDE)
        score[rows, :] = contract_last(query[rows, :], keys)

    def bias_rows(layer):
        return jnp.concatenate(
            [
                jnp.concatenate(
                    [bias_all[layer, src, :, part * 64 : part * 64 + 64] for src in range(16)],
                    axis=-1,
                )
                for part in range(2)
            ],
            axis=0,
        )

    wait_bytes(bias_all.at[0, pl.ds(0, 1)], local.at[BIAS_FIRST])
    wait_bytes(bias_all.at[0, pl.ds(0, 15)], recv.at[BIAS_FIRST])
    first_bias = bias_rows(0)
    biases[0] = first_bias
    first_bias = first_bias.astype(F32)
    present = mask_f > 0.0
    for sample in range(16):
        rows = slice(sample * 32, sample * 32 + 32)
        logits = score[rows, :] * HEAD_DIM ** (-0.5) + first_bias
        logits = jnp.where(present, logits, -1000000000.0)
        expo = jnp.exp(logits - jnp.max(logits, axis=1, keepdims=True))
        probs[rows, :] = (expo * (1.0 / jnp.sum(expo, axis=1, keepdims=True))).astype(BF16)
    for group in range(2):
        rows = slice(group * 256, group * 256 + 256)
        values = keyval[:, :, 2 + group].reshape(1024, WIDE)
        context = matmul(probs[rows, :], values)
        gated = (agate[rows, :] * context * own_in[...]).astype(BF16)
        gathered = matmul(gated, gather_in[...]).astype(BF16)
        heads_in[group * 8 : group * 8 + 8] = gathered.reshape(8, 32, 128)

    def send_heads(step):
        peer = after(head, step, 16)
        push(heads_in.at[peer], heads_all.at[head], HEADS_OUT, col_place(peer))

    each(15, send_heads)
    keep(heads_in.at[head], heads_all.at[head], HEADS_OUT)
    wait_bytes(bias_all.at[pl.ds(0, 3), 0], local.at[BIAS_REST])
    wait_bytes(bias_all.at[pl.ds(0, 3), pl.ds(0, 15)], recv.at[BIAS_REST])
    for layer in range(1, 4):
        biases[layer] = bias_rows(layer)
    wait_bytes(w_out_all.at[0], recv.at[OUT_CORE])
    wait_bytes(heads_all.at[pl.ds(0, 1)], local.at[HEADS_OUT])
    wait_bytes(heads_all.at[pl.ds(0, 15)], recv.at[HEADS_OUT])
    merged = jnp.concatenate([heads_all[src, :, 0:HEAD_DIM] for src in range(16)], axis=-1)
    for half in range(2):
        weights = w_out_all[half].reshape(HEADS * HEAD_DIM, 384)
        attended[:, half * 384 : half * 384 + 384] = matmul(merged, weights).astype(BF16)

    for slot in (LEFT_X, RIGHT_X, SUM_X):
        for step in range(4):
            wait_bytes(left_x.at[pl.ds(0, 4), pl.ds(0, 7)], send.at[slot + step])
    for slot in (RIGHT_Z, SUM_Z):
        wait_bytes(left_z.at[pl.ds(0, 15)], send.at[slot])
    for way in range(2):
        for step in range(4):
            wait_bytes(left_all.at[0, 0], send.at[(LEFT_UP, LEFT_DOWN)[way] + step])
        wait_bytes(left_all.at[0, pl.ds(0, 2)], send.at[LEFT_FAR + way])
        wait_bytes(keyval_in, send.at[KV_Z_NEAR + way])
        wait_bytes(keyval_in.at[pl.ds(0, 2)], send.at[KV_Z_FAR + way])
        wait_bytes(keyval.at[pl.ds(0, 4), 0], send.at[KV_X_NEAR + way])
        wait_bytes(keyval.at[pl.ds(0, 2), 0], send.at[KV_X_FAR + way])
    wait_bytes(w_out_all.at[0, pl.ds(0, 3)], send.at[OUT_Z])
    wait_bytes(w_out_all.at[0, pl.ds(0, 12)], send.at[OUT_Y])
    wait_bytes(w_out_all.at[0], send.at[OUT_CORE])
    wait_bytes(keyval.at[:, 0], send.at[KV_CORE])
    wait_bytes(bias_all.at[0, pl.ds(0, 15)], send.at[BIAS_FIRST])
    wait_bytes(bias_all.at[pl.ds(0, 3), pl.ds(0, 15)], send.at[BIAS_REST])
    wait_bytes(heads_all.at[pl.ds(0, 15)], send.at[HEADS_OUT])


def per_device(pair, mask, w_tri_in, w_tri_out, w_bias, single, w_attn, w_out):
    vmem = pl.BlockSpec(memory_space=pltpu.VMEM)
    blocks = pltpu.VMEM((16, 8, 16, 128), BF16)
    new_pair, biases, attended = pl.pallas_call(
        whole_kernel,
        out_shape=(
            jax.ShapeDtypeStruct((2048, 128), BF16),
            jax.ShapeDtypeStruct((LAYERS, 32, 1024), BF16),
            jax.ShapeDtypeStruct((32, 768), BF16),
        ),
        in_specs=[pl.BlockSpec(memory_space=pltpu.HBM)] * 8,
        out_specs=(vmem, vmem, vmem),
        scratch_shapes=[
            pltpu.VMEM((2048, 128), BF16),
            pltpu.VMEM((1, 1024), jnp.int32),
            pltpu.VMEM((128, 640), BF16),
            pltpu.VMEM((128, 128), BF16),
            pltpu.VMEM((64, 128), BF16),
            pltpu.VMEM((512, 768), BF16),
            pltpu.VMEM((4 * HEAD_DIM, 768), BF16),
            pltpu.VMEM((HEAD_DIM, 768), BF16),
        ]
        + [blocks] * 9
        + [
            pltpu.VMEM((WIDE, 128), BF16),
            pltpu.VMEM((256, WIDE), F32),
            pltpu.VMEM((4, 4, 256, 256), BF16),
            pltpu.VMEM((1024, 256), BF16),
            pltpu.VMEM((16, 2, 4, 32, WIDE), BF16),
            pltpu.VMEM((4, 32, WIDE), BF16),
            pltpu.VMEM((2, HEADS, HEAD_DIM, 384), BF16),
            pltpu.VMEM((2048, 128), BF16),
            pltpu.VMEM((2048, 128), F32),
            pltpu.VMEM((2048, 128), F32),
            pltpu.VMEM((512, 128), BF16),
            pltpu.VMEM((512, WIDE), BF16),
            pltpu.VMEM((512, WIDE), F32),
            pltpu.VMEM((512, 1024), F32),
            pltpu.VMEM((1024, 128), F32),
            pltpu.VMEM((512, 1024), BF16),
            pltpu.VMEM((LAYERS, 16, 16, 128), BF16),
            pltpu.VMEM((LAYERS, 16, 16, 128), BF16),
            pltpu.VMEM((16, 32, 128), BF16),
            pltpu.VMEM((16, 32, 128), BF16),
            pltpu.SemaphoreType.DMA((SLOTS,)),
            pltpu.SemaphoreType.DMA((SLOTS,)),
            pltpu.SemaphoreType.DMA((SLOTS,)),
            pltpu.SemaphoreType.DMA((8,)),
        ],
        compiler_params=pltpu.CompilerParams(
            collective_id=0, has_side_effects=True, vmem_limit_bytes=60 * 1024 * 1024
        ),
        name="whole",
    )(
        pair.reshape(2048, 128),
        mask.reshape(1, 1024),
        w_tri_in,
        w_tri_out,
        w_bias.T,
        single.reshape(512, 768),
        w_attn.transpose(1, 2, 0).reshape(4 * HEAD_DIM, 768),
        w_out,
    )
    return (
        new_pair.reshape(32, 64, 128),
        biases.reshape(LAYERS, 1, 32, 1024),
        attended.reshape(1, 32, 768),
    )


def solution(mesh):
    fine = Mesh(mesh.devices.reshape(4, 4, 2, 4, 4), ("z_hi", "x", "core", "y", "z_lo"))
    placed = (
        P(ROW, COL, None),
        P(),
        P(),
        P(),
        P(),
        P(None, ROW, None),
        P(None, COL, None),
        P(COL, None),
    )
    return jax.shard_map(
        per_device,
        mesh=fine,
        in_specs=placed,
        out_specs=(P(ROW, COL, None), P(None, COL, ROW, None), P(COL, ROW, None)),
        check_vma=False,
    )
```

```python
import jax
import jax.numpy as jnp
from jax import lax
from jax.experimental import pallas as pl
from jax.experimental.pallas import tpu as pltpu
from jax.sharding import Mesh
from jax.sharding import PartitionSpec as P

HEADS = 16
HEAD_DIM = 48
LAYERS = 4
WIDE = 8 * HEAD_DIM
ROW = ("z_hi", "x", "core")
COL = ("y", "z_lo")
BF16 = jnp.bfloat16
F32 = jnp.float32

LEFT_X, RIGHT_X, SUM_X = 0, 4, 8
SUM_Z = 14
OUT_Z, OUT_Y, OUT_CORE, KV_CORE = 15, 16, 17, 18
BIAS_FIRST, BIAS_REST, HEADS_OUT = 19, 20, 21
LEFT_FAR, KV_Z_NEAR, KV_Z_FAR, KV_X_NEAR, KV_X_FAR = 22, 24, 26, 28, 30
LEFT_UP, LEFT_DOWN, LEFT_QUARTER, RIGHT_QUARTER = 32, 36, 40, 44
SLOTS = 48


def block_of(index):
    return sum((index >= HEAD_DIM * edge).astype(jnp.int32) for edge in range(1, 32))


def layer_norm(value, axis):
    mean = jnp.mean(value, axis=axis, keepdims=True)
    centred = value - mean
    var = jnp.mean(centred * centred, axis=axis, keepdims=True)
    return centred * lax.rsqrt(var + 1e-05)


def each(count, body):
    lax.fori_loop(0, count, lambda step, carry: (body(step), carry)[1], 0)


def wait_bytes(ref, sem):
    pltpu.make_async_copy(ref, ref, sem).wait()


def contract_last(a, b):
    return lax.dot_general(a, b, (((1,), (1,)), ((), ())), preferred_element_type=F32)


def matmul(a, b):
    return jnp.dot(a, b, preferred_element_type=F32)


def whole_kernel(
    pair_h, mask_h, w_tri_in_h, w_tri_out_h, w_bias_h, single_h, w_attn_h, w_out_h,
    new_pair_h, biases, attended,
    pair, mask, w_tri_in, w_tri_out, w_bias, single, w_attn, w_out,
    left_in, right_in, left_x, right_x, left_z, right_z, sums, sums_x, tri,
    gather_in, own_in,
    left_all, totals, keyval, keyval_in, w_out_all,
    normed, gate, rows_f, w_in_t, query, agate, score, bias_f, probs,
    bias_in, bias_all, heads_in, heads_all, new_pair,
    send, recv, local, load,
):
    z_hi, z_lo = lax.axis_index("z_hi"), lax.axis_index("z_lo")
    x, core, y = lax.axis_index("x"), lax.axis_index("core"), lax.axis_index("y")
    z, xc, head = z_hi * 4 + z_lo, x * 2 + core, y * 4 + z_lo

    def z_place(peer):
        return {"z_hi": lax.div(peer, 4), "z_lo": lax.rem(peer, 4)}

    def xc_place(peer):
        return {"x": lax.div(peer, 2), "core": lax.rem(peer, 2)}

    def col_place(peer):
        return {"y": lax.div(peer, 4), "z_lo": lax.rem(peer, 4)}

    def after(place, step, size):
        return lax.rem(place + 1 + step, size)

    def near(axis, place, step, size):
        return {axis: after(place, step, size)}

    loads = [
        pltpu.make_async_copy(src, dst, load.at[slot])
        for slot, (src, dst) in enumerate(
            (
                (pair_h, pair), (w_tri_in_h, w_tri_in), (mask_h, mask), (w_out_h, w_out),
                (w_attn_h, w_attn), (single_h, single), (w_tri_out_h, w_tri_out), (w_bias_h, w_bias),
            )
        )
    ]
    for copy in loads:
        copy.start()
    barrier = pltpu.get_barrier_semaphore()

    def greet(peer):
        pl.semaphore_signal(barrier, inc=1, device_id=peer, device_id_type=pl.DeviceIdType.MESH)

    each(15, lambda step: greet(z_place(after(z, step, 16))))
    each(7, lambda step: greet(xc_place(after(xc, step, 8))))
    each(15, lambda step: greet(col_place(after(head, step, 16))))

    def push(src, dst, slot, peer):
        pltpu.make_async_remote_copy(
            src_ref=src, dst_ref=dst, send_sem=send.at[slot], recv_sem=recv.at[slot],
            device_id=peer, device_id_type=pl.DeviceIdType.MESH,
        ).start()

    def keep(src, dst, slot):
        pltpu.make_async_copy(src, dst, local.at[slot]).start()

    def quarter(step):
        return after(z_hi, step, 4)

    def over_x(src, dst, slot, step, first):
        part = pl.ds(first * 4, 4)

        def body(other):
            peer = after(xc, other, 8)
            push(src.at[part, peer], dst.at[part, xc], slot + step, xc_place(peer))

        each(7, body)
        keep(src.at[part, xc], dst.at[part, xc], slot + step)

    def end_x(dst, slot, step):
        wait_bytes(dst.at[0, pl.ds(0, 4)], local.at[slot + step])
        wait_bytes(dst.at[pl.ds(0, 4), pl.ds(0, 7)], recv.at[slot + step])

    def over_z(src, dst, slot, step):
        def body(low):
            peer = quarter(step) * 4 + low

            @pl.when(peer != z)
            def _():
                push(src.at[peer], dst.at[z], slot, z_place(peer))

            @pl.when(peer == z)
            def _():
                keep(src.at[z], dst.at[z], slot)

        each(4, body)

    def end_z(dst, slot):
        wait_bytes(dst.at[pl.ds(0, 1)], local.at[slot])
        wait_bytes(dst.at[pl.ds(0, 15)], recv.at[slot])

    for copy in loads[:3]:
        copy.wait()
    mask_f = mask[...].astype(F32)
    lane = lax.broadcasted_iota(jnp.int32, (1024, 128), 1)
    token = lax.broadcasted_iota(jnp.int32, (1024, 128), 0)
    low_lane = jnp.where(lane < 64, lane, lane - 64)
    chosen = (token == head * 64 + low_lane).astype(F32).astype(BF16)
    col_mask = matmul(jnp.broadcast_to(mask_f, (16, 1024)).astype(BF16), chosen)
    token = lax.broadcasted_iota(jnp.int32, (16, 1024), 1)
    line = lax.broadcasted_iota(jnp.int32, (16, 1024), 0) * 2 + (z_hi * 8 + xc) * 32
    even = jnp.sum(jnp.where(token == line, mask_f, 0.0), axis=1, keepdims=True)
    odd = jnp.sum(jnp.where(token == line + 1, mask_f, 0.0), axis=1, keepdims=True)
    low = lax.broadcasted_iota(jnp.int32, (16, 128), 1) < 64
    cell_mask = jnp.where(low, even, odd) * col_mask

    w_in_t[...] = w_tri_in[:, 0:512].T

    def factor(block, first, half):
        rows = slice(block * 256, block * 256 + 256)
        parts = (quarter(half * 2), quarter(half * 2 + 1))
        weights = [
            w_in_t[pl.ds(pl.multiple_of(start + part * 32, 32), 32), :]
            for start in (first, first + 128)
            for part in parts
        ]
        both = contract_last(jnp.concatenate(weights, axis=0), normed[rows, :])
        value = jax.nn.sigmoid(both[64:]) * both[:64]
        for side in range(2):
            line = block * 2 + side
            masked = value[:, side * 128 : side * 128 + 128] * cell_mask[line : line + 1]
            for place, part in enumerate(parts):
                rows_f[pl.ds(part * 512 + line, 32, stride=16), :] = masked[place * 32 : place * 32 + 32]

    def rounded(dst, step):
        part = quarter(step)
        lines = rows_f[pl.ds(pl.multiple_of(part * 512, 512), 512), :]
        dst[pl.ds(part * 4, 4)] = lines.astype(BF16).reshape(4, 8, 16, 128)

    for half in range(2):
        for block in range(8):
            if half == 0:
                rows = slice(block * 256, block * 256 + 256)
                normed[rows, :] = layer_norm(pair[rows, :].astype(F32), 1).astype(BF16)
            factor(block, 0, half)
        if half == 0:
            pl.semaphore_wait(barrier, 37)
        for step in (half * 2, half * 2 + 1):
            rounded(left_in, step)
            over_z(left_in, left_z, LEFT_QUARTER + step, step)
    for half in range(2):
        for block in range(8):
            factor(block, 256, half)
        for step in (half * 2, half * 2 + 1):
            rounded(right_in, step)
            over_x(right_in, right_x, RIGHT_X, step, quarter(step))
    loads[3].wait()
    half_out = w_out.at[:, pl.ds(pl.multiple_of(core * 384, 128), 384)]
    each(3, lambda step: push(half_out, w_out_all.at[core, head], OUT_Z, near("z_lo", z_lo, step, 4)))
    keep(half_out, w_out_all.at[core, head], OUT_Z)

    for copy in loads[4:]:
        copy.wait()
    lane = lax.broadcasted_iota(jnp.int32, (1, 4 * WIDE), 1)
    block = block_of(lane)
    source = lane - HEAD_DIM * block + HEAD_DIM * sum((block >= 8 * n).astype(jnp.int32) for n in (1, 2, 3))
    place = lax.broadcasted_iota(jnp.int32, (4 * HEAD_DIM, 4 * WIDE), 0)
    spread = (place == source).astype(F32).astype(BF16)
    place = lax.broadcasted_iota(jnp.int32, (256, WIDE), 0)
    own_block = ((place >= 32 * block[:, :WIDE]) & (place < 32 * block[:, :WIDE] + 32)).astype(F32)
    lane = lax.broadcasted_iota(jnp.int32, (WIDE, 128), 1)
    place = lax.broadcasted_iota(jnp.int32, (WIDE, 128), 0)
    gather = (place - HEAD_DIM * block_of(place) == lane).astype(F32).astype(BF16)
    own_in[...] = own_block
    gather_in[...] = gather
    w_wide = matmul(w_attn[...].T, spread).astype(BF16)
    for group in range(2):
        rows = slice(group * 256, group * 256 + 256)
        xn = layer_norm(single[rows, :].astype(F32), 1).astype(BF16)
        wide = matmul(xn, w_wide)
        query[rows, :] = (wide[:, 0:WIDE] * own_in[...]).astype(BF16)
        for which in range(2):
            part = wide[:, WIDE * (which + 1) : WIDE * (which + 2)] * own_in[...]
            packed = jnp.sum(part.reshape(8, 32, WIDE), axis=0)
            keyval_in[which * 2 + group] = packed.astype(BF16)
        agate[rows, :] = jax.nn.sigmoid(wide[:, 3 * WIDE :])

    def sent_z(slot, step):
        wait_bytes(left_z.at[pl.ds(0, 3 if step == 3 else 4)], send.at[slot + step])

    for step in range(4):
        end_x(right_x, RIGHT_X, step)
        sent_z(LEFT_QUARTER, step)
        over_z(right_x, right_z, RIGHT_QUARTER + step, step)
    mine = keyval.at[z_hi * 4 + x, core]
    z_up, z_down, x_up, x_down = after(z_hi, 0, 4), after(z_hi, 2, 4), after(x, 0, 4), after(x, 2, 4)
    push(keyval_in, mine, KV_Z_NEAR, {"z_hi": z_up})
    push(keyval_in, mine, KV_Z_NEAR + 1, {"z_hi": z_down})
    keep(keyval_in, mine, KV_Z_NEAR)
    wait_bytes(w_out_all.at[0, pl.ds(0, 1)], local.at[OUT_Z])
    wait_bytes(w_out_all.at[0, pl.ds(0, 3)], recv.at[OUT_Z])
    quad = w_out_all.at[core, pl.ds(y * 4, 4)]
    each(3, lambda step: push(quad, quad, OUT_Y, near("y", y, step, 4)))
    for block in range(8):
        rows = slice(block * 256, block * 256 + 256)
        gate[rows, :] = jax.nn.sigmoid(matmul(normed[rows, :], w_tri_in[:, 512:640]))

    def tiles(blocks, z_part, part):
        pieces = [blocks[z_part * 4 + low, :, :, part * 64 : part * 64 + 64] for low in range(4)]
        return jnp.concatenate(pieces, axis=-1).reshape(128, 256)

    up, down = after(y, 0, 4), after(y, 2, 4)

    def origin(step):
        return lax.rem(z_hi + 3 - step, 4)

    def end_quarter(slot, step):
        if step == 3:
            wait_bytes(left_z.at[pl.ds(0, 1)], local.at[slot + step])
        wait_bytes(left_z.at[pl.ds(0, 3 if step == 3 else 4)], recv.at[slot + step])

    for step in range(4):
        end_quarter(LEFT_QUARTER, step)
        over_x(left_z, left_x, LEFT_X, step, origin(step))
    for step in range(4):
        end_x(left_x, LEFT_X, step)
        source = origin(step)
        for part in range(2):
            left_all[y, source, :, part * 128 : part * 128 + 128] = tiles(left_x, source, part).T
        own = left_all.at[y, source]
        push(own, own, LEFT_UP + step, {"y": up})
        push(own, own, LEFT_DOWN + step, {"y": down})
    for step in range(4):
        source = origin(step)
        wait_bytes(left_all.at[y, 0], recv.at[LEFT_UP + step])
        passed = left_all.at[down, source, pl.ds(0, 128)]
        push(passed, passed, LEFT_FAR, {"y": up})
        wait_bytes(left_all.at[y, 0], recv.at[LEFT_DOWN + step])
        passed = left_all.at[up, source, pl.ds(128, 128)]
        push(passed, passed, LEFT_FAR + 1, {"y": down})
    def over_x_ring(part):
        block = keyval.at[part * 4 + x, core]
        push(block, block, KV_X_NEAR, {"x": x_up})
        push(block, block, KV_X_NEAR + 1, {"x": x_down})

    for way in range(2):
        wait_bytes(left_all.at[0, pl.ds(0, 2)], recv.at[LEFT_FAR + way])
    for step in range(4):
        if step == 3:
            wait_bytes(keyval_in, local.at[KV_Z_NEAR])
            wait_bytes(keyval_in, recv.at[KV_Z_NEAR])
            wait_bytes(keyval_in, recv.at[KV_Z_NEAR + 1])
            each(3, lambda step: over_x_ring(lax.rem(z_hi + 3 + step, 4)))
        end_quarter(RIGHT_QUARTER, step)
        if step == 3:
            passed = keyval.at[z_down * 4 + x, core, pl.ds(0, 2)]
            push(passed, passed, KV_Z_FAR, {"z_hi": z_up})
            passed = keyval.at[z_up * 4 + x, core, pl.ds(2, 2)]
            push(passed, passed, KV_Z_FAR + 1, {"z_hi": z_down})
        source = origin(step)
        block = jnp.concatenate([tiles(right_z, source, part) for part in range(2)], axis=0)
        for turn in range(4):
            part = quarter(turn)
            product = matmul(left_all[part, source], block)
            if step > 0:
                product += totals[turn]
            if step < 3:
                totals[turn] = product
                continue
            product = product.astype(BF16).reshape(8, 2, 16, 256)
            for low in range(4):
                cut = slice(low * 64, low * 64 + 64)
                sums[part * 4 + low] = jnp.concatenate(
                    [product[:, 0, :, cut], product[:, 1, :, cut]], axis=-1
                )
            over_x(sums, sums_x, SUM_X, turn, part)
    for step in range(4):
        end_x(sums_x, SUM_X, step)
        over_z(sums_x, tri, SUM_Z, step)
    wait_bytes(w_out_all.at[0, pl.ds(0, 12)], recv.at[OUT_Y])
    push(w_out_all.at[core], w_out_all.at[core], OUT_CORE, {"core": 1 - core})
    wait_bytes(keyval_in.at[pl.ds(0, 2)], recv.at[KV_Z_FAR])
    wait_bytes(keyval_in.at[pl.ds(0, 2)], recv.at[KV_Z_FAR + 1])
    over_x_ring(lax.rem(z_hi + 2, 4))

    def pass_x(first, src, slot, place):
        def body(part):
            passed = keyval.at[part * 4 + src, core, pl.ds(first, 2)]
            push(passed, passed, slot, place)

        wait_bytes(keyval.at[pl.ds(0, 4), 0], recv.at[slot - 2])
        each(4, body)

    pass_x(0, x_down, KV_X_FAR, {"x": x_up})
    pass_x(2, x_up, KV_X_FAR + 1, {"x": x_down})
    wait_bytes(keyval.at[pl.ds(0, 2), 0], recv.at[KV_X_FAR])
    wait_bytes(keyval.at[pl.ds(0, 2), 0], recv.at[KV_X_FAR + 1])
    push(keyval.at[:, core], keyval.at[:, core], KV_CORE, {"core": 1 - core})

    end_z(tri, SUM_Z)
    rows_f[...] = tri[...].reshape(2048, 128).astype(F32)
    for block in range(8):
        lines = (block * 2, block * 2 + 16, block * 2 + 1, block * 2 + 17)
        value = jnp.concatenate(
            [rows_f[pl.ds(block * 2 + half, 128, stride=16), :] for half in range(2)], axis=1
        )
        tnorm = layer_norm(value, 0).T.astype(BF16)
        update = matmul(tnorm, w_tri_out[...])
        updated = []
        for place, line in enumerate(lines):
            cells = slice(line * 64, line * 64 + 64)
            change = gate[cells, :] * update[place * 64 : place * 64 + 64]
            updated.append((pair[cells, :].astype(F32) + change).astype(BF16))
            new_pair[cells, :] = updated[-1]
        pnorm = layer_norm(jnp.concatenate(updated, axis=0).astype(F32), 1).astype(BF16)
        bias = contract_last(w_bias[...], pnorm)
        for half in range(2):
            rows = pl.ds(block * 2 + half, 64, stride=16)
            bias_f[rows, :] = bias[:, half * 128 : half * 128 + 128]

    def send_bias(layers, slot):
        def body(step):
            peer = after(head, step, 16)
            push(bias_in.at[layers, peer], bias_all.at[layers, head], slot, col_place(peer))

        each(15, body)
        keep(bias_in.at[layers, head], bias_all.at[layers, head], slot)

    bias_in[0] = bias_f[0:256, :].astype(BF16).reshape(16, 16, 128)
    send_bias(pl.ds(0, 1), BIAS_FIRST)
    bias_in[1:4] = bias_f[256:1024, :].astype(BF16).reshape(3, 16, 16, 128)
    send_bias(pl.ds(1, 3), BIAS_REST)
    store = pltpu.make_async_copy(new_pair, new_pair_h, load.at[8])
    store.start()
    wait_bytes(keyval.at[:, 0], recv.at[KV_CORE])
    for group in range(2):
        rows = slice(group * 256, group * 256 + 256)
        keys = keyval[:, :, group].reshape(1024, WIDE)
        score[rows, :] = contract_last(query[rows, :], keys)

    def bias_rows(layer):
        return jnp.concatenate(
            [
                jnp.concatenate(
                    [bias_all[layer, src, :, part * 64 : part * 64 + 64] for src in range(16)],
                    axis=-1,
                )
                for part in range(2)
            ],
            axis=0,
        )

    wait_bytes(bias_all.at[0, pl.ds(0, 1)], local.at[BIAS_FIRST])
    wait_bytes(bias_all.at[0, pl.ds(0, 15)], recv.at[BIAS_FIRST])
    first_bias = bias_rows(0)
    biases[0] = first_bias
    first_bias = first_bias.astype(F32)
    present = mask_f > 0.0
    for sample in range(16):
        rows = slice(sample * 32, sample * 32 + 32)
        logits = score[rows, :] * HEAD_DIM ** (-0.5) + first_bias
        logits = jnp.where(present, logits, -1000000000.0)
        expo = jnp.exp(logits - jnp.max(logits, axis=1, keepdims=True))
        probs[rows, :] = (expo * (1.0 / jnp.sum(expo, axis=1, keepdims=True))).astype(BF16)
    for group in range(2):
        rows = slice(group * 256, group * 256 + 256)
        values = keyval[:, :, 2 + group].reshape(1024, WIDE)
        context = matmul(probs[rows, :], values)
        gated = (agate[rows, :] * context * own_in[...]).astype(BF16)
        gathered = matmul(gated, gather_in[...]).astype(BF16)
        heads_in[group * 8 : group * 8 + 8] = gathered.reshape(8, 32, 128)

    def send_heads(step):
        peer = after(head, step, 16)
        push(heads_in.at[peer], heads_all.at[head], HEADS_OUT, col_place(peer))

    each(15, send_heads)
    keep(heads_in.at[head], heads_all.at[head], HEADS_OUT)
    wait_bytes(bias_all.at[pl.ds(0, 3), 0], local.at[BIAS_REST])
    wait_bytes(bias_all.at[pl.ds(0, 3), pl.ds(0, 15)], recv.at[BIAS_REST])
    for layer in range(1, 4):
        biases[layer] = bias_rows(layer)
    wait_bytes(w_out_all.at[0], recv.at[OUT_CORE])
    wait_bytes(heads_all.at[pl.ds(0, 1)], local.at[HEADS_OUT])
    wait_bytes(heads_all.at[pl.ds(0, 15)], recv.at[HEADS_OUT])
    merged = jnp.concatenate([heads_all[src, :, 0:HEAD_DIM] for src in range(16)], axis=-1)
    for half in range(2):
        weights = w_out_all[half].reshape(HEADS * HEAD_DIM, 384)
        attended[:, half * 384 : half * 384 + 384] = matmul(merged, weights).astype(BF16)

    store.wait()
    for slot in (LEFT_X, RIGHT_X, SUM_X):
        for step in range(4):
            wait_bytes(left_x.at[pl.ds(0, 4), pl.ds(0, 7)], send.at[slot + step])
    for step in range(4):
        sent_z(RIGHT_QUARTER, step)
    wait_bytes(left_z.at[pl.ds(0, 15)], send.at[SUM_Z])
    for way in range(2):
        for step in range(4):
            wait_bytes(left_all.at[0, 0], send.at[(LEFT_UP, LEFT_DOWN)[way] + step])
        wait_bytes(left_all.at[0, pl.ds(0, 2)], send.at[LEFT_FAR + way])
        wait_bytes(keyval_in, send.at[KV_Z_NEAR + way])
        wait_bytes(keyval_in.at[pl.ds(0, 2)], send.at[KV_Z_FAR + way])
        wait_bytes(keyval.at[pl.ds(0, 4), 0], send.at[KV_X_NEAR + way])
        wait_bytes(keyval.at[pl.ds(0, 2), 0], send.at[KV_X_FAR + way])
    wait_bytes(w_out_all.at[0, pl.ds(0, 3)], send.at[OUT_Z])
    wait_bytes(w_out_all.at[0, pl.ds(0, 12)], send.at[OUT_Y])
    wait_bytes(w_out_all.at[0], send.at[OUT_CORE])
    wait_bytes(keyval.at[:, 0], send.at[KV_CORE])
    wait_bytes(bias_all.at[0, pl.ds(0, 15)], send.at[BIAS_FIRST])
    wait_bytes(bias_all.at[pl.ds(0, 3), pl.ds(0, 15)], send.at[BIAS_REST])
    wait_bytes(heads_all.at[pl.ds(0, 15)], send.at[HEADS_OUT])


def per_device(pair, mask, w_tri_in, w_tri_out, w_bias, single, w_attn, w_out):
    vmem = pl.BlockSpec(memory_space=pltpu.VMEM)
    blocks = pltpu.VMEM((16, 8, 16, 128), BF16)
    new_pair, biases, attended = pl.pallas_call(
        whole_kernel,
        out_shape=(
            jax.ShapeDtypeStruct((2048, 128), BF16),
            jax.ShapeDtypeStruct((LAYERS, 32, 1024), BF16),
            jax.ShapeDtypeStruct((32, 768), BF16),
        ),
        in_specs=[pl.BlockSpec(memory_space=pltpu.HBM)] * 8,
        out_specs=(pl.BlockSpec(memory_space=pltpu.HBM), vmem, vmem),
        scratch_shapes=[
            pltpu.VMEM((2048, 128), BF16),
            pltpu.VMEM((1, 1024), jnp.int32),
            pltpu.VMEM((128, 640), BF16),
            pltpu.VMEM((128, 128), BF16),
            pltpu.VMEM((64, 128), BF16),
            pltpu.VMEM((512, 768), BF16),
            pltpu.VMEM((4 * HEAD_DIM, 768), BF16),
            pltpu.VMEM((HEAD_DIM, 768), BF16),
        ]
        + [blocks] * 9
        + [
            pltpu.VMEM((WIDE, 128), BF16),
            pltpu.VMEM((256, WIDE), F32),
            pltpu.VMEM((4, 4, 256, 256), BF16),
            pltpu.VMEM((4, 256, 256), F32),
            pltpu.VMEM((16, 2, 4, 32, WIDE), BF16),
            pltpu.VMEM((4, 32, WIDE), BF16),
            pltpu.VMEM((2, HEADS, HEAD_DIM, 384), BF16),
            pltpu.VMEM((2048, 128), BF16),
            pltpu.VMEM((2048, 128), F32),
            pltpu.VMEM((2048, 128), F32),
            pltpu.VMEM((512, 128), BF16),
            pltpu.VMEM((512, WIDE), BF16),
            pltpu.VMEM((512, WIDE), F32),
            pltpu.VMEM((512, 1024), F32),
            pltpu.VMEM((1024, 128), F32),
            pltpu.VMEM((512, 1024), BF16),
            pltpu.VMEM((LAYERS, 16, 16, 128), BF16),
            pltpu.VMEM((LAYERS, 16, 16, 128), BF16),
            pltpu.VMEM((16, 32, 128), BF16),
            pltpu.VMEM((16, 32, 128), BF16),
            pltpu.VMEM((2048, 128), BF16),
            pltpu.SemaphoreType.DMA((SLOTS,)),
            pltpu.SemaphoreType.DMA((SLOTS,)),
            pltpu.SemaphoreType.DMA((SLOTS,)),
            pltpu.SemaphoreType.DMA((9,)),
        ],
        compiler_params=pltpu.CompilerParams(
            collective_id=0, has_side_effects=True, vmem_limit_bytes=60 * 1024 * 1024
        ),
        name="whole",
    )(
        pair.reshape(2048, 128),
        mask.reshape(1, 1024),
        w_tri_in,
        w_tri_out,
        w_bias.T,
        single.reshape(512, 768),
        w_attn.transpose(1, 2, 0).reshape(4 * HEAD_DIM, 768),
        w_out,
    )
    return (
        new_pair.reshape(32, 64, 128),
        biases.reshape(LAYERS, 1, 32, 1024),
        attended.reshape(1, 32, 768),
    )


def solution(mesh):
    fine = Mesh(mesh.devices.reshape(4, 4, 2, 4, 4), ("z_hi", "x", "core", "y", "z_lo"))
    placed = (
        P(ROW, COL, None),
        P(),
        P(),
        P(),
        P(),
        P(None, ROW, None),
        P(None, COL, None),
        P(COL, None),
    )
    return jax.shard_map(
        per_device,
        mesh=fine,
        in_specs=placed,
        out_specs=(P(ROW, COL, None), P(None, COL, ROW, None), P(COL, ROW, None)),
        check_vma=False,
    )
```

```python
import jax
import jax.numpy as jnp
from jax import lax
from jax.experimental import pallas as pl
from jax.experimental.pallas import tpu as pltpu
from jax.sharding import Mesh
from jax.sharding import PartitionSpec as P

HEADS = 16
HEAD_DIM = 48
LAYERS = 4
WIDE = 8 * HEAD_DIM
ROW = ("z_hi", "x", "core")
COL = ("y", "z_lo")
BF16 = jnp.bfloat16
F32 = jnp.float32

LEFT_X, RIGHT_X, SUM_X = 0, 4, 8
SUM_Z = 14
OUT_Z, OUT_Y, OUT_CORE, KV_CORE = 15, 16, 17, 18
BIAS_FIRST, BIAS_REST, HEADS_OUT = 19, 20, 21
LEFT_FAR, KV_Z_NEAR, KV_Z_FAR, KV_X_NEAR, KV_X_FAR = 22, 24, 26, 28, 30
LEFT_UP, LEFT_DOWN, LEFT_QUARTER, RIGHT_QUARTER = 32, 36, 40, 44
SLOTS = 48


def block_of(index):
    return sum((index >= HEAD_DIM * edge).astype(jnp.int32) for edge in range(1, 32))


def layer_norm(value, axis):
    mean = jnp.mean(value, axis=axis, keepdims=True)
    centred = value - mean
    var = jnp.mean(centred * centred, axis=axis, keepdims=True)
    return centred * lax.rsqrt(var + 1e-05)


def each(count, body):
    lax.fori_loop(0, count, lambda step, carry: (body(step), carry)[1], 0)


def wait_bytes(ref, sem):
    pltpu.make_async_copy(ref, ref, sem).wait()


def contract_last(a, b):
    return lax.dot_general(a, b, (((1,), (1,)), ((), ())), preferred_element_type=F32)


def matmul(a, b):
    return jnp.dot(a, b, preferred_element_type=F32)


def whole_kernel(
    pair_h, mask_h, w_tri_in_h, w_tri_out_h, w_bias_h, single_h, w_attn_h, w_out_h,
    new_pair_h, biases, attended,
    pair, mask, w_tri_in, w_tri_out, w_bias, single, w_attn, w_out,
    left_in, right_in, left_x, right_x, left_z, right_z, sums, sums_x, tri,
    gather_in, own_in,
    left_all, totals, keyval, keyval_in, w_out_all,
    normed, gate, rows_f, w_in_t, query, agate, score, bias_f, probs,
    bias_in, bias_all, heads_in, heads_all, new_pair,
    send, recv, local, load,
):
    z_hi, z_lo = lax.axis_index("z_hi"), lax.axis_index("z_lo")
    x, core, y = lax.axis_index("x"), lax.axis_index("core"), lax.axis_index("y")
    z, xc, head = z_hi * 4 + z_lo, x * 2 + core, y * 4 + z_lo

    def z_place(peer):
        return {"z_hi": lax.div(peer, 4), "z_lo": lax.rem(peer, 4)}

    def xc_place(peer):
        return {"x": lax.div(peer, 2), "core": lax.rem(peer, 2)}

    def col_place(peer):
        return {"y": lax.div(peer, 4), "z_lo": lax.rem(peer, 4)}

    def after(place, step, size):
        return lax.rem(place + 1 + step, size)

    def near(axis, place, step, size):
        return {axis: after(place, step, size)}

    loads = [
        pltpu.make_async_copy(src, dst, load.at[slot])
        for slot, (src, dst) in enumerate(
            (
                (pair_h, pair), (w_tri_in_h, w_tri_in), (mask_h, mask), (w_out_h, w_out),
                (w_attn_h, w_attn), (single_h, single), (w_tri_out_h, w_tri_out), (w_bias_h, w_bias),
            )
        )
    ]
    for copy in loads:
        copy.start()
    barrier = pltpu.get_barrier_semaphore()

    def greet(peer):
        pl.semaphore_signal(barrier, inc=1, device_id=peer, device_id_type=pl.DeviceIdType.MESH)

    each(15, lambda step: greet(z_place(after(z, step, 16))))
    each(7, lambda step: greet(xc_place(after(xc, step, 8))))
    each(15, lambda step: greet(col_place(after(head, step, 16))))

    def push(src, dst, slot, peer):
        pltpu.make_async_remote_copy(
            src_ref=src, dst_ref=dst, send_sem=send.at[slot], recv_sem=recv.at[slot],
            device_id=peer, device_id_type=pl.DeviceIdType.MESH,
        ).start()

    def keep(src, dst, slot):
        pltpu.make_async_copy(src, dst, local.at[slot]).start()

    def quarter(step):
        return after(z_hi, step, 4)

    def over_x(src, dst, slot, step, first):
        part = pl.ds(first * 4, 4)

        def body(other):
            peer = after(xc, other, 8)
            push(src.at[part, peer], dst.at[part, xc], slot + step, xc_place(peer))

        each(7, body)
        keep(src.at[part, xc], dst.at[part, xc], slot + step)

    def end_x(dst, slot, step):
        wait_bytes(dst.at[0, pl.ds(0, 4)], local.at[slot + step])
        wait_bytes(dst.at[pl.ds(0, 4), pl.ds(0, 7)], recv.at[slot + step])

    def over_z(src, dst, slot, step):
        def body(low):
            peer = quarter(step) * 4 + low

            @pl.when(peer != z)
            def _():
                push(src.at[peer], dst.at[z], slot, z_place(peer))

            @pl.when(peer == z)
            def _():
                keep(src.at[z], dst.at[z], slot)

        each(4, body)

    def end_z(dst, slot):
        wait_bytes(dst.at[pl.ds(0, 1)], local.at[slot])
        wait_bytes(dst.at[pl.ds(0, 15)], recv.at[slot])

    for copy in loads[:3]:
        copy.wait()
    mask_f = mask[...].astype(F32)
    lane = lax.broadcasted_iota(jnp.int32, (1024, 128), 1)
    token = lax.broadcasted_iota(jnp.int32, (1024, 128), 0)
    low_lane = jnp.where(lane < 64, lane, lane - 64)
    chosen = (token == head * 64 + low_lane).astype(F32).astype(BF16)
    col_mask = matmul(jnp.broadcast_to(mask_f, (16, 1024)).astype(BF16), chosen)
    token = lax.broadcasted_iota(jnp.int32, (16, 1024), 1)
    line = lax.broadcasted_iota(jnp.int32, (16, 1024), 0) * 2 + (z_hi * 8 + xc) * 32
    even = jnp.sum(jnp.where(token == line, mask_f, 0.0), axis=1, keepdims=True)
    odd = jnp.sum(jnp.where(token == line + 1, mask_f, 0.0), axis=1, keepdims=True)
    low = lax.broadcasted_iota(jnp.int32, (16, 128), 1) < 64
    cell_mask = jnp.where(low, even, odd) * col_mask

    w_in_t[...] = w_tri_in[:, 0:512].T

    def factor(block, first):
        rows = slice(block * 256, block * 256 + 256)
        both = contract_last(w_in_t[first : first + 256, :], normed[rows, :])
        value = jax.nn.sigmoid(both[128:]) * both[:128]
        for half in range(2):
            line = block * 2 + half
            part = value[:, half * 128 : half * 128 + 128] * cell_mask[line : line + 1]
            rows_f[pl.ds(line, 128, stride=16), :] = part

    for block in range(8):
        rows = slice(block * 256, block * 256 + 256)
        normed[rows, :] = layer_norm(pair[rows, :].astype(F32), 1).astype(BF16)
        factor(block, 0)
    left_in[...] = rows_f[...].astype(BF16).reshape(16, 8, 16, 128)
    pl.semaphore_wait(barrier, 37)
    for step in range(4):
        over_z(left_in, left_z, LEFT_QUARTER + step, step)
    for block in range(8):
        factor(block, 256)
    right_in[...] = rows_f[...].astype(BF16).reshape(16, 8, 16, 128)
    for step in range(4):
        over_x(right_in, right_x, RIGHT_X, step, quarter(step))
    loads[3].wait()
    half_out = w_out.at[:, pl.ds(pl.multiple_of(core * 384, 128), 384)]
    each(3, lambda step: push(half_out, w_out_all.at[core, head], OUT_Z, near("z_lo", z_lo, step, 4)))
    keep(half_out, w_out_all.at[core, head], OUT_Z)

    for copy in loads[4:]:
        copy.wait()
    lane = lax.broadcasted_iota(jnp.int32, (1, 4 * WIDE), 1)
    block = block_of(lane)
    source = lane - HEAD_DIM * block + HEAD_DIM * sum((block >= 8 * n).astype(jnp.int32) for n in (1, 2, 3))
    place = lax.broadcasted_iota(jnp.int32, (4 * HEAD_DIM, 4 * WIDE), 0)
    spread = (place == source).astype(F32).astype(BF16)
    place = lax.broadcasted_iota(jnp.int32, (256, WIDE), 0)
    own_block = ((place >= 32 * block[:, :WIDE]) & (place < 32 * block[:, :WIDE] + 32)).astype(F32)
    lane = lax.broadcasted_iota(jnp.int32, (WIDE, 128), 1)
    place = lax.broadcasted_iota(jnp.int32, (WIDE, 128), 0)
    gather = (place - HEAD_DIM * block_of(place) == lane).astype(F32).astype(BF16)
    own_in[...] = own_block
    gather_in[...] = gather
    w_wide = matmul(w_attn[...].T, spread).astype(BF16)
    for group in range(2):
        rows = slice(group * 256, group * 256 + 256)
        xn = layer_norm(single[rows, :].astype(F32), 1).astype(BF16)
        wide = matmul(xn, w_wide)
        query[rows, :] = (wide[:, 0:WIDE] * own_in[...]).astype(BF16)
        for which in range(2):
            part = wide[:, WIDE * (which + 1) : WIDE * (which + 2)] * own_in[...]
            packed = jnp.sum(part.reshape(8, 32, WIDE), axis=0)
            keyval_in[which * 2 + group] = packed.astype(BF16)
        agate[rows, :] = jax.nn.sigmoid(wide[:, 3 * WIDE :])

    def sent_z(slot, step):
        wait_bytes(left_z.at[pl.ds(0, 3 if step == 3 else 4)], send.at[slot + step])

    for step in range(4):
        end_x(right_x, RIGHT_X, step)
        sent_z(LEFT_QUARTER, step)
        over_z(right_x, right_z, RIGHT_QUARTER + step, step)
    mine = keyval.at[z_hi * 4 + x, core]
    z_up, z_down, x_up, x_down = after(z_hi, 0, 4), after(z_hi, 2, 4), after(x, 0, 4), after(x, 2, 4)
    push(keyval_in, mine, KV_Z_NEAR, {"z_hi": z_up})
    push(keyval_in, mine, KV_Z_NEAR + 1, {"z_hi": z_down})
    keep(keyval_in, mine, KV_Z_NEAR)
    wait_bytes(w_out_all.at[0, pl.ds(0, 1)], local.at[OUT_Z])
    wait_bytes(w_out_all.at[0, pl.ds(0, 3)], recv.at[OUT_Z])
    quad = w_out_all.at[core, pl.ds(y * 4, 4)]
    each(3, lambda step: push(quad, quad, OUT_Y, near("y", y, step, 4)))
    for block in range(8):
        rows = slice(block * 256, block * 256 + 256)
        gate[rows, :] = jax.nn.sigmoid(matmul(normed[rows, :], w_tri_in[:, 512:640]))

    def tiles(blocks, z_part, part):
        pieces = [blocks[z_part * 4 + low, :, :, part * 64 : part * 64 + 64] for low in range(4)]
        return jnp.concatenate(pieces, axis=-1).reshape(128, 256)

    up, down = after(y, 0, 4), after(y, 2, 4)

    def origin(step):
        return lax.rem(z_hi + 3 - step, 4)

    def end_quarter(slot, step):
        if step == 3:
            wait_bytes(left_z.at[pl.ds(0, 1)], local.at[slot + step])
        wait_bytes(left_z.at[pl.ds(0, 3 if step == 3 else 4)], recv.at[slot + step])

    for step in range(4):
        end_quarter(LEFT_QUARTER, step)
        over_x(left_z, left_x, LEFT_X, step, origin(step))
    for step in range(4):
        end_x(left_x, LEFT_X, step)
        source = origin(step)
        for part in range(2):
            left_all[y, source, :, part * 128 : part * 128 + 128] = tiles(left_x, source, part).T
        own = left_all.at[y, source]
        push(own, own, LEFT_UP + step, {"y": up})
        push(own, own, LEFT_DOWN + step, {"y": down})
    for step in range(4):
        source = origin(step)
        wait_bytes(left_all.at[y, 0], recv.at[LEFT_UP + step])
        passed = left_all.at[down, source, pl.ds(0, 128)]
        push(passed, passed, LEFT_FAR, {"y": up})
        wait_bytes(left_all.at[y, 0], recv.at[LEFT_DOWN + step])
        passed = left_all.at[up, source, pl.ds(128, 128)]
        push(passed, passed, LEFT_FAR + 1, {"y": down})
    def over_x_ring(part):
        block = keyval.at[part * 4 + x, core]
        push(block, block, KV_X_NEAR, {"x": x_up})
        push(block, block, KV_X_NEAR + 1, {"x": x_down})

    for way in range(2):
        wait_bytes(left_all.at[0, pl.ds(0, 2)], recv.at[LEFT_FAR + way])
    for step in range(4):
        if step == 3:
            wait_bytes(keyval_in, local.at[KV_Z_NEAR])
            wait_bytes(keyval_in, recv.at[KV_Z_NEAR])
            wait_bytes(keyval_in, recv.at[KV_Z_NEAR + 1])
            each(3, lambda step: over_x_ring(lax.rem(z_hi + 3 + step, 4)))
        end_quarter(RIGHT_QUARTER, step)
        if step == 3:
            passed = keyval.at[z_down * 4 + x, core, pl.ds(0, 2)]
            push(passed, passed, KV_Z_FAR, {"z_hi": z_up})
            passed = keyval.at[z_up * 4 + x, core, pl.ds(2, 2)]
            push(passed, passed, KV_Z_FAR + 1, {"z_hi": z_down})
        source = origin(step)
        block = jnp.concatenate([tiles(right_z, source, part) for part in range(2)], axis=0)
        for turn in range(4):
            part = quarter(turn)
            product = matmul(left_all[part, source], block)
            if step > 0:
                product += totals[turn]
            if step < 3:
                totals[turn] = product
                continue
            product = product.astype(BF16).reshape(8, 2, 16, 256)
            for low in range(4):
                cut = slice(low * 64, low * 64 + 64)
                sums[part * 4 + low] = jnp.concatenate(
                    [product[:, 0, :, cut], product[:, 1, :, cut]], axis=-1
                )
            over_x(sums, sums_x, SUM_X, turn, part)
    for step in range(4):
        end_x(sums_x, SUM_X, step)
        over_z(sums_x, tri, SUM_Z, step)
    wait_bytes(w_out_all.at[0, pl.ds(0, 12)], recv.at[OUT_Y])
    push(w_out_all.at[core], w_out_all.at[core], OUT_CORE, {"core": 1 - core})
    wait_bytes(keyval_in.at[pl.ds(0, 2)], recv.at[KV_Z_FAR])
    wait_bytes(keyval_in.at[pl.ds(0, 2)], recv.at[KV_Z_FAR + 1])
    over_x_ring(lax.rem(z_hi + 2, 4))

    def pass_x(first, src, slot, place):
        def body(part):
            passed = keyval.at[part * 4 + src, core, pl.ds(first, 2)]
            push(passed, passed, slot, place)

        wait_bytes(keyval.at[pl.ds(0, 4), 0], recv.at[slot - 2])
        each(4, body)

    pass_x(0, x_down, KV_X_FAR, {"x": x_up})
    pass_x(2, x_up, KV_X_FAR + 1, {"x": x_down})
    wait_bytes(keyval.at[pl.ds(0, 2), 0], recv.at[KV_X_FAR])
    wait_bytes(keyval.at[pl.ds(0, 2), 0], recv.at[KV_X_FAR + 1])
    push(keyval.at[:, core], keyval.at[:, core], KV_CORE, {"core": 1 - core})

    end_z(tri, SUM_Z)
    rows_f[...] = tri[...].reshape(2048, 128).astype(F32)
    for block in range(8):
        lines = (block * 2, block * 2 + 16, block * 2 + 1, block * 2 + 17)
        value = jnp.concatenate(
            [rows_f[pl.ds(block * 2 + half, 128, stride=16), :] for half in range(2)], axis=1
        )
        tnorm = layer_norm(value, 0).T.astype(BF16)
        update = matmul(tnorm, w_tri_out[...])
        updated = []
        for place, line in enumerate(lines):
            cells = slice(line * 64, line * 64 + 64)
            change = gate[cells, :] * update[place * 64 : place * 64 + 64]
            updated.append((pair[cells, :].astype(F32) + change).astype(BF16))
            new_pair[cells, :] = updated[-1]
        pnorm = layer_norm(jnp.concatenate(updated, axis=0).astype(F32), 1).astype(BF16)
        bias = contract_last(w_bias[...], pnorm)
        for half in range(2):
            rows = pl.ds(block * 2 + half, 64, stride=16)
            bias_f[rows, :] = bias[:, half * 128 : half * 128 + 128]

    def send_bias(layers, slot):
        def body(step):
            peer = after(head, step, 16)
            push(bias_in.at[layers, peer], bias_all.at[layers, head], slot, col_place(peer))

        each(15, body)
        keep(bias_in.at[layers, head], bias_all.at[layers, head], slot)

    bias_in[0] = bias_f[0:256, :].astype(BF16).reshape(16, 16, 128)
    send_bias(pl.ds(0, 1), BIAS_FIRST)
    bias_in[1:4] = bias_f[256:1024, :].astype(BF16).reshape(3, 16, 16, 128)
    send_bias(pl.ds(1, 3), BIAS_REST)
    store = pltpu.make_async_copy(new_pair, new_pair_h, load.at[8])
    store.start()
    wait_bytes(keyval.at[:, 0], recv.at[KV_CORE])
    for group in range(2):
        rows = slice(group * 256, group * 256 + 256)
        keys = keyval[:, :, group].reshape(1024, WIDE)
        score[rows, :] = contract_last(query[rows, :], keys)

    def bias_rows(layer):
        return jnp.concatenate(
            [
                jnp.concatenate(
                    [bias_all[layer, src, :, part * 64 : part * 64 + 64] for src in range(16)],
                    axis=-1,
                )
                for part in range(2)
            ],
            axis=0,
        )

    wait_bytes(bias_all.at[0, pl.ds(0, 1)], local.at[BIAS_FIRST])
    wait_bytes(bias_all.at[0, pl.ds(0, 15)], recv.at[BIAS_FIRST])
    first_bias = bias_rows(0)
    biases[0] = first_bias
    first_bias = first_bias.astype(F32)
    present = mask_f > 0.0
    for sample in range(16):
        rows = slice(sample * 32, sample * 32 + 32)
        logits = score[rows, :] * HEAD_DIM ** (-0.5) + first_bias
        logits = jnp.where(present, logits, -1000000000.0)
        expo = jnp.exp(logits - jnp.max(logits, axis=1, keepdims=True))
        probs[rows, :] = (expo * (1.0 / jnp.sum(expo, axis=1, keepdims=True))).astype(BF16)
    for group in range(2):
        rows = slice(group * 256, group * 256 + 256)
        values = keyval[:, :, 2 + group].reshape(1024, WIDE)
        context = matmul(probs[rows, :], values)
        gated = (agate[rows, :] * context * own_in[...]).astype(BF16)
        gathered = matmul(gated, gather_in[...]).astype(BF16)
        heads_in[group * 8 : group * 8 + 8] = gathered.reshape(8, 32, 128)

    def send_heads(step):
        peer = after(head, step, 16)
        push(heads_in.at[peer], heads_all.at[head], HEADS_OUT, col_place(peer))

    each(15, send_heads)
    keep(heads_in.at[head], heads_all.at[head], HEADS_OUT)
    wait_bytes(bias_all.at[pl.ds(0, 3), 0], local.at[BIAS_REST])
    wait_bytes(bias_all.at[pl.ds(0, 3), pl.ds(0, 15)], recv.at[BIAS_REST])
    for layer in range(1, 4):
        biases[layer] = bias_rows(layer)
    wait_bytes(w_out_all.at[0], recv.at[OUT_CORE])
    wait_bytes(heads_all.at[pl.ds(0, 1)], local.at[HEADS_OUT])
    wait_bytes(heads_all.at[pl.ds(0, 15)], recv.at[HEADS_OUT])
    merged = jnp.concatenate([heads_all[src, :, 0:HEAD_DIM] for src in range(16)], axis=-1)
    for half in range(2):
        weights = w_out_all[half].reshape(HEADS * HEAD_DIM, 384)
        attended[:, half * 384 : half * 384 + 384] = matmul(merged, weights).astype(BF16)

    store.wait()
    for slot in (LEFT_X, RIGHT_X, SUM_X):
        for step in range(4):
            wait_bytes(left_x.at[pl.ds(0, 4), pl.ds(0, 7)], send.at[slot + step])
    for step in range(4):
        sent_z(RIGHT_QUARTER, step)
    wait_bytes(left_z.at[pl.ds(0, 15)], send.at[SUM_Z])
    for way in range(2):
        for step in range(4):
            wait_bytes(left_all.at[0, 0], send.at[(LEFT_UP, LEFT_DOWN)[way] + step])
        wait_bytes(left_all.at[0, pl.ds(0, 2)], send.at[LEFT_FAR + way])
        wait_bytes(keyval_in, send.at[KV_Z_NEAR + way])
        wait_bytes(keyval_in.at[pl.ds(0, 2)], send.at[KV_Z_FAR + way])
        wait_bytes(keyval.at[pl.ds(0, 4), 0], send.at[KV_X_NEAR + way])
        wait_bytes(keyval.at[pl.ds(0, 2), 0], send.at[KV_X_FAR + way])
    wait_bytes(w_out_all.at[0, pl.ds(0, 3)], send.at[OUT_Z])
    wait_bytes(w_out_all.at[0, pl.ds(0, 12)], send.at[OUT_Y])
    wait_bytes(w_out_all.at[0], send.at[OUT_CORE])
    wait_bytes(keyval.at[:, 0], send.at[KV_CORE])
    wait_bytes(bias_all.at[0, pl.ds(0, 15)], send.at[BIAS_FIRST])
    wait_bytes(bias_all.at[pl.ds(0, 3), pl.ds(0, 15)], send.at[BIAS_REST])
    wait_bytes(heads_all.at[pl.ds(0, 15)], send.at[HEADS_OUT])


def per_device(pair, mask, w_tri_in, w_tri_out, w_bias, single, w_attn, w_out):
    vmem = pl.BlockSpec(memory_space=pltpu.VMEM)
    blocks = pltpu.VMEM((16, 8, 16, 128), BF16)
    new_pair, biases, attended = pl.pallas_call(
        whole_kernel,
        out_shape=(
            jax.ShapeDtypeStruct((2048, 128), BF16),
            jax.ShapeDtypeStruct((LAYERS, 32, 1024), BF16),
            jax.ShapeDtypeStruct((32, 768), BF16),
        ),
        in_specs=[pl.BlockSpec(memory_space=pltpu.HBM)] * 8,
        out_specs=(pl.BlockSpec(memory_space=pltpu.HBM), vmem, vmem),
        scratch_shapes=[
            pltpu.VMEM((2048, 128), BF16),
            pltpu.VMEM((1, 1024), jnp.int32),
            pltpu.VMEM((128, 640), BF16),
            pltpu.VMEM((128, 128), BF16),
            pltpu.VMEM((64, 128), BF16),
            pltpu.VMEM((512, 768), BF16),
            pltpu.VMEM((4 * HEAD_DIM, 768), BF16),
            pltpu.VMEM((HEAD_DIM, 768), BF16),
        ]
        + [blocks] * 9
        + [
            pltpu.VMEM((WIDE, 128), BF16),
            pltpu.VMEM((256, WIDE), F32),
            pltpu.VMEM((4, 4, 256, 256), BF16),
            pltpu.VMEM((4, 256, 256), F32),
            pltpu.VMEM((16, 2, 4, 32, WIDE), BF16),
            pltpu.VMEM((4, 32, WIDE), BF16),
            pltpu.VMEM((2, HEADS, HEAD_DIM, 384), BF16),
            pltpu.VMEM((2048, 128), BF16),
            pltpu.VMEM((2048, 128), F32),
            pltpu.VMEM((2048, 128), F32),
            pltpu.VMEM((512, 128), BF16),
            pltpu.VMEM((512, WIDE), BF16),
            pltpu.VMEM((512, WIDE), F32),
            pltpu.VMEM((512, 1024), F32),
            pltpu.VMEM((1024, 128), F32),
            pltpu.VMEM((512, 1024), BF16),
            pltpu.VMEM((LAYERS, 16, 16, 128), BF16),
            pltpu.VMEM((LAYERS, 16, 16, 128), BF16),
            pltpu.VMEM((16, 32, 128), BF16),
            pltpu.VMEM((16, 32, 128), BF16),
            pltpu.VMEM((2048, 128), BF16),
            pltpu.SemaphoreType.DMA((SLOTS,)),
            pltpu.SemaphoreType.DMA((SLOTS,)),
            pltpu.SemaphoreType.DMA((SLOTS,)),
            pltpu.SemaphoreType.DMA((9,)),
        ],
        compiler_params=pltpu.CompilerParams(
            collective_id=0, has_side_effects=True, vmem_limit_bytes=60 * 1024 * 1024
        ),
        name="whole",
    )(
        pair.reshape(2048, 128),
        mask.reshape(1, 1024),
        w_tri_in,
        w_tri_out,
        w_bias.T,
        single.reshape(512, 768),
        w_attn.transpose(1, 2, 0).reshape(4 * HEAD_DIM, 768),
        w_out,
    )
    return (
        new_pair.reshape(32, 64, 128),
        biases.reshape(LAYERS, 1, 32, 1024),
        attended.reshape(1, 32, 768),
    )


def solution(mesh):
    fine = Mesh(mesh.devices.reshape(4, 4, 2, 4, 4), ("z_hi", "x", "core", "y", "z_lo"))
    placed = (
        P(ROW, COL, None),
        P(),
        P(),
        P(),
        P(),
        P(None, ROW, None),
        P(None, COL, None),
        P(COL, None),
    )
    return jax.shard_map(
        per_device,
        mesh=fine,
        in_specs=placed,
        out_specs=(P(ROW, COL, None), P(None, COL, ROW, None), P(COL, ROW, None)),
        check_vma=False,
    )
```

```python
import jax
import jax.numpy as jnp
from jax import lax
from jax.experimental import pallas as pl
from jax.experimental.pallas import tpu as pltpu
from jax.sharding import Mesh
from jax.sharding import PartitionSpec as P

HEADS = 16
HEAD_DIM = 48
LAYERS = 4
WIDE = 8 * HEAD_DIM
ROW = ("z_hi", "x", "core")
COL = ("y", "z_lo")
BF16 = jnp.bfloat16
F32 = jnp.float32

LEFT_X, RIGHT_X, SUM_X = 0, 4, 8
SUM_Z = 14
OUT_Z, OUT_Y, OUT_CORE, KV_CORE = 15, 16, 17, 18
BIAS_FIRST, BIAS_REST, HEADS_OUT = 19, 20, 21
LEFT_FAR, KV_Z_NEAR, KV_Z_FAR, KV_X_NEAR, KV_X_FAR = 22, 24, 26, 28, 30
LEFT_UP, LEFT_DOWN, LEFT_QUARTER, RIGHT_QUARTER = 32, 36, 40, 44
SLOTS = 48


def block_of(index):
    return sum((index >= HEAD_DIM * edge).astype(jnp.int32) for edge in range(1, 32))


def layer_norm(value, axis):
    mean = jnp.mean(value, axis=axis, keepdims=True)
    centred = value - mean
    var = jnp.mean(centred * centred, axis=axis, keepdims=True)
    return centred * lax.rsqrt(var + 1e-05)


def each(count, body):
    lax.fori_loop(0, count, lambda step, carry: (body(step), carry)[1], 0)


def wait_bytes(ref, sem):
    pltpu.make_async_copy(ref, ref, sem).wait()


def contract_last(a, b):
    return lax.dot_general(a, b, (((1,), (1,)), ((), ())), preferred_element_type=F32)


def matmul(a, b):
    return jnp.dot(a, b, preferred_element_type=F32)


def whole_kernel(
    pair_h, mask_h, w_tri_in_h, w_tri_out_h, w_bias_h, single_h, w_attn_h, w_out_h,
    new_pair_h, biases, attended,
    pair, mask, w_tri_in, w_tri_out, w_bias, single, w_attn, w_out,
    left_in, right_in, left_x, right_x, left_z, right_z, sums, sums_x, tri,
    gather_in, own_in,
    left_all, right_own, keyval, keyval_in, w_out_all,
    normed, gate, rows_f, w_in_t, query, agate, score, bias_f, probs,
    bias_in, bias_all, heads_in, heads_all, new_pair,
    send, recv, local, load,
):
    z_hi, z_lo = lax.axis_index("z_hi"), lax.axis_index("z_lo")
    x, core, y = lax.axis_index("x"), lax.axis_index("core"), lax.axis_index("y")
    z, xc, head = z_hi * 4 + z_lo, x * 2 + core, y * 4 + z_lo

    def z_place(peer):
        return {"z_hi": lax.div(peer, 4), "z_lo": lax.rem(peer, 4)}

    def xc_place(peer):
        return {"x": lax.div(peer, 2), "core": lax.rem(peer, 2)}

    def col_place(peer):
        return {"y": lax.div(peer, 4), "z_lo": lax.rem(peer, 4)}

    def after(place, step, size):
        return lax.rem(place + 1 + step, size)

    def near(axis, place, step, size):
        return {axis: after(place, step, size)}

    loads = [
        pltpu.make_async_copy(src, dst, load.at[slot])
        for slot, (src, dst) in enumerate(
            (
                (pair_h, pair), (w_tri_in_h, w_tri_in), (mask_h, mask), (w_out_h, w_out),
                (w_attn_h, w_attn), (single_h, single), (w_tri_out_h, w_tri_out), (w_bias_h, w_bias),
            )
        )
    ]
    for copy in loads:
        copy.start()
    barrier = pltpu.get_barrier_semaphore()

    def greet(peer):
        pl.semaphore_signal(barrier, inc=1, device_id=peer, device_id_type=pl.DeviceIdType.MESH)

    each(15, lambda step: greet(z_place(after(z, step, 16))))
    each(7, lambda step: greet(xc_place(after(xc, step, 8))))
    each(15, lambda step: greet(col_place(after(head, step, 16))))

    def push(src, dst, slot, peer):
        pltpu.make_async_remote_copy(
            src_ref=src, dst_ref=dst, send_sem=send.at[slot], recv_sem=recv.at[slot],
            device_id=peer, device_id_type=pl.DeviceIdType.MESH,
        ).start()

    def keep(src, dst, slot):
        pltpu.make_async_copy(src, dst, local.at[slot]).start()

    def quarter(step):
        return after(z_hi, step, 4)

    def over_x(src, dst, slot, step, first):
        part = pl.ds(first * 4, 4)

        def body(other):
            peer = after(xc, other, 8)
            push(src.at[part, peer], dst.at[part, xc], slot + step, xc_place(peer))

        each(7, body)
        keep(src.at[part, xc], dst.at[part, xc], slot + step)

    def end_x(dst, slot, step):
        wait_bytes(dst.at[0, pl.ds(0, 4)], local.at[slot + step])
        wait_bytes(dst.at[pl.ds(0, 4), pl.ds(0, 7)], recv.at[slot + step])

    def over_z(src, dst, slot, step):
        def body(low):
            peer = quarter(step) * 4 + low

            @pl.when(peer != z)
            def _():
                push(src.at[peer], dst.at[z], slot, z_place(peer))

            @pl.when(peer == z)
            def _():
                keep(src.at[z], dst.at[z], slot)

        each(4, body)

    def end_z(dst, slot):
        wait_bytes(dst.at[pl.ds(0, 1)], local.at[slot])
        wait_bytes(dst.at[pl.ds(0, 15)], recv.at[slot])

    for copy in loads[:3]:
        copy.wait()
    mask_f = mask[...].astype(F32)
    lane = lax.broadcasted_iota(jnp.int32, (1024, 128), 1)
    token = lax.broadcasted_iota(jnp.int32, (1024, 128), 0)
    low_lane = jnp.where(lane < 64, lane, lane - 64)
    chosen = (token == head * 64 + low_lane).astype(F32).astype(BF16)
    col_mask = matmul(jnp.broadcast_to(mask_f, (16, 1024)).astype(BF16), chosen)
    token = lax.broadcasted_iota(jnp.int32, (16, 1024), 1)
    line = lax.broadcasted_iota(jnp.int32, (16, 1024), 0) * 2 + (z_hi * 8 + xc) * 32
    even = jnp.sum(jnp.where(token == line, mask_f, 0.0), axis=1, keepdims=True)
    odd = jnp.sum(jnp.where(token == line + 1, mask_f, 0.0), axis=1, keepdims=True)
    low = lax.broadcasted_iota(jnp.int32, (16, 128), 1) < 64
    cell_mask = jnp.where(low, even, odd) * col_mask

    w_in_t[...] = w_tri_in[:, 0:512].T

    def factor(block, first):
        rows = slice(block * 256, block * 256 + 256)
        both = contract_last(w_in_t[first : first + 256, :], normed[rows, :])
        value = jax.nn.sigmoid(both[128:]) * both[:128]
        for half in range(2):
            line = block * 2 + half
            part = value[:, half * 128 : half * 128 + 128] * cell_mask[line : line + 1]
            rows_f[pl.ds(line, 128, stride=16), :] = part

    for block in range(8):
        rows = slice(block * 256, block * 256 + 256)
        normed[rows, :] = layer_norm(pair[rows, :].astype(F32), 1).astype(BF16)
        factor(block, 0)
    left_in[...] = rows_f[...].astype(BF16).reshape(16, 8, 16, 128)
    pl.semaphore_wait(barrier, 37)
    for step in range(4):
        over_z(left_in, left_z, LEFT_QUARTER + step, step)
    for block in range(8):
        factor(block, 256)
    right_in[...] = rows_f[...].astype(BF16).reshape(16, 8, 16, 128)
    for step in range(4):
        over_x(right_in, right_x, RIGHT_X, step, quarter(step))
    loads[3].wait()
    half_out = w_out.at[:, pl.ds(pl.multiple_of(core * 384, 128), 384)]
    each(3, lambda step: push(half_out, w_out_all.at[core, head], OUT_Z, near("z_lo", z_lo, step, 4)))
    keep(half_out, w_out_all.at[core, head], OUT_Z)

    for copy in loads[4:]:
        copy.wait()
    lane = lax.broadcasted_iota(jnp.int32, (1, 4 * WIDE), 1)
    block = block_of(lane)
    source = lane - HEAD_DIM * block + HEAD_DIM * sum((block >= 8 * n).astype(jnp.int32) for n in (1, 2, 3))
    place = lax.broadcasted_iota(jnp.int32, (4 * HEAD_DIM, 4 * WIDE), 0)
    spread = (place == source).astype(F32).astype(BF16)
    place = lax.broadcasted_iota(jnp.int32, (256, WIDE), 0)
    own_block = ((place >= 32 * block[:, :WIDE]) & (place < 32 * block[:, :WIDE] + 32)).astype(F32)
    lane = lax.broadcasted_iota(jnp.int32, (WIDE, 128), 1)
    place = lax.broadcasted_iota(jnp.int32, (WIDE, 128), 0)
    gather = (place - HEAD_DIM * block_of(place) == lane).astype(F32).astype(BF16)
    own_in[...] = own_block
    gather_in[...] = gather
    w_wide = matmul(w_attn[...].T, spread).astype(BF16)
    for group in range(2):
        rows = slice(group * 256, group * 256 + 256)
        xn = layer_norm(single[rows, :].astype(F32), 1).astype(BF16)
        wide = matmul(xn, w_wide)
        query[rows, :] = (wide[:, 0:WIDE] * own_in[...]).astype(BF16)
        for which in range(2):
            part = wide[:, WIDE * (which + 1) : WIDE * (which + 2)] * own_in[...]
            packed = jnp.sum(part.reshape(8, 32, WIDE), axis=0)
            keyval_in[which * 2 + group] = packed.astype(BF16)
        agate[rows, :] = jax.nn.sigmoid(wide[:, 3 * WIDE :])

    def sent_z(slot, step):
        wait_bytes(left_z.at[pl.ds(0, 3 if step == 3 else 4)], send.at[slot + step])

    for step in range(4):
        end_x(right_x, RIGHT_X, step)
        sent_z(LEFT_QUARTER, step)
        over_z(right_x, right_z, RIGHT_QUARTER + step, step)
    mine = keyval.at[z_hi * 4 + x, core]
    z_up, z_down, x_up, x_down = after(z_hi, 0, 4), after(z_hi, 2, 4), after(x, 0, 4), after(x, 2, 4)
    push(keyval_in, mine, KV_Z_NEAR, {"z_hi": z_up})
    push(keyval_in, mine, KV_Z_NEAR + 1, {"z_hi": z_down})
    keep(keyval_in, mine, KV_Z_NEAR)
    wait_bytes(w_out_all.at[0, pl.ds(0, 1)], local.at[OUT_Z])
    wait_bytes(w_out_all.at[0, pl.ds(0, 3)], recv.at[OUT_Z])
    quad = w_out_all.at[core, pl.ds(y * 4, 4)]
    each(3, lambda step: push(quad, quad, OUT_Y, near("y", y, step, 4)))
    for block in range(8):
        rows = slice(block * 256, block * 256 + 256)
        gate[rows, :] = jax.nn.sigmoid(matmul(normed[rows, :], w_tri_in[:, 512:640]))

    def tiles(blocks, z_part, part):
        pieces = [blocks[z_part * 4 + low, :, :, part * 64 : part * 64 + 64] for low in range(4)]
        return jnp.concatenate(pieces, axis=-1).reshape(128, 256)

    up, down = after(y, 0, 4), after(y, 2, 4)

    def origin(step):
        return lax.rem(z_hi + 3 - step, 4)

    def end_quarter(slot, step):
        if step == 3:
            wait_bytes(left_z.at[pl.ds(0, 1)], local.at[slot + step])
        wait_bytes(left_z.at[pl.ds(0, 3 if step == 3 else 4)], recv.at[slot + step])

    for step in range(4):
        end_quarter(LEFT_QUARTER, step)
        over_x(left_z, left_x, LEFT_X, step, origin(step))
    for step in range(4):
        end_x(left_x, LEFT_X, step)
        source = origin(step)
        for part in range(2):
            left_all[y, source, :, part * 128 : part * 128 + 128] = tiles(left_x, source, part).T
        own = left_all.at[y, source]
        push(own, own, LEFT_UP + step, {"y": up})
        push(own, own, LEFT_DOWN + step, {"y": down})
    for step in range(4):
        source = origin(step)
        wait_bytes(left_all.at[y, 0], recv.at[LEFT_UP + step])
        passed = left_all.at[down, source, pl.ds(0, 128)]
        push(passed, passed, LEFT_FAR, {"y": up})
        wait_bytes(left_all.at[y, 0], recv.at[LEFT_DOWN + step])
        passed = left_all.at[up, source, pl.ds(128, 128)]
        push(passed, passed, LEFT_FAR + 1, {"y": down})
    def over_x_ring(part):
        block = keyval.at[part * 4 + x, core]
        push(block, block, KV_X_NEAR, {"x": x_up})
        push(block, block, KV_X_NEAR + 1, {"x": x_down})

    wait_bytes(keyval_in, local.at[KV_Z_NEAR])
    wait_bytes(keyval_in, recv.at[KV_Z_NEAR])
    wait_bytes(keyval_in, recv.at[KV_Z_NEAR + 1])
    each(3, lambda step: over_x_ring(lax.rem(z_hi + 3 + step, 4)))
    for step in range(4):
        end_quarter(RIGHT_QUARTER, step)
        if step == 3:
            passed = keyval.at[z_down * 4 + x, core, pl.ds(0, 2)]
            push(passed, passed, KV_Z_FAR, {"z_hi": z_up})
            passed = keyval.at[z_up * 4 + x, core, pl.ds(2, 2)]
            push(passed, passed, KV_Z_FAR + 1, {"z_hi": z_down})
        source = origin(step)
        for part in range(2):
            right_own[source, part * 128 : part * 128 + 128, :] = tiles(right_z, source, part)
    for way in range(2):
        wait_bytes(left_all.at[0, pl.ds(0, 2)], recv.at[LEFT_FAR + way])
    for step in range(4):
        part = quarter(step)
        product = sum(matmul(left_all[part, quad], right_own[quad]) for quad in range(4))
        product = product.astype(BF16).reshape(8, 2, 16, 256)
        for low in range(4):
            cut = slice(low * 64, low * 64 + 64)
            sums[part * 4 + low] = jnp.concatenate(
                [product[:, 0, :, cut], product[:, 1, :, cut]], axis=-1
            )
        over_x(sums, sums_x, SUM_X, step, part)
    for step in range(4):
        end_x(sums_x, SUM_X, step)
        over_z(sums_x, tri, SUM_Z, step)
    wait_bytes(w_out_all.at[0, pl.ds(0, 12)], recv.at[OUT_Y])
    push(w_out_all.at[core], w_out_all.at[core], OUT_CORE, {"core": 1 - core})
    wait_bytes(keyval_in.at[pl.ds(0, 2)], recv.at[KV_Z_FAR])
    wait_bytes(keyval_in.at[pl.ds(0, 2)], recv.at[KV_Z_FAR + 1])
    over_x_ring(lax.rem(z_hi + 2, 4))

    def pass_x(first, src, slot, place):
        def body(part):
            passed = keyval.at[part * 4 + src, core, pl.ds(first, 2)]
            push(passed, passed, slot, place)

        wait_bytes(keyval.at[pl.ds(0, 4), 0], recv.at[slot - 2])
        each(4, body)

    pass_x(0, x_down, KV_X_FAR, {"x": x_up})
    pass_x(2, x_up, KV_X_FAR + 1, {"x": x_down})
    wait_bytes(keyval.at[pl.ds(0, 2), 0], recv.at[KV_X_FAR])
    wait_bytes(keyval.at[pl.ds(0, 2), 0], recv.at[KV_X_FAR + 1])
    push(keyval.at[:, core], keyval.at[:, core], KV_CORE, {"core": 1 - core})

    end_z(tri, SUM_Z)
    rows_f[...] = tri[...].reshape(2048, 128).astype(F32)
    for block in range(8):
        lines = (block * 2, block * 2 + 16, block * 2 + 1, block * 2 + 17)
        value = jnp.concatenate(
            [rows_f[pl.ds(block * 2 + half, 128, stride=16), :] for half in range(2)], axis=1
        )
        tnorm = layer_norm(value, 0).T.astype(BF16)
        update = matmul(tnorm, w_tri_out[...])
        updated = []
        for place, line in enumerate(lines):
            cells = slice(line * 64, line * 64 + 64)
            change = gate[cells, :] * update[place * 64 : place * 64 + 64]
            updated.append((pair[cells, :].astype(F32) + change).astype(BF16))
            new_pair[cells, :] = updated[-1]
        pnorm = layer_norm(jnp.concatenate(updated, axis=0).astype(F32), 1).astype(BF16)
        bias = contract_last(w_bias[...], pnorm)
        for half in range(2):
            rows = pl.ds(block * 2 + half, 64, stride=16)
            bias_f[rows, :] = bias[:, half * 128 : half * 128 + 128]

    def send_bias(layers, slot):
        def body(step):
            peer = after(head, step, 16)
            push(bias_in.at[layers, peer], bias_all.at[layers, head], slot, col_place(peer))

        each(15, body)
        keep(bias_in.at[layers, head], bias_all.at[layers, head], slot)

    bias_in[0] = bias_f[0:256, :].astype(BF16).reshape(16, 16, 128)
    send_bias(pl.ds(0, 1), BIAS_FIRST)
    bias_in[1:4] = bias_f[256:1024, :].astype(BF16).reshape(3, 16, 16, 128)
    send_bias(pl.ds(1, 3), BIAS_REST)
    store = pltpu.make_async_copy(new_pair, new_pair_h, load.at[8])
    store.start()
    wait_bytes(keyval.at[:, 0], recv.at[KV_CORE])
    for group in range(2):
        rows = slice(group * 256, group * 256 + 256)
        keys = keyval[:, :, group].reshape(1024, WIDE)
        score[rows, :] = contract_last(query[rows, :], keys)

    def bias_rows(layer):
        return jnp.concatenate(
            [
                jnp.concatenate(
                    [bias_all[layer, src, :, part * 64 : part * 64 + 64] for src in range(16)],
                    axis=-1,
                )
                for part in range(2)
            ],
            axis=0,
        )

    wait_bytes(bias_all.at[0, pl.ds(0, 1)], local.at[BIAS_FIRST])
    wait_bytes(bias_all.at[0, pl.ds(0, 15)], recv.at[BIAS_FIRST])
    first_bias = bias_rows(0)
    biases[0] = first_bias
    first_bias = first_bias.astype(F32)
    present = mask_f > 0.0
    for sample in range(16):
        rows = slice(sample * 32, sample * 32 + 32)
        logits = score[rows, :] * HEAD_DIM ** (-0.5) + first_bias
        logits = jnp.where(present, logits, -1000000000.0)
        expo = jnp.exp(logits - jnp.max(logits, axis=1, keepdims=True))
        probs[rows, :] = (expo * (1.0 / jnp.sum(expo, axis=1, keepdims=True))).astype(BF16)
    for group in range(2):
        rows = slice(group * 256, group * 256 + 256)
        values = keyval[:, :, 2 + group].reshape(1024, WIDE)
        context = matmul(probs[rows, :], values)
        gated = (agate[rows, :] * context * own_in[...]).astype(BF16)
        gathered = matmul(gated, gather_in[...]).astype(BF16)
        heads_in[group * 8 : group * 8 + 8] = gathered.reshape(8, 32, 128)

    def send_heads(step):
        peer = after(head, step, 16)
        push(heads_in.at[peer], heads_all.at[head], HEADS_OUT, col_place(peer))

    each(15, send_heads)
    keep(heads_in.at[head], heads_all.at[head], HEADS_OUT)
    wait_bytes(bias_all.at[pl.ds(0, 3), 0], local.at[BIAS_REST])
    wait_bytes(bias_all.at[pl.ds(0, 3), pl.ds(0, 15)], recv.at[BIAS_REST])
    for layer in range(1, 4):
        biases[layer] = bias_rows(layer)
    wait_bytes(w_out_all.at[0], recv.at[OUT_CORE])
    wait_bytes(heads_all.at[pl.ds(0, 1)], local.at[HEADS_OUT])
    wait_bytes(heads_all.at[pl.ds(0, 15)], recv.at[HEADS_OUT])
    merged = jnp.concatenate([heads_all[src, :, 0:HEAD_DIM] for src in range(16)], axis=-1)
    for half in range(2):
        weights = w_out_all[half].reshape(HEADS * HEAD_DIM, 384)
        attended[:, half * 384 : half * 384 + 384] = matmul(merged, weights).astype(BF16)

    store.wait()
    for slot in (LEFT_X, RIGHT_X, SUM_X):
        for step in range(4):
            wait_bytes(left_x.at[pl.ds(0, 4), pl.ds(0, 7)], send.at[slot + step])
    for step in range(4):
        sent_z(RIGHT_QUARTER, step)
    wait_bytes(left_z.at[pl.ds(0, 15)], send.at[SUM_Z])
    for way in range(2):
        for step in range(4):
            wait_bytes(left_all.at[0, 0], send.at[(LEFT_UP, LEFT_DOWN)[way] + step])
        wait_bytes(left_all.at[0, pl.ds(0, 2)], send.at[LEFT_FAR + way])
        wait_bytes(keyval_in, send.at[KV_Z_NEAR + way])
        wait_bytes(keyval_in.at[pl.ds(0, 2)], send.at[KV_Z_FAR + way])
        wait_bytes(keyval.at[pl.ds(0, 4), 0], send.at[KV_X_NEAR + way])
        wait_bytes(keyval.at[pl.ds(0, 2), 0], send.at[KV_X_FAR + way])
    wait_bytes(w_out_all.at[0, pl.ds(0, 3)], send.at[OUT_Z])
    wait_bytes(w_out_all.at[0, pl.ds(0, 12)], send.at[OUT_Y])
    wait_bytes(w_out_all.at[0], send.at[OUT_CORE])
    wait_bytes(keyval.at[:, 0], send.at[KV_CORE])
    wait_bytes(bias_all.at[0, pl.ds(0, 15)], send.at[BIAS_FIRST])
    wait_bytes(bias_all.at[pl.ds(0, 3), pl.ds(0, 15)], send.at[BIAS_REST])
    wait_bytes(heads_all.at[pl.ds(0, 15)], send.at[HEADS_OUT])


def per_device(pair, mask, w_tri_in, w_tri_out, w_bias, single, w_attn, w_out):
    vmem = pl.BlockSpec(memory_space=pltpu.VMEM)
    blocks = pltpu.VMEM((16, 8, 16, 128), BF16)
    new_pair, biases, attended = pl.pallas_call(
        whole_kernel,
        out_shape=(
            jax.ShapeDtypeStruct((2048, 128), BF16),
            jax.ShapeDtypeStruct((LAYERS, 32, 1024), BF16),
            jax.ShapeDtypeStruct((32, 768), BF16),
        ),
        in_specs=[pl.BlockSpec(memory_space=pltpu.HBM)] * 8,
        out_specs=(pl.BlockSpec(memory_space=pltpu.HBM), vmem, vmem),
        scratch_shapes=[
            pltpu.VMEM((2048, 128), BF16),
            pltpu.VMEM((1, 1024), jnp.int32),
            pltpu.VMEM((128, 640), BF16),
            pltpu.VMEM((128, 128), BF16),
            pltpu.VMEM((64, 128), BF16),
            pltpu.VMEM((512, 768), BF16),
            pltpu.VMEM((4 * HEAD_DIM, 768), BF16),
            pltpu.VMEM((HEAD_DIM, 768), BF16),
        ]
        + [blocks] * 9
        + [
            pltpu.VMEM((WIDE, 128), BF16),
            pltpu.VMEM((256, WIDE), F32),
            pltpu.VMEM((4, 4, 256, 256), BF16),
            pltpu.VMEM((4, 256, 256), BF16),
            pltpu.VMEM((16, 2, 4, 32, WIDE), BF16),
            pltpu.VMEM((4, 32, WIDE), BF16),
            pltpu.VMEM((2, HEADS, HEAD_DIM, 384), BF16),
            pltpu.VMEM((2048, 128), BF16),
            pltpu.VMEM((2048, 128), F32),
            pltpu.VMEM((2048, 128), F32),
            pltpu.VMEM((512, 128), BF16),
            pltpu.VMEM((512, WIDE), BF16),
            pltpu.VMEM((512, WIDE), F32),
            pltpu.VMEM((512, 1024), F32),
            pltpu.VMEM((1024, 128), F32),
            pltpu.VMEM((512, 1024), BF16),
            pltpu.VMEM((LAYERS, 16, 16, 128), BF16),
            pltpu.VMEM((LAYERS, 16, 16, 128), BF16),
            pltpu.VMEM((16, 32, 128), BF16),
            pltpu.VMEM((16, 32, 128), BF16),
            pltpu.VMEM((2048, 128), BF16),
            pltpu.SemaphoreType.DMA((SLOTS,)),
            pltpu.SemaphoreType.DMA((SLOTS,)),
            pltpu.SemaphoreType.DMA((SLOTS,)),
            pltpu.SemaphoreType.DMA((9,)),
        ],
        compiler_params=pltpu.CompilerParams(
            collective_id=0, has_side_effects=True, vmem_limit_bytes=60 * 1024 * 1024
        ),
        name="whole",
    )(
        pair.reshape(2048, 128),
        mask.reshape(1, 1024),
        w_tri_in,
        w_tri_out,
        w_bias.T,
        single.reshape(512, 768),
        w_attn.transpose(1, 2, 0).reshape(4 * HEAD_DIM, 768),
        w_out,
    )
    return (
        new_pair.reshape(32, 64, 128),
        biases.reshape(LAYERS, 1, 32, 1024),
        attended.reshape(1, 32, 768),
    )


def solution(mesh):
    fine = Mesh(mesh.devices.reshape(4, 4, 2, 4, 4), ("z_hi", "x", "core", "y", "z_lo"))
    placed = (
        P(ROW, COL, None),
        P(),
        P(),
        P(),
        P(),
        P(None, ROW, None),
        P(None, COL, None),
        P(COL, None),
    )
    return jax.shard_map(
        per_device,
        mesh=fine,
        in_specs=placed,
        out_specs=(P(ROW, COL, None), P(None, COL, ROW, None), P(COL, ROW, None)),
        check_vma=False,
    )
```

```python
import jax
import jax.numpy as jnp
from jax import lax
from jax.experimental import pallas as pl
from jax.experimental.pallas import tpu as pltpu
from jax.sharding import Mesh
from jax.sharding import PartitionSpec as P

HEADS = 16
HEAD_DIM = 48
LAYERS = 4
WIDE = 8 * HEAD_DIM
ROW = ("z_hi", "x", "core")
COL = ("y", "z_lo")
BF16 = jnp.bfloat16
F32 = jnp.float32

LEFT_X, RIGHT_X, SUM_X = 0, 4, 8
SUM_Z = 14
OUT_Z, OUT_Y, OUT_CORE, KV_CORE = 15, 16, 17, 18
BIAS_FIRST, BIAS_REST, HEADS_OUT = 19, 20, 21
LEFT_FAR, KV_Z_NEAR, KV_Z_FAR, KV_X_NEAR, KV_X_FAR = 22, 24, 26, 28, 30
LEFT_UP, LEFT_DOWN, LEFT_QUARTER, RIGHT_QUARTER = 32, 36, 40, 44
SLOTS = 48


def block_of(index):
    return sum((index >= HEAD_DIM * edge).astype(jnp.int32) for edge in range(1, 32))


def layer_norm(value, axis):
    mean = jnp.mean(value, axis=axis, keepdims=True)
    centred = value - mean
    var = jnp.mean(centred * centred, axis=axis, keepdims=True)
    return centred * lax.rsqrt(var + 1e-05)


def each(count, body):
    lax.fori_loop(0, count, lambda step, carry: (body(step), carry)[1], 0)


def wait_bytes(ref, sem):
    pltpu.make_async_copy(ref, ref, sem).wait()


def contract_last(a, b):
    return lax.dot_general(a, b, (((1,), (1,)), ((), ())), preferred_element_type=F32)


def matmul(a, b):
    return jnp.dot(a, b, preferred_element_type=F32)


def whole_kernel(
    pair_h, mask_h, w_tri_in_h, w_tri_out_h, w_bias_h, single_h, w_attn_h, w_out_h,
    new_pair_h, biases, attended,
    pair, mask, w_tri_in, w_tri_out, w_bias, single, w_attn, w_out,
    left_in, right_in, left_x, right_x, left_z, right_z, sums, sums_x, tri,
    gather_in, own_in, xn, projected,
    left_all, right_own, keyval, keyval_in, w_out_all,
    normed, gate, rows_f, w_in_t, query, agate, score, bias_f, probs,
    bias_in, bias_all, heads_in, heads_all, new_pair,
    send, recv, local, load,
):
    z_hi, z_lo = lax.axis_index("z_hi"), lax.axis_index("z_lo")
    x, core, y = lax.axis_index("x"), lax.axis_index("core"), lax.axis_index("y")
    z, xc, head = z_hi * 4 + z_lo, x * 2 + core, y * 4 + z_lo

    def z_place(peer):
        return {"z_hi": lax.div(peer, 4), "z_lo": lax.rem(peer, 4)}

    def xc_place(peer):
        return {"x": lax.div(peer, 2), "core": lax.rem(peer, 2)}

    def col_place(peer):
        return {"y": lax.div(peer, 4), "z_lo": lax.rem(peer, 4)}

    def after(place, step, size):
        return lax.rem(place + 1 + step, size)

    def near(axis, place, step, size):
        return {axis: after(place, step, size)}

    loads = [
        pltpu.make_async_copy(src, dst, load.at[slot])
        for slot, (src, dst) in enumerate(
            (
                (single_h, single), (w_attn_h, w_attn), (pair_h, pair), (w_tri_in_h, w_tri_in),
                (mask_h, mask), (w_out_h, w_out), (w_tri_out_h, w_tri_out), (w_bias_h, w_bias),
            )
        )
    ]
    for copy in loads:
        copy.start()
    barrier = pltpu.get_barrier_semaphore()

    def greet(peer):
        pl.semaphore_signal(barrier, inc=1, device_id=peer, device_id_type=pl.DeviceIdType.MESH)

    each(15, lambda step: greet(z_place(after(z, step, 16))))
    each(7, lambda step: greet(xc_place(after(xc, step, 8))))
    each(15, lambda step: greet(col_place(after(head, step, 16))))

    def push(src, dst, slot, peer):
        pltpu.make_async_remote_copy(
            src_ref=src, dst_ref=dst, send_sem=send.at[slot], recv_sem=recv.at[slot],
            device_id=peer, device_id_type=pl.DeviceIdType.MESH,
        ).start()

    def keep(src, dst, slot):
        pltpu.make_async_copy(src, dst, local.at[slot]).start()

    def quarter(step):
        return after(z_hi, step, 4)

    def over_x(src, dst, slot, step, first):
        part = pl.ds(first * 4, 4)

        def body(other):
            peer = after(xc, other, 8)
            push(src.at[part, peer], dst.at[part, xc], slot + step, xc_place(peer))

        each(7, body)
        keep(src.at[part, xc], dst.at[part, xc], slot + step)

    def end_x(dst, slot, step):
        wait_bytes(dst.at[0, pl.ds(0, 4)], local.at[slot + step])
        wait_bytes(dst.at[pl.ds(0, 4), pl.ds(0, 7)], recv.at[slot + step])

    def over_z(src, dst, slot, step):
        def body(low):
            peer = quarter(step) * 4 + low

            @pl.when(peer != z)
            def _():
                push(src.at[peer], dst.at[z], slot, z_place(peer))

            @pl.when(peer == z)
            def _():
                keep(src.at[z], dst.at[z], slot)

        each(4, body)

    def end_z(dst, slot):
        wait_bytes(dst.at[pl.ds(0, 1)], local.at[slot])
        wait_bytes(dst.at[pl.ds(0, 15)], recv.at[slot])

    head_lane = lax.broadcasted_iota(jnp.int32, (1, WIDE), 1)
    head_block = block_of(head_lane)
    place = lax.broadcasted_iota(jnp.int32, (256, WIDE), 0)
    own_in[...] = ((place >= 32 * head_block) & (place < 32 * head_block + 32)).astype(F32)

    def spread(first, count):
        place = lax.broadcasted_iota(jnp.int32, (4 * HEAD_DIM, WIDE), 0)
        source = head_lane - HEAD_DIM * head_block
        parts = [
            (place == source + HEAD_DIM * (first + n)).astype(F32).astype(BF16) for n in range(count)
        ]
        return jnp.concatenate(parts, axis=1) if count > 1 else parts[0]

    for copy in loads[:2]:
        copy.wait()
    key_value = spread(1, 2)
    for group in range(2):
        rows = slice(group * 256, group * 256 + 256)
        xn[rows, :] = layer_norm(single[rows, :].astype(F32), 1).astype(BF16)
        projected[rows, :] = contract_last(xn[rows, :], w_attn[...]).astype(BF16)
        wide = matmul(projected[rows, :], key_value)
        for which in range(2):
            part = wide[:, WIDE * which : WIDE * (which + 1)] * own_in[...]
            packed = jnp.sum(part.reshape(8, 32, WIDE), axis=0)
            keyval_in[which * 2 + group] = packed.astype(BF16)
    pl.semaphore_wait(barrier, 37)
    mine = keyval.at[z_hi * 4 + x, core]
    z_up, z_down, x_up, x_down = after(z_hi, 0, 4), after(z_hi, 2, 4), after(x, 0, 4), after(x, 2, 4)
    push(keyval_in, mine, KV_Z_NEAR, {"z_hi": z_up})
    push(keyval_in, mine, KV_Z_NEAR + 1, {"z_hi": z_down})
    keep(keyval_in, mine, KV_Z_NEAR)

    for copy in loads[2:]:
        copy.wait()
    mask_f = mask[...].astype(F32)
    lane = lax.broadcasted_iota(jnp.int32, (1024, 128), 1)
    token = lax.broadcasted_iota(jnp.int32, (1024, 128), 0)
    low_lane = jnp.where(lane < 64, lane, lane - 64)
    chosen = (token == head * 64 + low_lane).astype(F32).astype(BF16)
    col_mask = matmul(jnp.broadcast_to(mask_f, (16, 1024)).astype(BF16), chosen)
    token = lax.broadcasted_iota(jnp.int32, (16, 1024), 1)
    line = lax.broadcasted_iota(jnp.int32, (16, 1024), 0) * 2 + (z_hi * 8 + xc) * 32
    even = jnp.sum(jnp.where(token == line, mask_f, 0.0), axis=1, keepdims=True)
    odd = jnp.sum(jnp.where(token == line + 1, mask_f, 0.0), axis=1, keepdims=True)
    low = lax.broadcasted_iota(jnp.int32, (16, 128), 1) < 64
    cell_mask = jnp.where(low, even, odd) * col_mask

    w_in_t[...] = w_tri_in[:, 0:512].T

    def factor(block, first):
        rows = slice(block * 256, block * 256 + 256)
        both = contract_last(w_in_t[first : first + 256, :], normed[rows, :])
        value = jax.nn.sigmoid(both[128:]) * both[:128]
        for half in range(2):
            line = block * 2 + half
            part = value[:, half * 128 : half * 128 + 128] * cell_mask[line : line + 1]
            rows_f[pl.ds(line, 128, stride=16), :] = part

    for block in range(8):
        rows = slice(block * 256, block * 256 + 256)
        normed[rows, :] = layer_norm(pair[rows, :].astype(F32), 1).astype(BF16)
        factor(block, 0)
    left_in[...] = rows_f[...].astype(BF16).reshape(16, 8, 16, 128)
    for step in range(4):
        over_z(left_in, left_z, LEFT_QUARTER + step, step)
    for block in range(8):
        factor(block, 256)
    right_in[...] = rows_f[...].astype(BF16).reshape(16, 8, 16, 128)
    for step in range(4):
        over_x(right_in, right_x, RIGHT_X, step, quarter(step))
    half_out = w_out.at[:, pl.ds(pl.multiple_of(core * 384, 128), 384)]
    each(3, lambda step: push(half_out, w_out_all.at[core, head], OUT_Z, near("z_lo", z_lo, step, 4)))
    keep(half_out, w_out_all.at[core, head], OUT_Z)

    lane = lax.broadcasted_iota(jnp.int32, (WIDE, 128), 1)
    place = lax.broadcasted_iota(jnp.int32, (WIDE, 128), 0)
    gather_in[...] = (place - HEAD_DIM * block_of(place) == lane).astype(F32).astype(BF16)
    w_gate = matmul(w_attn[...].T, spread(3, 1)).astype(BF16)
    for group in range(2):
        rows = slice(group * 256, group * 256 + 256)
        query[rows, :] = (matmul(projected[rows, :], spread(0, 1)) * own_in[...]).astype(BF16)
        agate[rows, :] = jax.nn.sigmoid(matmul(xn[rows, :], w_gate))

    def sent_z(slot, step):
        wait_bytes(left_z.at[pl.ds(0, 3 if step == 3 else 4)], send.at[slot + step])

    for step in range(4):
        end_x(right_x, RIGHT_X, step)
        sent_z(LEFT_QUARTER, step)
        over_z(right_x, right_z, RIGHT_QUARTER + step, step)
    wait_bytes(w_out_all.at[0, pl.ds(0, 1)], local.at[OUT_Z])
    wait_bytes(w_out_all.at[0, pl.ds(0, 3)], recv.at[OUT_Z])
    quad = w_out_all.at[core, pl.ds(y * 4, 4)]
    each(3, lambda step: push(quad, quad, OUT_Y, near("y", y, step, 4)))
    for block in range(8):
        rows = slice(block * 256, block * 256 + 256)
        gate[rows, :] = jax.nn.sigmoid(matmul(normed[rows, :], w_tri_in[:, 512:640]))

    def tiles(blocks, z_part, part):
        pieces = [blocks[z_part * 4 + low, :, :, part * 64 : part * 64 + 64] for low in range(4)]
        return jnp.concatenate(pieces, axis=-1).reshape(128, 256)

    up, down = after(y, 0, 4), after(y, 2, 4)

    def origin(step):
        return lax.rem(z_hi + 3 - step, 4)

    def end_quarter(slot, step):
        if step == 3:
            wait_bytes(left_z.at[pl.ds(0, 1)], local.at[slot + step])
        wait_bytes(left_z.at[pl.ds(0, 3 if step == 3 else 4)], recv.at[slot + step])

    for step in range(4):
        end_quarter(LEFT_QUARTER, step)
        over_x(left_z, left_x, LEFT_X, step, origin(step))
    for step in range(4):
        end_x(left_x, LEFT_X, step)
        source = origin(step)
        for part in range(2):
            left_all[y, source, :, part * 128 : part * 128 + 128] = tiles(left_x, source, part).T
        own = left_all.at[y, source]
        push(own, own, LEFT_UP + step, {"y": up})
        push(own, own, LEFT_DOWN + step, {"y": down})
    for step in range(4):
        source = origin(step)
        wait_bytes(left_all.at[y, 0], recv.at[LEFT_UP + step])
        passed = left_all.at[down, source, pl.ds(0, 128)]
        push(passed, passed, LEFT_FAR, {"y": up})
        wait_bytes(left_all.at[y, 0], recv.at[LEFT_DOWN + step])
        passed = left_all.at[up, source, pl.ds(128, 128)]
        push(passed, passed, LEFT_FAR + 1, {"y": down})
    def over_x_ring(part):
        block = keyval.at[part * 4 + x, core]
        push(block, block, KV_X_NEAR, {"x": x_up})
        push(block, block, KV_X_NEAR + 1, {"x": x_down})

    wait_bytes(keyval_in, local.at[KV_Z_NEAR])
    wait_bytes(keyval_in, recv.at[KV_Z_NEAR])
    wait_bytes(keyval_in, recv.at[KV_Z_NEAR + 1])
    each(3, lambda step: over_x_ring(lax.rem(z_hi + 3 + step, 4)))
    for step in range(4):
        end_quarter(RIGHT_QUARTER, step)
        if step == 3:
            passed = keyval.at[z_down * 4 + x, core, pl.ds(0, 2)]
            push(passed, passed, KV_Z_FAR, {"z_hi": z_up})
            passed = keyval.at[z_up * 4 + x, core, pl.ds(2, 2)]
            push(passed, passed, KV_Z_FAR + 1, {"z_hi": z_down})
        source = origin(step)
        for part in range(2):
            right_own[source, part * 128 : part * 128 + 128, :] = tiles(right_z, source, part)
    for way in range(2):
        wait_bytes(left_all.at[0, pl.ds(0, 2)], recv.at[LEFT_FAR + way])
    for step in range(4):
        part = quarter(step)
        product = sum(matmul(left_all[part, quad], right_own[quad]) for quad in range(4))
        product = product.astype(BF16).reshape(8, 2, 16, 256)
        for low in range(4):
            cut = slice(low * 64, low * 64 + 64)
            sums[part * 4 + low] = jnp.concatenate(
                [product[:, 0, :, cut], product[:, 1, :, cut]], axis=-1
            )
        over_x(sums, sums_x, SUM_X, step, part)
    for step in range(4):
        end_x(sums_x, SUM_X, step)
        over_z(sums_x, tri, SUM_Z, step)
    wait_bytes(w_out_all.at[0, pl.ds(0, 12)], recv.at[OUT_Y])
    push(w_out_all.at[core], w_out_all.at[core], OUT_CORE, {"core": 1 - core})
    wait_bytes(keyval_in.at[pl.ds(0, 2)], recv.at[KV_Z_FAR])
    wait_bytes(keyval_in.at[pl.ds(0, 2)], recv.at[KV_Z_FAR + 1])
    over_x_ring(lax.rem(z_hi + 2, 4))

    def pass_x(first, src, slot, place):
        def body(part):
            passed = keyval.at[part * 4 + src, core, pl.ds(first, 2)]
            push(passed, passed, slot, place)

        wait_bytes(keyval.at[pl.ds(0, 4), 0], recv.at[slot - 2])
        each(4, body)

    pass_x(0, x_down, KV_X_FAR, {"x": x_up})
    pass_x(2, x_up, KV_X_FAR + 1, {"x": x_down})
    wait_bytes(keyval.at[pl.ds(0, 2), 0], recv.at[KV_X_FAR])
    wait_bytes(keyval.at[pl.ds(0, 2), 0], recv.at[KV_X_FAR + 1])
    push(keyval.at[:, core], keyval.at[:, core], KV_CORE, {"core": 1 - core})

    end_z(tri, SUM_Z)
    rows_f[...] = tri[...].reshape(2048, 128).astype(F32)
    for block in range(8):
        lines = (block * 2, block * 2 + 16, block * 2 + 1, block * 2 + 17)
        value = jnp.concatenate(
            [rows_f[pl.ds(block * 2 + half, 128, stride=16), :] for half in range(2)], axis=1
        )
        tnorm = layer_norm(value, 0).T.astype(BF16)
        update = matmul(tnorm, w_tri_out[...])
        updated = []
        for place, line in enumerate(lines):
            cells = slice(line * 64, line * 64 + 64)
            change = gate[cells, :] * update[place * 64 : place * 64 + 64]
            updated.append((pair[cells, :].astype(F32) + change).astype(BF16))
            new_pair[cells, :] = updated[-1]
        pnorm = layer_norm(jnp.concatenate(updated, axis=0).astype(F32), 1).astype(BF16)
        bias = contract_last(w_bias[...], pnorm)
        for half in range(2):
            rows = pl.ds(block * 2 + half, 64, stride=16)
            bias_f[rows, :] = bias[:, half * 128 : half * 128 + 128]

    def send_bias(layers, slot):
        def body(step):
            peer = after(head, step, 16)
            push(bias_in.at[layers, peer], bias_all.at[layers, head], slot, col_place(peer))

        each(15, body)
        keep(bias_in.at[layers, head], bias_all.at[layers, head], slot)

    bias_in[0] = bias_f[0:256, :].astype(BF16).reshape(16, 16, 128)
    send_bias(pl.ds(0, 1), BIAS_FIRST)
    bias_in[1:4] = bias_f[256:1024, :].astype(BF16).reshape(3, 16, 16, 128)
    send_bias(pl.ds(1, 3), BIAS_REST)
    store = pltpu.make_async_copy(new_pair, new_pair_h, load.at[8])
    store.start()
    wait_bytes(keyval.at[:, 0], recv.at[KV_CORE])
    for group in range(2):
        rows = slice(group * 256, group * 256 + 256)
        keys = keyval[:, :, group].reshape(1024, WIDE)
        score[rows, :] = contract_last(query[rows, :], keys)

    def bias_rows(layer):
        return jnp.concatenate(
            [
                jnp.concatenate(
                    [bias_all[layer, src, :, part * 64 : part * 64 + 64] for src in range(16)],
                    axis=-1,
                )
                for part in range(2)
            ],
            axis=0,
        )

    wait_bytes(bias_all.at[0, pl.ds(0, 1)], local.at[BIAS_FIRST])
    wait_bytes(bias_all.at[0, pl.ds(0, 15)], recv.at[BIAS_FIRST])
    first_bias = bias_rows(0)
    biases[0] = first_bias
    first_bias = first_bias.astype(F32)
    present = mask_f > 0.0
    for sample in range(16):
        rows = slice(sample * 32, sample * 32 + 32)
        logits = score[rows, :] * HEAD_DIM ** (-0.5) + first_bias
        logits = jnp.where(present, logits, -1000000000.0)
        expo = jnp.exp(logits - jnp.max(logits, axis=1, keepdims=True))
        probs[rows, :] = (expo * (1.0 / jnp.sum(expo, axis=1, keepdims=True))).astype(BF16)
    for group in range(2):
        rows = slice(group * 256, group * 256 + 256)
        values = keyval[:, :, 2 + group].reshape(1024, WIDE)
        context = matmul(probs[rows, :], values)
        gated = (agate[rows, :] * context * own_in[...]).astype(BF16)
        gathered = matmul(gated, gather_in[...]).astype(BF16)
        heads_in[group * 8 : group * 8 + 8] = gathered.reshape(8, 32, 128)

    def send_heads(step):
        peer = after(head, step, 16)
        push(heads_in.at[peer], heads_all.at[head], HEADS_OUT, col_place(peer))

    each(15, send_heads)
    keep(heads_in.at[head], heads_all.at[head], HEADS_OUT)
    wait_bytes(bias_all.at[pl.ds(0, 3), 0], local.at[BIAS_REST])
    wait_bytes(bias_all.at[pl.ds(0, 3), pl.ds(0, 15)], recv.at[BIAS_REST])
    for layer in range(1, 4):
        biases[layer] = bias_rows(layer)
    wait_bytes(w_out_all.at[0], recv.at[OUT_CORE])
    wait_bytes(heads_all.at[pl.ds(0, 1)], local.at[HEADS_OUT])
    wait_bytes(heads_all.at[pl.ds(0, 15)], recv.at[HEADS_OUT])
    merged = jnp.concatenate([heads_all[src, :, 0:HEAD_DIM] for src in range(16)], axis=-1)
    for half in range(2):
        weights = w_out_all[half].reshape(HEADS * HEAD_DIM, 384)
        attended[:, half * 384 : half * 384 + 384] = matmul(merged, weights).astype(BF16)

    store.wait()
    for slot in (LEFT_X, RIGHT_X, SUM_X):
        for step in range(4):
            wait_bytes(left_x.at[pl.ds(0, 4), pl.ds(0, 7)], send.at[slot + step])
    for step in range(4):
        sent_z(RIGHT_QUARTER, step)
    wait_bytes(left_z.at[pl.ds(0, 15)], send.at[SUM_Z])
    for way in range(2):
        for step in range(4):
            wait_bytes(left_all.at[0, 0], send.at[(LEFT_UP, LEFT_DOWN)[way] + step])
        wait_bytes(left_all.at[0, pl.ds(0, 2)], send.at[LEFT_FAR + way])
        wait_bytes(keyval_in, send.at[KV_Z_NEAR + way])
        wait_bytes(keyval_in.at[pl.ds(0, 2)], send.at[KV_Z_FAR + way])
        wait_bytes(keyval.at[pl.ds(0, 4), 0], send.at[KV_X_NEAR + way])
        wait_bytes(keyval.at[pl.ds(0, 2), 0], send.at[KV_X_FAR + way])
    wait_bytes(w_out_all.at[0, pl.ds(0, 3)], send.at[OUT_Z])
    wait_bytes(w_out_all.at[0, pl.ds(0, 12)], send.at[OUT_Y])
    wait_bytes(w_out_all.at[0], send.at[OUT_CORE])
    wait_bytes(keyval.at[:, 0], send.at[KV_CORE])
    wait_bytes(bias_all.at[0, pl.ds(0, 15)], send.at[BIAS_FIRST])
    wait_bytes(bias_all.at[pl.ds(0, 3), pl.ds(0, 15)], send.at[BIAS_REST])
    wait_bytes(heads_all.at[pl.ds(0, 15)], send.at[HEADS_OUT])


def per_device(pair, mask, w_tri_in, w_tri_out, w_bias, single, w_attn, w_out):
    vmem = pl.BlockSpec(memory_space=pltpu.VMEM)
    blocks = pltpu.VMEM((16, 8, 16, 128), BF16)
    new_pair, biases, attended = pl.pallas_call(
        whole_kernel,
        out_shape=(
            jax.ShapeDtypeStruct((2048, 128), BF16),
            jax.ShapeDtypeStruct((LAYERS, 32, 1024), BF16),
            jax.ShapeDtypeStruct((32, 768), BF16),
        ),
        in_specs=[pl.BlockSpec(memory_space=pltpu.HBM)] * 8,
        out_specs=(pl.BlockSpec(memory_space=pltpu.HBM), vmem, vmem),
        scratch_shapes=[
            pltpu.VMEM((2048, 128), BF16),
            pltpu.VMEM((1, 1024), jnp.int32),
            pltpu.VMEM((128, 640), BF16),
            pltpu.VMEM((128, 128), BF16),
            pltpu.VMEM((64, 128), BF16),
            pltpu.VMEM((512, 768), BF16),
            pltpu.VMEM((4 * HEAD_DIM, 768), BF16),
            pltpu.VMEM((HEAD_DIM, 768), BF16),
        ]
        + [blocks] * 9
        + [
            pltpu.VMEM((WIDE, 128), BF16),
            pltpu.VMEM((256, WIDE), F32),
            pltpu.VMEM((512, 768), BF16),
            pltpu.VMEM((512, 4 * HEAD_DIM), BF16),
            pltpu.VMEM((4, 4, 256, 256), BF16),
            pltpu.VMEM((4, 256, 256), BF16),
            pltpu.VMEM((16, 2, 4, 32, WIDE), BF16),
            pltpu.VMEM((4, 32, WIDE), BF16),
            pltpu.VMEM((2, HEADS, HEAD_DIM, 384), BF16),
            pltpu.VMEM((2048, 128), BF16),
            pltpu.VMEM((2048, 128), F32),
            pltpu.VMEM((2048, 128), F32),
            pltpu.VMEM((512, 128), BF16),
            pltpu.VMEM((512, WIDE), BF16),
            pltpu.VMEM((512, WIDE), F32),
            pltpu.VMEM((512, 1024), F32),
            pltpu.VMEM((1024, 128), F32),
            pltpu.VMEM((512, 1024), BF16),
            pltpu.VMEM((LAYERS, 16, 16, 128), BF16),
            pltpu.VMEM((LAYERS, 16, 16, 128), BF16),
            pltpu.VMEM((16, 32, 128), BF16),
            pltpu.VMEM((16, 32, 128), BF16),
            pltpu.VMEM((2048, 128), BF16),
            pltpu.SemaphoreType.DMA((SLOTS,)),
            pltpu.SemaphoreType.DMA((SLOTS,)),
            pltpu.SemaphoreType.DMA((SLOTS,)),
            pltpu.SemaphoreType.DMA((9,)),
        ],
        compiler_params=pltpu.CompilerParams(
            collective_id=0, has_side_effects=True, vmem_limit_bytes=60 * 1024 * 1024
        ),
        name="whole",
    )(
        pair.reshape(2048, 128),
        mask.reshape(1, 1024),
        w_tri_in,
        w_tri_out,
        w_bias.T,
        single.reshape(512, 768),
        w_attn.transpose(1, 2, 0).reshape(4 * HEAD_DIM, 768),
        w_out,
    )
    return (
        new_pair.reshape(32, 64, 128),
        biases.reshape(LAYERS, 1, 32, 1024),
        attended.reshape(1, 32, 768),
    )


def solution(mesh):
    fine = Mesh(mesh.devices.reshape(4, 4, 2, 4, 4), ("z_hi", "x", "core", "y", "z_lo"))
    placed = (
        P(ROW, COL, None),
        P(),
        P(),
        P(),
        P(),
        P(None, ROW, None),
        P(None, COL, None),
        P(COL, None),
    )
    return jax.shard_map(
        per_device,
        mesh=fine,
        in_specs=placed,
        out_specs=(P(ROW, COL, None), P(None, COL, ROW, None), P(COL, ROW, None)),
        check_vma=False,
    )
```
